32 devices in a mesh: expert: 8 (over z, y), head: 4 (over x, core).
Axes of the slice: x: 2, y: 2, z: 4, core: 2. Of those that a mesh axis runs over, the one named last changes fastest.
Arguments:
- tokens: bfloat16 [32768, 512], P(('expert', 'head')), may hold values from -6 to 6
- segment_ids: int32 [32768], P('expert'), may hold values from 0 to 1023, never falling along the last dimension, each value on 1 to 64 neighbouring positions
- task_ids: int32 [1024], replicated, may hold values from 0 to 63
- task_table: int32 [64, 2], replicated, may hold values from 0 to 7, as said below
- weight_qkv: float32 [3, 512, 512], P(None, 'expert', 'head'), may hold values from -0.25 to 0.25
- weight_out: float32 [512, 512], P('head', 'expert'), may hold values from -1 to 1
- gain_one: float32 [512], P('expert'), may hold values from 0.5 to 1.5
- gain_two: float32 [512], P('expert'), may hold values from 0.5 to 1.5
- weight_router: float32 [512, 8], P('expert'), may hold values from -0.1875 to 0.1875
- weight_in: float32 [8, 512, 2048], P('expert', 'head'), may hold values from -0.25 to 0.25
- weight_hidden: float32 [8, 2048, 512], P('expert', 'head'), may hold values from -0.1875 to 0.1875
- cotangent: bfloat16 [32768, 512], P(('expert', 'head')), may hold values from -6 to 6
Outputs:
- output: bfloat16 [32768, 512], P(('expert', 'head'))
- grad_tokens: float32 [32768, 512], P(('expert', 'head'))
- grad_qkv: float32 [3, 512, 512], P(None, 'expert', 'head')
- grad_out: float32 [512, 512], P('head', 'expert')
- grad_gain_one: float32 [512], P('expert')
- grad_gain_two: float32 [512], P('expert')
- grad_router: float32 [512, 8], P('expert')
- grad_in: float32 [8, 512, 2048], P('expert', 'head')
- grad_hidden: float32 [8, 2048, 512], P('expert', 'head')
The draws below stay inside these ranges and needn't reach their ends.
Inputs may be any that keep to these rules, and one draw needn't show every extreme that they name: `task_table`: each row names two different experts; every expert stands in the first column of some row.
All inputs are finite; a program needn't handle non-finite values.
Results may differ from the reference program's by a relative error of at most 0.024.
Values may be sent and summed in bfloat16 or wider, within the bound.
No kernel may reach another device: no remote copies, remote signals or barrier semaphores. Data moves between devices by JAX's collectives and lax.ppermute only.
A program may use at most 192 MiB of HBM per device.

```python
import math
import jax
import jax.numpy as jnp
import numpy as np
from jax import lax

D = 512
HEADS = 8
HDIM = 64
FF = 2048
TASKS = 64
ROWS = 1024
PACK = 1024
DOC = 32
EXPERTS = 8
TOKENS = 32768
SEGMENTS = 1024
CAP = 512
DEVICES = 32


def draw_task_table(key, part):
    key = jax.random.fold_in(key, 7)
    first_key, second_key = jax.random.split(key)
    first_column = jax.random.permutation(first_key, TASKS) % EXPERTS
    offset = jax.random.randint(second_key, (TASKS,), 1, EXPERTS)
    second = (first_column + offset) % EXPERTS
    return jnp.stack([first_column, second], axis=1).astype(jnp.int32)


def touch_ends(values, own_key, smallest, top_value):
    longest = values.shape.index(max(values.shape))
    spots = []
    for shift in (0, 1):
        where = [jax.random.randint(jax.random.fold_in(own_key, axis), (), 0, length) for axis, length in enumerate(values.shape)]
        where[longest] = (where[longest] + shift) % values.shape[longest]
        spots.append(tuple(where))
    return values.at[spots[0]].set(smallest).at[spots[1]].set(top_value)


def block_levels(rng, extent, cuts, smallest, largest):
    def one(axis_at, parts):
        draws = jax.random.uniform(jax.random.fold_in(jax.random.fold_in(rng, 6), axis_at), (parts,), jnp.float32, smallest / len(cuts), largest / len(cuts))
        return jnp.repeat(jnp.exp(draws), extent[axis_at] // parts).reshape((-1,) + (1,) * (len(extent) - axis_at - 1))

    factor_of = one(*cuts[0])
    for cut in cuts[1:]:
        factor_of = factor_of * one(*cut)
    return factor_of


def cumulative_ranks(count, slope):
    portions = [(1 << 20) // math.isqrt(rank ** slope) + 1 for rank in range(1, count + 1)]
    width = 1 + sum(portions) // (1 << 30)
    return np.cumsum(np.array([max(1, weight // width) for weight in portions]))


def ranked_ids(own_key, shape, number_of, lean):
    table = cumulative_ranks(number_of, lean)
    ticket = jax.random.randint(jax.random.fold_in(own_key, 1), shape, 0, int(table[number_of - 1]))
    grade = jnp.searchsorted(jnp.asarray(table, jnp.int32), ticket, side="right")
    return jax.random.permutation(jax.random.fold_in(own_key, 2), number_of)[grade].astype(jnp.int32)


def length_profile(amount, total, reach, skew):
    loads = [(1 << 20) // math.isqrt(rank ** skew) + 1 for rank in range(2, amount + 1)]
    spare, counts = total - reach - (amount - 1), [1] * (amount - 1)
    while spare > 0:
        movable = [i for i in range(amount - 1) if counts[i] < reach]
        whole, remaining = sum([loads[i] for i in movable]), spare
        for i in movable:
            extra = min(reach - counts[i], max(1, remaining * loads[i] // whole), spare)
            counts[i] = counts[i] + extra
            spare = spare - extra
    return np.array([reach] + counts)


def uneven_parts(stream_key, amount, total, bound, skew):
    if amount == 2:
        one = jax.random.randint(stream_key, (), max(1, total - bound), min(bound, total - 1) + 1)
        return jnp.stack([one, total - one])
    sizes = jnp.asarray(length_profile(amount, total, bound, skew), jnp.int32)
    pairs = (amount - 1) // 2
    source_of, taker = sizes[1:1 + 2 * pairs:2], sizes[2:2 + 2 * pairs:2]
    margin = jnp.minimum(source_of - 1, bound - taker)
    moved = jax.random.randint(jax.random.fold_in(stream_key, 1), (pairs,), 0, 1 << 20) % (margin + 1)
    sizes = sizes.at[1:1 + 2 * pairs:2].set(source_of - moved).at[2:2 + 2 * pairs:2].set(taker + moved)
    return sizes[jax.random.permutation(jax.random.fold_in(stream_key, 2), amount)]


def bell_draw(rng, dims, spread, reach, pieces=(), held_as=jnp.bfloat16):
    entries = spread * jax.random.normal(rng, dims, jnp.float32)
    if pieces:
        entries = entries * block_levels(rng, dims, pieces, -0.22, 0.18)
    return jnp.clip(entries, -reach, reach).astype(held_as)


def setup_inputs(seed: int = 0) -> dict:
    key_list = jax.random.split(jax.random.key(seed), 13)
    return {
        "tokens": bell_draw(key_list[0], (TOKENS, D), 1.0, 6.0, ((0, 32),)),
        "segment_ids": jnp.searchsorted(jnp.cumsum(uneven_parts(key_list[1], SEGMENTS, TOKENS, 2 * DOC, 1)), jnp.arange(TOKENS), side="right").astype(jnp.int32),
        "task_ids": touch_ends(ranked_ids(key_list[2], (SEGMENTS,), TASKS, 2), jax.random.fold_in(key_list[2], 3), 0, TASKS - 1).astype(jnp.int32),
        "task_table": draw_task_table(jax.random.fold_in(key_list[12], 71), 0),
        "weight_qkv": bell_draw(key_list[4], (3, D, D), D ** -0.5, 0.25, ((1, 8), (2, 4)), jnp.float32),
        "weight_out": bell_draw(key_list[5], (D, D), (D // 16) ** -0.5, 1.0, ((0, 4), (1, 8)), jnp.float32),
        "gain_one": jnp.clip(1.0 + 0.1 * jax.random.normal(key_list[6], (D,), jnp.float32), 0.5, 1.5),
        "gain_two": jnp.clip(1.0 + 0.1 * jax.random.normal(key_list[7], (D,), jnp.float32), 0.5, 1.5),
        "weight_router": bell_draw(key_list[8], (D, EXPERTS), (2 * D) ** -0.5, 0.1875, ((0, 8),), jnp.float32),
        "weight_in": bell_draw(key_list[9], (EXPERTS, D, FF), D ** -0.5, 0.25, ((0, 8), (1, 4)), jnp.float32),
        "weight_hidden": bell_draw(key_list[10], (EXPERTS, FF, D), (FF // 2) ** -0.5, 0.1875, ((0, 8), (1, 4)), jnp.float32),
        "cotangent": bell_draw(key_list[11], (TOKENS, D), 1.0, 6.0, ((0, 32),)),
    }


EPSILON = 1e-05
NEGATIVE = -1e+30
highest = lax.Precision.HIGHEST

@jax.custom_vjp
def low(v):
    return lax.optimization_barrier(v.astype(jnp.bfloat16)).astype(jnp.float32)

@jax.custom_vjp
def low_back(v):
    return v

def low_keep(v):
    return (low(v), None)

def low_pass(kept, grad):
    return (grad,)

def back_keep(v):
    return (v, None)

def back_low(kept, grad):
    return (low(grad),)
low.defvjp(low_keep, low_pass)
low_back.defvjp(back_keep, back_low)

def layer_norm(values, gain_vector):
    centered = values - lax.optimization_barrier(jnp.mean(values, axis=-1, keepdims=True))
    return centered * lax.rsqrt(lax.optimization_barrier(jnp.mean(centered * centered, axis=-1, keepdims=True)) + EPSILON) * gain_vector

def attend_pack(operands):
    queries, keys_block, values_block, segments = operands
    score_scale = HDIM ** (-0.5)
    scores = low_back(jnp.einsum('qhd,khd->hqk', queries, keys_block, precision=highest) * score_scale)
    same_segment = segments[:, None] == segments[None, :]
    scores = jnp.where(same_segment[None], scores, NEGATIVE)
    row_peak = lax.optimization_barrier(jnp.max(scores, axis=-1, keepdims=True))
    exponent = jnp.exp(scores - row_peak)
    softmax_low = low(exponent / lax.optimization_barrier(jnp.sum(exponent, axis=-1, keepdims=True)))
    return jnp.einsum('hqk,khd->qhd', softmax_low, values_block, precision=highest)

def expert_block(operands):
    rows_in, matrix_in, matrix_hidden = operands
    hidden_pre = low_back(jnp.dot(rows_in, matrix_in, precision=highest))
    activated = low(jax.nn.gelu(hidden_pre, approximate=True))
    return low_back(low(jnp.dot(activated, matrix_hidden, precision=highest)))

def reference(tokens, segment_ids, task_ids, task_table, weight_qkv, weight_out, gain_one, gain_two, weight_router, weight_in, weight_hidden, cotangent):
    chosen = task_table[task_ids[segment_ids]]
    block_choice = chosen.reshape(DEVICES, 2 * ROWS)
    expert_marks = (block_choice[:, :, None] == jnp.arange(EXPERTS, dtype=jnp.int32)).astype(jnp.int32)
    running = jnp.cumsum(expert_marks, axis=1)
    slot_index = lax.optimization_barrier(jnp.sum((running - 1) * expert_marks, axis=2))
    source = jnp.arange(DEVICES, dtype=jnp.int32)[:, None]
    dummy_index = EXPERTS * DEVICES * CAP
    position = jnp.where(slot_index < CAP, block_choice * (DEVICES * CAP) + source * CAP + slot_index, dummy_index).reshape(-1)
    lookup = jnp.full((dummy_index + 1,), 2 * TOKENS, jnp.int32).at[position].set(jnp.arange(2 * TOKENS, dtype=jnp.int32))
    lookup = lookup[:dummy_index].reshape(EXPERTS, DEVICES * CAP)
    pair_marks = chosen[:, :, None] == jnp.arange(EXPERTS, dtype=jnp.int32)
    segment_packs = segment_ids.reshape(TOKENS // PACK, PACK)

    def forward(token_values, matrix_qkv, matrix_out, first_gain, second_gain, matrix_router, matrix_in, matrix_hidden):
        normed_one = low(layer_norm(token_values, low(first_gain)))
        qkv_weights = low(matrix_qkv)
        projected = [low_back(low(jnp.dot(normed_one, qkv_weights[member], precision=highest))).reshape(TOKENS // PACK, PACK, HEADS, HDIM) for member in range(3)]
        attended = lax.map(jax.checkpoint(attend_pack), (projected[0], projected[1], projected[2], segment_packs))
        attn_heads = low_back(low(attended.reshape(TOKENS, D)))
        residual = token_values + low_back(jnp.dot(attn_heads, low(matrix_out), precision=highest))
        normed_two = low(layer_norm(residual, low(second_gain)))
        logits = jnp.dot(normed_two, low(matrix_router), precision=highest)
        picked = lax.optimization_barrier(jnp.sum(jnp.where(pair_marks, logits[:, None, :], 0.0), axis=-1))
        gate_weights = jax.nn.softmax(picked, axis=-1)
        copies = low_back(jnp.repeat(normed_two, 2, axis=0))
        padded = jnp.concatenate([copies, jnp.zeros((1, D), copies.dtype)])
        expert_rows = padded[lookup]
        results = lax.map(jax.checkpoint(expert_block), (expert_rows, low(matrix_in), low(matrix_hidden)))
        flat_results = jnp.concatenate([results.reshape(-1, D), jnp.zeros((1, D), results.dtype)])
        back_pairs = flat_results[position].reshape(TOKENS, 2, D)
        return residual + lax.optimization_barrier(jnp.sum(gate_weights[:, :, None] * back_pairs, axis=1))
    token_values = tokens.astype(jnp.float32)
    output, pullback = jax.vjp(forward, token_values, weight_qkv, weight_out, gain_one, gain_two, weight_router, weight_in, weight_hidden)
    gradients = pullback(cotangent.astype(jnp.float32))
    return (output.astype(jnp.bfloat16), gradients[0], gradients[1], gradients[2], gradients[3], gradients[4], gradients[5], gradients[6], gradients[7])
```

```python
import jax
import jax.numpy as jnp
from jax import lax
from jax.experimental import pallas as pl
from jax.experimental.pallas import tpu as pltpu
from jax.sharding import PartitionSpec as P

HDIM = 64
PACK = 1024
SPAN = 64
BLOCK = 128
WINDOW = BLOCK + 2 * SPAN
CHUNK = 256
LANES = 128

EPSILON = 1e-05
NEGATIVE = -1e30

bfloat = jnp.bfloat16
single = jnp.float32
VMEM_LIMIT = 56 * 1024 * 1024


def dot_nn(a, b):
    return lax.dot_general(a, b, (((1,), (0,)), ((), ())), preferred_element_type=single)


def dot_nt(a, b):
    return lax.dot_general(a, b, (((1,), (1,)), ((), ())), preferred_element_type=single)


def dot_tn(a, b):
    return lax.dot_general(a, b, (((0,), (0,)), ((), ())), preferred_element_type=single)


def normalise(values):
    centered = values - jnp.mean(values, axis=-1, keepdims=True)
    inverse = lax.rsqrt(jnp.mean(centered * centered, axis=-1, keepdims=True) + EPSILON)
    return centered * inverse, inverse


def norm_pull(grad_normed, scaled, inverse, gain):
    weighted = grad_normed * gain
    return inverse * (
        weighted
        - jnp.mean(weighted, axis=-1, keepdims=True)
        - scaled * jnp.mean(weighted * scaled, axis=-1, keepdims=True)
    )


def split_heads(pair, first_half):
    zero = jnp.zeros_like(pair)
    return jnp.concatenate(
        [jnp.where(first_half, pair, zero), jnp.where(first_half, zero, pair)], axis=0
    )


def window_start(block, rows):
    return pl.multiple_of(jnp.clip(block * BLOCK - SPAN, 0, rows - WINDOW), SPAN)


def forward_kernel(
    tok, wqkv, wot, gain1, gain2, router, segc, segw, first, second,
    proj, attn, res, two, stat, gate,
):
    rows, width = tok.shape

    def project(step, carry):
        at = pl.ds(pl.multiple_of(step * CHUNK, CHUNK), CHUNK)
        scaled, _ = normalise(tok[at, :].astype(single))
        low = (scaled * gain1[...]).astype(bfloat)
        for part in range(3):
            proj[part, at, :] = dot_nn(low, wqkv[part]).astype(bfloat)
        return carry

    lax.fori_loop(0, rows // CHUNK, project, 0)
    lane = lax.broadcasted_iota(jnp.int32, (BLOCK, LANES), 1)
    first_half = lane < HDIM
    expert = lax.broadcasted_iota(jnp.int32, (router.shape[0], BLOCK), 0)

    def attend(block, carry):
        q_at = pl.ds(pl.multiple_of(block * BLOCK, BLOCK), BLOCK)
        k_at = pl.ds(window_start(block, rows), WINDOW)
        same = (segc[q_at, :] == segw[pl.ds(block, 1), :])[None]
        totals = jnp.zeros((BLOCK, LANES), single)
        for pair in range(width // LANES):
            cols = slice(pair * LANES, (pair + 1) * LANES)
            queries = split_heads(proj[0, q_at, cols] * HDIM**-0.5, first_half)
            scores = dot_nt(queries, proj[1, k_at, cols]).reshape(2, BLOCK, WINDOW)
            scores = jnp.where(same, scores, NEGATIVE)
            peak = jnp.max(scores, axis=-1, keepdims=True)
            exponent = jnp.exp(scores - peak)
            total = jnp.sum(exponent, axis=-1, keepdims=True)
            probs = (exponent * (1.0 / total)).astype(bfloat).reshape(2 * BLOCK, WINDOW)
            out = dot_nn(probs, proj[2, k_at, cols])
            attn[q_at, cols] = jnp.where(first_half, out[:BLOCK], out[BLOCK:]).astype(bfloat)
            log_total = peak + jnp.log(total)
            for half in range(2):
                totals = jnp.where(lane == 2 * pair + half, log_total[half], totals)
        stat[q_at, :] = totals
        residual = tok[q_at, :].astype(single) + dot_nt(attn[q_at, :], wot[...])
        res[q_at, :] = residual
        scaled, _ = normalise(residual)
        low = (scaled * gain2[...]).astype(bfloat)
        two[q_at, :] = low
        logits = dot_nt(router[...], low)
        mark0 = first[:, q_at] == expert
        mark1 = second[:, q_at] == expert
        logit0 = jnp.sum(jnp.where(mark0, logits, 0.0), axis=0, keepdims=True)
        logit1 = jnp.sum(jnp.where(mark1, logits, 0.0), axis=0, keepdims=True)
        top = jnp.maximum(logit0, logit1)
        part0, part1 = jnp.exp(logit0 - top), jnp.exp(logit1 - top)
        scale = 1.0 / (part0 + part1)
        gate[:, q_at] = jnp.where(mark0, part0 * scale, jnp.where(mark1, part1 * scale, 0.0))
        return carry

    lax.fori_loop(0, rows // BLOCK, attend, 0)


def backward_kernel(
    tok, cot, res, two, proj, attn, stat, wqkv, wot, gain1, gain2, router, segc, segw,
    gate, inner, copies,
    grad_tok, grad_w, grad_gain1, grad_gain2, grad_router,
    grad_res, grad_attn, grad_heads, grad_proj, grad_key, grad_value, normed,
):
    rows, width = tok.shape
    weights = gate[...]
    inner_products = inner[...]
    grad_logits = weights * (
        inner_products - jnp.sum(weights * inner_products, axis=0, keepdims=True)
    )
    logits_high = grad_logits.astype(bfloat)
    logits_low = (grad_logits - logits_high.astype(single)).astype(bfloat)
    grad_logits = jnp.concatenate([logits_high, logits_low], axis=0)
    router_twice = jnp.concatenate([router[...], router[...]], axis=0)
    count = router.shape[0]
    routed = dot_nn(grad_logits, two[...])
    grad_router[...] = routed[:count] + routed[count:]
    grad_gain1[...] = jnp.zeros_like(grad_gain1)
    grad_gain2[...] = jnp.zeros_like(grad_gain2)
    grad_key[...] = jnp.zeros_like(grad_key)
    grad_value[...] = jnp.zeros_like(grad_value)
    for step in range(rows // CHUNK):
        at = slice(step * CHUNK, (step + 1) * CHUNK)
        scaled, inverse = normalise(res[at, :])
        grad_normed = copies[at, :].astype(single) + dot_tn(grad_logits[:, at], router_twice)
        grad_gain2[...] += jnp.sum(grad_normed * scaled, axis=0, keepdims=True)
        grad_row = cot[at, :].astype(single) + norm_pull(grad_normed, scaled, inverse, gain2[...])
        grad_res[at, :] = grad_row
        low = grad_row.astype(bfloat)
        grad_attn[at, :] = low
        grad_heads[at, :] = dot_nn(low, wot[...]).astype(bfloat)
    grad_w[3] = dot_tn(grad_attn[...], attn[...]).astype(bfloat)
    lane = lax.broadcasted_iota(jnp.int32, (BLOCK, LANES), 1)
    first_half = lane < HDIM

    def attend(block, carry):
        q_at = pl.ds(pl.multiple_of(block * BLOCK, BLOCK), BLOCK)
        k_at = pl.ds(window_start(block, rows), WINDOW)
        same = (segc[q_at, :] == segw[pl.ds(block, 1), :])[None]
        totals = stat[q_at, :]
        for pair in range(width // LANES):
            cols = slice(pair * LANES, (pair + 1) * LANES)
            queries = split_heads(proj[0, q_at, cols] * HDIM**-0.5, first_half)
            keys_block = proj[1, k_at, cols]
            scores = dot_nt(queries, keys_block).reshape(2, BLOCK, WINDOW)
            scores = jnp.where(same, scores, NEGATIVE)
            log_total = jnp.stack([totals[:, 2 * pair : 2 * pair + 1], totals[:, 2 * pair + 1 : 2 * pair + 2]])
            probs = jnp.exp(scores - log_total).reshape(2 * BLOCK, WINDOW)
            heads = split_heads(grad_heads[q_at, cols], first_half)
            grad_probs = dot_nt(heads, proj[2, k_at, cols])
            delta = jnp.sum(probs * grad_probs, axis=-1, keepdims=True)
            grad_scores = (probs * (grad_probs - delta)).astype(bfloat)
            grad_query = dot_nn(grad_scores, keys_block) * HDIM**-0.5
            grad_proj[0, q_at, cols] = jnp.where(
                first_half, grad_query[:BLOCK], grad_query[BLOCK:]
            ).astype(bfloat)
            grad_key[k_at, cols] += dot_tn(grad_scores, queries)
            grad_value[k_at, cols] += dot_tn(probs.astype(bfloat), heads)
        return carry

    lax.fori_loop(0, rows // BLOCK, attend, 0)
    for step in range(rows // CHUNK):
        at = slice(step * CHUNK, (step + 1) * CHUNK)
        grad_proj[1, at, :] = grad_key[at, :].astype(bfloat)
        grad_proj[2, at, :] = grad_value[at, :].astype(bfloat)
        grad_normed = dot_nt(grad_proj[0, at, :], wqkv[0])
        for part in (1, 2):
            grad_normed += dot_nt(grad_proj[part, at, :], wqkv[part])
        scaled, inverse = normalise(tok[at, :].astype(single))
        normed[at, :] = (scaled * gain1[...]).astype(bfloat)
        grad_gain1[...] += jnp.sum(grad_normed * scaled, axis=0, keepdims=True)
        grad_tok[at, :] = grad_res[at, :] + norm_pull(grad_normed, scaled, inverse, gain1[...])
    for part in range(3):
        grad_w[part] = dot_tn(normed[...], grad_proj[part]).astype(bfloat)


def whole_call(kernel, out_shape, scratch=(), flops=0, moved=0):
    return pl.pallas_call(
        kernel,
        out_shape=out_shape,
        scratch_shapes=scratch,
        compiler_params=pltpu.CompilerParams(vmem_limit_bytes=VMEM_LIMIT),
        cost_estimate=pl.CostEstimate(flops=flops, bytes_accessed=moved, transcendentals=0),
    )


class Grid:
    names = ("zh", "zl", "y", "x", "c")

    def __init__(self, mesh):
        experts, heads = mesh.shape["expert"], mesh.shape["head"]
        self.shape = (2, experts // 4, 2, heads // 2, 2)
        self.experts, self.heads = experts, heads
        self.total = experts * heads

    def size(self, name):
        return self.shape[self.names.index(name)]

    def coords(self, linear):
        out = []
        for extent in reversed(self.shape):
            out.append(linear % extent)
            linear = linear // extent
        return dict(zip(self.names, reversed(out)))

    def linear(self, coords):
        at = 0
        for name, extent in zip(self.names, self.shape):
            at = at * extent + coords[name] % extent
        return at

    def me(self, name):
        linear = lax.axis_index("expert") * self.heads + lax.axis_index("head")
        return self.coords(linear)[name]

    def send(self, value, target):
        pairs = [(i, self.linear(target(self.coords(i)))) for i in range(self.total)]
        return lax.ppermute(value, ("expert", "head"), pairs)

    def shift(self, value, name, by):
        return self.send(value, lambda at: {**at, name: at[name] - by})

    def gather(self, value, name):
        extent, own = self.size(name), self.me(name)
        parts = [value] + [self.shift(value, name, by) for by in range(1, extent)]
        if extent == 2:
            return jnp.where(own == 0, jnp.stack(parts), jnp.stack(parts[::-1]))
        return jnp.roll(jnp.stack(parts), own, axis=0)

    def scatter_sum(self, value, name):
        extent, own = self.size(name), self.me(name)
        if extent == 2:
            kept = jnp.where(own == 0, value[0], value[1])
            others = [self.shift(jnp.where(own == 0, value[1], value[0]), name, 1)]
        else:
            value = jnp.roll(value, -own, axis=0)
            kept = value[0]
            others = [self.shift(value[by], name, -by) for by in range(1, extent)]
        total = kept.astype(single)
        for other in others:
            total = total + other.astype(single)
        return total.astype(value.dtype)


def gelu_tanh(values):
    return jax.nn.gelu(values, approximate=True)


def per_device(
    grid,
    tokens,
    segment_ids,
    task_ids,
    task_table,
    weight_qkv,
    weight_out,
    gain_one,
    gain_two,
    weight_router,
    weight_in,
    weight_hidden,
    cotangent,
):
    expert_count, head_count = grid.experts, grid.heads
    head_index = lax.axis_index("head")
    row_count, model_width = tokens.shape
    cap = 4 * row_count // expert_count
    deep, wide = weight_qkv.shape[1:]
    padded = -(-expert_count // 16) * 16

    pieces = jnp.concatenate([weight_qkv, weight_out.T[None]]).astype(bfloat)
    small = jnp.concatenate(
        [gain_one[None], gain_two[None], weight_router.T]
    ).astype(bfloat).reshape(-1)
    small_rows = -(-small.shape[0] // wide)
    small = jnp.pad(small, (0, small_rows * wide - small.shape[0])).reshape(small_rows, wide)
    packed = jnp.concatenate([pieces.reshape(4 * deep, wide), small])
    for name in ("zh", "zl", "y", "x", "c"):
        packed = grid.gather(packed, name)
    packed = packed.transpose(4, 3, 2, 1, 0, 5, 6).reshape(
        expert_count, head_count, 4 * deep + small_rows, wide
    )
    weights = (
        packed[:, :, : 4 * deep]
        .reshape(expert_count, head_count, 4, deep, wide)
        .transpose(2, 0, 3, 1, 4)
        .reshape(4, model_width, model_width)
    )
    smalls = packed[:, 0, 4 * deep :].reshape(expert_count, -1)[:, : (2 + expert_count) * deep]
    smalls = smalls.reshape(expert_count, 2 + expert_count, deep).transpose(1, 0, 2)
    smalls = smalls.reshape(2 + expert_count, model_width)
    gain1, gain2 = smalls[0:1].astype(single), smalls[1:2].astype(single)
    router = jnp.pad(smalls[2:], ((0, padded - expert_count), (0, 0)))
    wqkv, wot = weights[:3], weights[3]

    own_segments = lax.dynamic_slice_in_dim(segment_ids, head_index * row_count, row_count)
    chosen = task_table[task_ids[own_segments]]
    expert_range = jnp.arange(expert_count, dtype=jnp.int32)
    flat_choice = chosen.reshape(-1)
    expert_marks = (flat_choice[:, None] == expert_range).astype(jnp.int32)
    running = jnp.cumsum(expert_marks, axis=0)
    slot_index = jnp.sum((running - 1) * expert_marks, axis=1)
    destination = jnp.where(slot_index < cap, flat_choice * cap + slot_index, expert_count * cap)
    first, second = chosen[:, 0][None], chosen[:, 1][None]
    segc = own_segments[:, None]
    starts = [min(max(at - SPAN, 0), row_count - WINDOW) for at in range(0, row_count, BLOCK)]
    segw = jnp.stack([own_segments[at : at + WINDOW] for at in starts])

    shape = jax.ShapeDtypeStruct
    proj, attn, res, two_low, stat, gate = whole_call(
        forward_kernel,
        (
            shape((3, row_count, model_width), bfloat),
            shape((row_count, model_width), bfloat),
            shape((row_count, model_width), single),
            shape((row_count, model_width), bfloat),
            shape((row_count, LANES), single),
            shape((padded, row_count), single),
        ),
        flops=2 * 5 * row_count * model_width**2,
        moved=16 * row_count * model_width,
    )(tokens, wqkv, wot, gain1, gain2, router, segc, segw, first, second)

    expert_in = lax.all_gather(weight_in.astype(bfloat), "head", axis=1, tiled=True)[0]
    expert_hidden = lax.all_gather(weight_hidden.astype(bfloat), "head", axis=1, tiled=True)[0]
    pair_marks = chosen[:, :, None] == expert_range
    gate_weights = jnp.sum(jnp.where(pair_marks, gate[:expert_count].T[:, None, :], 0.0), axis=-1)
    send_rows = (
        jnp.zeros((expert_count * cap + 1, model_width), bfloat)
        .at[destination]
        .set(jnp.repeat(two_low, 2, axis=0))
    )
    send_rows = send_rows[:-1].reshape(expert_count, cap, model_width)
    received = lax.all_to_all(send_rows, "expert", split_axis=0, concat_axis=0, tiled=True)
    flat_in = received.reshape(-1, model_width)
    hidden_pre = jnp.dot(flat_in, expert_in, preferred_element_type=single)
    activated, gelu_pullback = jax.vjp(gelu_tanh, hidden_pre)
    act_low = activated.astype(bfloat)
    results = jnp.dot(act_low, expert_hidden, preferred_element_type=single).astype(bfloat)
    returned = lax.all_to_all(
        results.reshape(expert_count, cap, model_width),
        "expert",
        split_axis=0,
        concat_axis=0,
        tiled=True,
    )
    zero_row = jnp.zeros((1, model_width), bfloat)
    back_pairs = (
        jnp.concatenate([returned.reshape(-1, model_width), zero_row])[destination]
        .astype(single)
        .reshape(row_count, 2, model_width)
    )
    output = (res + jnp.sum(gate_weights[:, :, None] * back_pairs, axis=1)).astype(bfloat)
    grad_top = cotangent.astype(single)
    grad_pairs = (
        (gate_weights[:, :, None] * grad_top[:, None, :]).reshape(-1, model_width).astype(bfloat)
    )
    send_grad = (
        jnp.zeros((expert_count * cap + 1, model_width), bfloat).at[destination].set(grad_pairs)
    )
    send_grad = send_grad[:-1].reshape(expert_count, cap, model_width)
    grad_gates = jnp.sum(back_pairs * grad_top[:, None, :], axis=-1)
    inner = jnp.sum(jnp.where(pair_marks, grad_gates[:, :, None], 0.0), axis=1)
    inner = jnp.pad(inner, ((0, 0), (0, padded - expert_count))).T
    grad_results = lax.all_to_all(send_grad, "expert", split_axis=0, concat_axis=0, tiled=True)
    flat_grad = grad_results.reshape(-1, model_width)
    grad_act = jnp.einsum("rd,fd->rf", flat_grad, expert_hidden, preferred_element_type=single)
    grad_hidden_local = jnp.einsum("rf,rd->fd", act_low, flat_grad, preferred_element_type=single)
    grad_pre = gelu_pullback(grad_act)[0].astype(bfloat)
    grad_in_local = jnp.einsum("rd,rf->df", flat_in, grad_pre, preferred_element_type=single)
    grad_rows = jnp.einsum("rf,df->rd", grad_pre, expert_in, preferred_element_type=single).astype(
        bfloat
    )
    grad_back = lax.all_to_all(
        grad_rows.reshape(expert_count, cap, model_width),
        "expert",
        split_axis=0,
        concat_axis=0,
        tiled=True,
    )
    grad_copies = jnp.concatenate([grad_back.reshape(-1, model_width), zero_row])[
        destination
    ].astype(single)
    grad_copies = jnp.sum(grad_copies.reshape(row_count, 2, model_width), axis=1)

    grad_tokens, grad_w, grad_gain1, grad_gain2, grad_router = whole_call(
        backward_kernel,
        (
            shape((row_count, model_width), single),
            shape((4, model_width, model_width), bfloat),
            shape((1, model_width), single),
            shape((1, model_width), single),
            shape((padded, model_width), single),
        ),
        scratch=[
            pltpu.VMEM((row_count, model_width), single),
            pltpu.VMEM((row_count, model_width), bfloat),
            pltpu.VMEM((row_count, model_width), bfloat),
            pltpu.VMEM((3, row_count, model_width), bfloat),
            pltpu.VMEM((row_count, model_width), single),
            pltpu.VMEM((row_count, model_width), single),
            pltpu.VMEM((row_count, model_width), bfloat),
        ],
        flops=2 * 10 * row_count * model_width**2,
        moved=24 * row_count * model_width,
    )(
        tokens, cotangent, res, two_low, proj, attn, stat, wqkv, wot, gain1, gain2, router,
        segc, segw, gate, inner, grad_copies,
    )

    pieces = (
        grad_w.reshape(4, expert_count, deep, head_count, wide)
        .transpose(1, 3, 0, 2, 4)
        .reshape(expert_count, head_count, 4 * deep, wide)
    )
    smalls = jnp.concatenate([grad_gain1, grad_gain2, grad_router[:expert_count]]).astype(bfloat)
    smalls = smalls.reshape(2 + expert_count, expert_count, deep).transpose(1, 0, 2)
    smalls = smalls.reshape(expert_count, -1)
    smalls = jnp.pad(smalls, ((0, 0), (0, small_rows * wide - smalls.shape[1])))
    smalls = jnp.broadcast_to(
        smalls.reshape(expert_count, 1, small_rows, wide),
        (expert_count, head_count, small_rows, wide),
    )
    packed = jnp.concatenate([pieces, smalls], axis=2)
    packed = packed.reshape(*grid.shape, 4 * deep + small_rows, wide).transpose(4, 3, 2, 1, 0, 5, 6)
    for name in ("c", "x", "y", "zl", "zh"):
        packed = grid.scatter_sum(packed, name)
    pieces = packed[: 4 * deep].reshape(4, deep, wide).astype(single)
    smalls = packed[4 * deep :].reshape(-1)[: (2 + expert_count) * deep].astype(single)
    smalls = smalls.reshape(2 + expert_count, deep)
    expert_totals = (
        lax.psum_scatter(
            grad_in_local[None].astype(jnp.bfloat16), "head", scatter_dimension=1, tiled=True
        ).astype(jnp.float32),
        lax.psum_scatter(
            grad_hidden_local[None].astype(jnp.bfloat16), "head", scatter_dimension=1, tiled=True
        ).astype(jnp.float32),
    )
    return (
        output,
        grad_tokens,
        pieces[:3],
        pieces[3].T,
        smalls[0],
        smalls[1],
        smalls[2:].T,
        expert_totals[0],
        expert_totals[1],
    )


def solution(mesh):
    grid = Grid(mesh)
    placed = (
        P(("expert", "head"), None),
        P("expert"),
        P(),
        P(),
        P(None, "expert", "head"),
        P("head", "expert"),
        P("expert"),
        P("expert"),
        P("expert", None),
        P("expert", "head", None),
        P("expert", "head", None),
        P(("expert", "head"), None),
    )

    def step(*arrays):
        return per_device(grid, *arrays)

    return jax.shard_map(
        step,
        mesh=mesh,
        in_specs=placed,
        out_specs=(
            P(("expert", "head"), None),
            P(("expert", "head"), None),
            P(None, "expert", "head"),
            P("head", "expert"),
            P("expert"),
            P("expert"),
            P("expert", None),
            P("expert", "head", None),
            P("expert", "head", None),
        ),
        check_vma=False,
    )
```

```python
import jax
import jax.numpy as jnp
from jax import lax
from jax.experimental import pallas as pl
from jax.experimental.pallas import tpu as pltpu
from jax.sharding import PartitionSpec as P

HDIM = 64
PACK = 1024
SPAN = 64
BLOCK = 128
WINDOW = BLOCK + 2 * SPAN
CHUNK = 256
LANES = 128
TILE = 256
HALF = 128
EXTRA = 16
ABSENT = -1e6

EPSILON = 1e-05
NEGATIVE = -1e30

bfloat = jnp.bfloat16
single = jnp.float32
VMEM_LIMIT = 56 * 1024 * 1024


def dot_nn(a, b):
    return lax.dot_general(a, b, (((1,), (0,)), ((), ())), preferred_element_type=single)


def dot_nt(a, b):
    return lax.dot_general(a, b, (((1,), (1,)), ((), ())), preferred_element_type=single)


def dot_tn(a, b):
    return lax.dot_general(a, b, (((0,), (0,)), ((), ())), preferred_element_type=single)


def normalise(values):
    centered = values - jnp.mean(values, axis=-1, keepdims=True)
    inverse = lax.rsqrt(jnp.mean(centered * centered, axis=-1, keepdims=True) + EPSILON)
    return centered * inverse, inverse


def norm_pull(grad_normed, scaled, inverse, gain):
    weighted = grad_normed * gain
    return inverse * (
        weighted
        - jnp.mean(weighted, axis=-1, keepdims=True)
        - scaled * jnp.mean(weighted * scaled, axis=-1, keepdims=True)
    )


def split_heads(pair, first_half):
    zero = jnp.zeros_like(pair)
    return jnp.concatenate(
        [jnp.where(first_half, pair, zero), jnp.where(first_half, zero, pair)], axis=0
    )


def window_start(block, rows):
    return pl.multiple_of(jnp.clip(block * BLOCK - SPAN, 0, rows - WINDOW), SPAN)


def fetch_weights(heads, core, own, other, weights, sem):
    wide = weights.shape[2] // heads
    copies = []
    if own.shape == weights.shape:
        copies = [pltpu.make_async_copy(own, weights, sem.at[0, 0])]
        heads = 0
    for by in range(heads // 2):
        for i, (ref, at) in enumerate(((own, core), (other, 1 - core))):
            start = (2 * by + at) * wide
            start = pl.multiple_of(start, LANES)
            copies.append(
                pltpu.make_async_copy(
                    ref.at[:, :, pl.ds(by * wide, wide)],
                    weights.at[:, :, pl.ds(start, wide)],
                    sem.at[i, by],
                )
            )
    for copy in copies:
        copy.start()
    for copy in copies:
        copy.wait()


def forward_kernel(
    cap, heads, meta, tok, weights_own, weights_other, gain1, gain2, router, segc, segw, first, second, slots,
    proj, attn, res, two, stat, gate, *refs,
):
    *parcels, weights, sem = refs
    rows, width = tok.shape
    fetch_weights(heads, meta[4 * len(parcels)], weights_own, weights_other, weights, sem)
    wqkv, wot = weights, weights.at[3]

    def project(step, carry):
        at = pl.ds(pl.multiple_of(step * CHUNK, CHUNK), CHUNK)
        scaled, _ = normalise(tok[at, :].astype(single))
        low = (scaled * gain1[...]).astype(bfloat)
        for part in range(3):
            proj[part, at, :] = dot_nn(low, wqkv[part]).astype(bfloat)
        return carry

    lax.fori_loop(0, rows // CHUNK, project, 0)
    lane = lax.broadcasted_iota(jnp.int32, (BLOCK, LANES), 1)
    first_half = lane < HDIM
    expert = lax.broadcasted_iota(jnp.int32, (router.shape[0], BLOCK), 0)

    def attend(block, carry):
        q_at = pl.ds(pl.multiple_of(block * BLOCK, BLOCK), BLOCK)
        k_at = pl.ds(window_start(block, rows), WINDOW)
        same = (segc[q_at, :] == segw[pl.ds(block, 1), :])[None]
        totals = jnp.zeros((BLOCK, LANES), single)
        for pair in range(width // LANES):
            cols = slice(pair * LANES, (pair + 1) * LANES)
            queries = split_heads(proj[0, q_at, cols] * HDIM**-0.5, first_half)
            scores = dot_nt(queries, proj[1, k_at, cols]).reshape(2, BLOCK, WINDOW)
            scores = jnp.where(same, scores, NEGATIVE)
            peak = jnp.max(scores, axis=-1, keepdims=True)
            exponent = jnp.exp(scores - peak)
            total = jnp.sum(exponent, axis=-1, keepdims=True)
            probs = (exponent * (1.0 / total)).astype(bfloat).reshape(2 * BLOCK, WINDOW)
            out = dot_nn(probs, proj[2, k_at, cols])
            attn[q_at, cols] = jnp.where(first_half, out[:BLOCK], out[BLOCK:]).astype(bfloat)
            log_total = peak + jnp.log(total)
            for half in range(2):
                totals = jnp.where(lane == 2 * pair + half, log_total[half], totals)
        stat[q_at, :] = totals
        residual = tok[q_at, :].astype(single) + dot_nt(attn[q_at, :], wot[...])
        res[q_at, :] = residual
        scaled, _ = normalise(residual)
        low = (scaled * gain2[...]).astype(bfloat)
        two[q_at, :] = low
        logits = dot_nt(router[...], low)
        mark0 = first[:, q_at] == expert
        mark1 = second[:, q_at] == expert
        logit0 = jnp.sum(jnp.where(mark0, logits, 0.0), axis=0, keepdims=True)
        logit1 = jnp.sum(jnp.where(mark1, logits, 0.0), axis=0, keepdims=True)
        top = jnp.maximum(logit0, logit1)
        part0, part1 = jnp.exp(logit0 - top), jnp.exp(logit1 - top)
        scale = 1.0 / (part0 + part1)
        gate[:, q_at] = jnp.where(mark0, part0 * scale, jnp.where(mark1, part1 * scale, 0.0))
        return carry

    lax.fori_loop(0, rows // BLOCK, attend, 0)
    pack_parcels(cap, meta, two, slots, parcels)


def pack_parcels(cap, meta, rows, slots, parcels):
    tile = min(TILE, cap)
    for at, parcel in enumerate(parcels):
        for local in range(2):
            for step in range(cap // tile):

                @pl.when(meta[2 * len(parcels) + 2 * at + local] > step * tile)
                def _():
                    ones = onehot(slots[pl.ds(meta[2 * at + local], 1), :], step * tile, tile)
                    parcel[local * cap + step * tile : local * cap + (step + 1) * tile, :] = dot_nn(
                        ones, rows[...]
                    ).astype(bfloat)


def split_two(values):
    high = values.astype(bfloat)
    return high, (values - high.astype(single)).astype(bfloat)


def pack_rows(rows):
    at = lax.broadcasted_iota(jnp.int32, (EXTRA, rows.shape[1]), 0)
    out = jnp.zeros((EXTRA, rows.shape[1]), single)
    for local in range(2):
        high = rows[local : local + 1, :].astype(bfloat).astype(single)
        out = jnp.where(at == 2 * local, high, out)
        out = jnp.where(at == 2 * local + 1, rows[local : local + 1, :] - high, out)
    return out.astype(bfloat)


def unpack_row(packed, local):
    packed = packed.astype(single)
    return packed[2 * local : 2 * local + 1, :] + packed[2 * local + 1 : 2 * local + 2, :]


def routing_kernel(
    cap, segments, tasks, table, weight_in, weight_hidden,
    first, second, slots, other, kept, piece,
):
    rows = segments.shape[1]
    deep, hidden = weight_in.shape[1:]
    width = piece.shape[1]
    for part in range(hidden // width):
        piece[part * deep : (part + 1) * deep, :] = weight_in[
            0, :, part * width : (part + 1) * width
        ].astype(bfloat)
    piece[hidden // width * deep :, :] = weight_hidden[0].astype(bfloat)
    names = lax.broadcasted_iota(jnp.int32, (table.shape[1], tasks.shape[1]), 0)
    experts = dot_nn(table[...], jnp.where(names == tasks[...], 1.0, 0.0).astype(bfloat))
    experts = experts.astype(bfloat)
    chosen = jnp.zeros((table.shape[0], rows), single)
    for start in range(0, tasks.shape[1], 1024):
        size = min(1024, tasks.shape[1] - start)
        at = lax.broadcasted_iota(jnp.int32, (size, rows), 0) + start
        ones = jnp.where(at == segments[...], 1.0, 0.0).astype(bfloat)
        chosen = chosen + dot_nn(experts[:, start : start + size], ones)
    zero, one = chosen[0:1, :], chosen[1:2, :]
    first[...] = zero.astype(jnp.int32)
    second[...] = one.astype(jnp.int32)
    which = lax.broadcasted_iota(jnp.int32, slots.shape, 0).astype(single)
    is_first, is_second = which == zero, which == one
    other[...] = jnp.where(is_first, one, jnp.where(is_second, zero, 0.0))
    marks = jnp.where(is_first | is_second, 1.0, 0.0)
    earlier = lax.broadcasted_iota(jnp.int32, (rows, rows), 0) < lax.broadcasted_iota(
        jnp.int32, (rows, rows), 1
    )
    places = dot_nn(marks.astype(bfloat), jnp.where(earlier, 1.0, 0.0).astype(bfloat))
    inside = (marks > 0.5) & (places < cap)
    slots[...] = jnp.where(inside, places, ABSENT)
    total = jnp.sum(jnp.where(inside, 1.0, 0.0), axis=1, keepdims=True)
    kept[...] = jnp.broadcast_to(total, kept.shape).astype(jnp.int32)


def cotangent_kernel(cap, meta, cot, slots, other, waited, *parcels):
    pack_parcels(cap, meta, cot, slots, parcels)
    tile = min(TILE, cap)
    at_row = lax.broadcasted_iota(jnp.int32, (EXTRA, tile), 0)
    which = lax.broadcasted_iota(jnp.int32, (other.shape[0], 1), 0)
    others = other[...].astype(bfloat)
    for at, parcel in enumerate(parcels):
        for step in range(cap // tile):
            out = jnp.zeros((EXTRA, tile), single)
            for local in range(2):
                chosen = meta[2 * at + local]
                number = meta[2 * len(parcels) + 2 * at + local]
                ones = onehot(slots[pl.ds(chosen, 1), :], step * tile, tile)
                moved = dot_nt(others, ones)
                moved = jnp.sum(jnp.where(which == chosen, moved, 0.0), axis=0, keepdims=True)
                high = number // 16 * 16
                out = jnp.where(at_row == local, moved, out)
                out = jnp.where(at_row == 2 + 2 * local, high.astype(single), out)
                out = jnp.where(at_row == 3 + 2 * local, (number - high).astype(single), out)
            parcel[2 * cap :, step * tile : (step + 1) * tile] = out.astype(bfloat)


def output_kernel(providers, cap, meta, res, slots, *refs):
    parcels, out = refs[:providers], refs[providers]
    for step in range(res.shape[0] // CHUNK):
        at = slice(step * CHUNK, (step + 1) * CHUNK)
        out[at, :] = (res[at, :] + returned_rows(parcels, cap, meta, slots, at)).astype(bfloat)


def returned_rows(parcels, cap, meta, slots, at):
    total = 0.0
    for provider, parcel in enumerate(parcels):
        for local in range(2):
            ones = onehot(slots[pl.ds(meta[2 * provider + local], 1), at], 0, cap)
            total = total + dot_tn(ones, parcel[local * cap : (local + 1) * cap, :])
    return total


def backward_kernel(
    providers, cap, heads, waited, meta,
    tok, cot, res, two, proj, attn, stat, weights_own, weights_other, gain1, gain2, router, segc, segw, gate, slots,
    *refs,
):
    parcels = refs[:providers]
    (
        grad_tok, grad_w, grad_gain1, grad_gain2, grad_router,
        products, grad_res, grad_attn, grad_heads, grad_proj, grad_key, grad_value, normed,
        weights, sem,
    ) = refs[providers + waited :]
    rows, width = tok.shape
    fetch_weights(heads, meta[4 * providers], weights_own, weights_other, weights, sem)
    wqkv, wot = weights, weights.at[3]
    products[...] = jnp.zeros_like(products)
    for provider in range(providers):
        for local in range(2):
            chosen = meta[2 * provider + local]
            ones = onehot(slots[pl.ds(chosen, 1), :], 0, cap)
            moved = dot_nn(parcels[provider][2 * cap :, :cap], ones)
            products[pl.ds(chosen, 1), :] = unpack_row(moved, local)
    gates = gate[...]
    inner_products = products[...]
    grad_logits = gates * (
        inner_products - jnp.sum(gates * inner_products, axis=0, keepdims=True)
    )
    logits_high = grad_logits.astype(bfloat)
    logits_low = (grad_logits - logits_high.astype(single)).astype(bfloat)
    grad_logits = jnp.concatenate([logits_high, logits_low], axis=0)
    router_twice = jnp.concatenate([router[...], router[...]], axis=0)
    count = router.shape[0]
    routed = dot_nn(grad_logits, two[...])
    grad_router[...] = routed[:count] + routed[count:]
    grad_gain1[...] = jnp.zeros_like(grad_gain1)
    grad_gain2[...] = jnp.zeros_like(grad_gain2)
    grad_key[...] = jnp.zeros_like(grad_key)
    grad_value[...] = jnp.zeros_like(grad_value)
    for step in range(rows // CHUNK):
        at = slice(step * CHUNK, (step + 1) * CHUNK)
        scaled, inverse = normalise(res[at, :])
        grad_normed = dot_tn(grad_logits[:, at], router_twice)
        grad_normed = grad_normed + returned_rows(parcels, cap, meta, slots, at)
        grad_gain2[...] += jnp.sum(grad_normed * scaled, axis=0, keepdims=True)
        grad_row = cot[at, :].astype(single) + norm_pull(grad_normed, scaled, inverse, gain2[...])
        grad_res[at, :] = grad_row
        low = grad_row.astype(bfloat)
        grad_attn[at, :] = low
        grad_heads[at, :] = dot_nn(low, wot[...]).astype(bfloat)
    grad_w[3] = dot_tn(grad_attn[...], attn[...]).astype(bfloat)
    lane = lax.broadcasted_iota(jnp.int32, (BLOCK, LANES), 1)
    first_half = lane < HDIM

    def attend(block, carry):
        q_at = pl.ds(pl.multiple_of(block * BLOCK, BLOCK), BLOCK)
        k_at = pl.ds(window_start(block, rows), WINDOW)
        same = (segc[q_at, :] == segw[pl.ds(block, 1), :])[None]
        totals = stat[q_at, :]
        for pair in range(width // LANES):
            cols = slice(pair * LANES, (pair + 1) * LANES)
            queries = split_heads(proj[0, q_at, cols] * HDIM**-0.5, first_half)
            keys_block = proj[1, k_at, cols]
            scores = dot_nt(queries, keys_block).reshape(2, BLOCK, WINDOW)
            scores = jnp.where(same, scores, NEGATIVE)
            log_total = jnp.stack([totals[:, 2 * pair : 2 * pair + 1], totals[:, 2 * pair + 1 : 2 * pair + 2]])
            probs = jnp.exp(scores - log_total).reshape(2 * BLOCK, WINDOW)
            heads = split_heads(grad_heads[q_at, cols], first_half)
            grad_probs = dot_nt(heads, proj[2, k_at, cols])
            delta = jnp.sum(probs * grad_probs, axis=-1, keepdims=True)
            grad_scores = (probs * (grad_probs - delta)).astype(bfloat)
            grad_query = dot_nn(grad_scores, keys_block) * HDIM**-0.5
            grad_proj[0, q_at, cols] = jnp.where(
                first_half, grad_query[:BLOCK], grad_query[BLOCK:]
            ).astype(bfloat)
            grad_key[k_at, cols] += dot_tn(grad_scores, queries)
            grad_value[k_at, cols] += dot_tn(probs.astype(bfloat), heads)
        return carry

    lax.fori_loop(0, rows // BLOCK, attend, 0)
    for step in range(rows // CHUNK):
        at = slice(step * CHUNK, (step + 1) * CHUNK)
        grad_proj[1, at, :] = grad_key[at, :].astype(bfloat)
        grad_proj[2, at, :] = grad_value[at, :].astype(bfloat)
        grad_normed = dot_nt(grad_proj[0, at, :], wqkv[0])
        for part in (1, 2):
            grad_normed += dot_nt(grad_proj[part, at, :], wqkv[part])
        scaled, inverse = normalise(tok[at, :].astype(single))
        normed[at, :] = (scaled * gain1[...]).astype(bfloat)
        grad_gain1[...] += jnp.sum(grad_normed * scaled, axis=0, keepdims=True)
        grad_tok[at, :] = grad_res[at, :] + norm_pull(grad_normed, scaled, inverse, gain1[...])
    for part in range(3):
        grad_w[part] = dot_tn(normed[...], grad_proj[part]).astype(bfloat)


def onehot(slots, base, rows):
    places = lax.broadcasted_iota(jnp.int32, (rows, slots.shape[1]), 0).astype(single)
    return jnp.where(places == slots - base, 1.0, 0.0).astype(bfloat)


def gelu_both(values):
    square = values * values
    rate = 0.7978845608028654 + 0.035677408136300125 * square
    slope = 0.7978845608028654 + 0.10703222440890037 * square
    bent = jnp.tanh(values * rate)
    half = 0.5 + 0.5 * bent
    return values * half, half + values * (0.5 - 0.5 * (bent * bent)) * slope


def expert_kernel(sources, heads, first, meta, router, *refs):
    refs = list(refs)

    def take(count):
        taken = refs[:count]
        del refs[:count]
        return taken

    rows_in, grads_in = take(sources), take(sources)
    pieces = take(2 * heads)
    if not first:
        take(4)
    saved = take(4)
    outs, grads = take(sources), take(sources)
    (
        win, wout, row_buf, grad_buf, out_buf, copy_buf, product_buf, top,
        st_x, st_g, st_act, st_pre, table, w_sem, in_sem, s_sem, out_sem,
    ) = refs
    width = row_buf.shape[2]
    cap = row_buf.shape[1] // 2
    hidden = wout.shape[1]
    deep, wide = width // heads, hidden // heads
    head_x, head_c = meta[0], meta[1]
    staged = (st_x, st_g, st_act, st_pre)

    def weight_copies(local):
        at = 0
        for by_x in range(heads // 2):
            for by_c in range(2):
                head = lax.rem(head_x + by_x, heads // 2) * 2 + lax.rem(head_c + by_c, 2)
                piece = pieces[(local * (heads // 2) + by_x) * 2 + by_c]
                for part in range(hidden // width):
                    yield pltpu.make_async_copy(
                        piece.at[pl.ds(part * deep, deep), :],
                        win.at[
                            local,
                            pl.ds(pl.multiple_of(head * deep, deep), deep),
                            pl.ds(part * width, width),
                        ],
                        w_sem.at[local, at],
                    )
                    at += 1
                yield pltpu.make_async_copy(
                    piece.at[pl.ds(hidden // width * deep, wide), :],
                    wout.at[local, pl.ds(pl.multiple_of(head * wide, wide), wide), :],
                    w_sem.at[local, at],
                )
                at += 1

    def source_copies():
        for source in range(sources):
            yield pltpu.make_async_copy(rows_in[source], row_buf.at[source], in_sem.at[0, source])
            yield pltpu.make_async_copy(grads_in[source], grad_buf.at[source], in_sem.at[1, source])

    for copy in weight_copies(0):
        copy.start()
    for copy in source_copies():
        copy.start()
    for copy in weight_copies(1):
        copy.start()
    out_buf[...] = jnp.zeros_like(out_buf)
    copy_buf[...] = jnp.zeros_like(copy_buf)
    product_buf[...] = jnp.zeros_like(product_buf)

    def save_copies(slot, local, tile):
        at = pl.ds(pl.multiple_of(tile * TILE, TILE), TILE)
        return [
            pltpu.make_async_copy(stage.at[slot], save.at[local, at, :], s_sem.at[slot, i])
            for i, (stage, save) in enumerate(zip(staged, saved))
        ]

    halves = []
    for local in range(2):
        number = 0
        for source in range(sources):
            for half in range(cap // HALF):
                table[local, number] = source * (cap // HALF) + half
                filled = meta[6 + local * sources + source] > half * HALF
                number = number + jnp.where(filled, 1, 0)
        halves.append(number)
    eye = lax.broadcasted_iota(jnp.int32, (HALF, HALF), 0) == lax.broadcasted_iota(
        jnp.int32, (HALF, HALF), 1
    )
    column = lax.broadcasted_iota(jnp.int32, (HALF, LANES), 1).astype(single)
    for copy in source_copies():
        copy.wait()
    done = 0
    for local in range(2):
        for copy in weight_copies(local):
            copy.wait()
        number = halves[local]

        def place(tile, half):
            entry = table[local, 2 * tile + half]
            step = lax.rem(entry, cap // HALF)
            start = pl.multiple_of(step * HALF, HALF)
            rows = pl.ds(pl.multiple_of(local * cap + start, HALF), HALF)
            return entry // (cap // HALF), rows, pl.ds(start, HALF)

        def one_tile(tile, done):
            slot = lax.rem(done, 2)

            @pl.when(done >= 2)
            def _():
                for copy in save_copies(slot, local, tile):
                    copy.wait()

            for half in range(2):
                at = pl.ds(half * HALF, HALF)

                @pl.when(2 * tile + half < number)
                def _():
                    source, rows, lanes = place(tile, half)
                    st_x[slot, at, :] = row_buf[source, rows, :]
                    other = grad_buf[source, pl.ds(2 * cap, EXTRA), lanes].astype(single)
                    other = jnp.where(eye, other[local : local + 1, :], 0.0)
                    other = jnp.sum(other, axis=1, keepdims=True)
                    logits = dot_nt(row_buf[source, rows, :], router[...])
                    own = meta[2 + local].astype(single)
                    own = jnp.sum(jnp.where(column == own, logits, 0.0), axis=1, keepdims=True)
                    other = jnp.sum(jnp.where(column == other, logits, 0.0), axis=1, keepdims=True)
                    peak = jnp.maximum(own, other)
                    own, other = jnp.exp(own - peak), jnp.exp(other - peak)
                    gate = own / (own + other)
                    grad = grad_buf[source, rows, :]
                    top[at, :width] = grad.astype(single)
                    top[at, width:] = jnp.broadcast_to(gate, (HALF, LANES))
                    st_g[slot, at, :] = (gate * grad.astype(single)).astype(bfloat)

                @pl.when(2 * tile + half >= number)
                def _():
                    st_x[slot, at, :] = jnp.zeros((HALF, width), bfloat)
                    st_g[slot, at, :] = jnp.zeros((HALF, width), bfloat)
                    top[at, :] = jnp.zeros((HALF, width + LANES), single)

            rows_low, grad_low = st_x[slot], st_g[slot]
            for part in range(hidden // width):
                cols = slice(part * width, (part + 1) * width)
                pre = dot_nn(rows_low, win[local, :, cols])
                grad_act = dot_nt(grad_low, wout[local, cols, :])
                act, slope = gelu_both(pre)
                st_act[slot, :, cols] = act.astype(bfloat)
                st_pre[slot, :, cols] = (slope * grad_act).astype(bfloat)
            result = dot_nn(st_act[slot], wout[local]).astype(bfloat).astype(single)
            grad_copy = dot_nt(st_pre[slot], win[local]).astype(bfloat)
            product = jnp.sum(top[:, :width] * result, axis=1, keepdims=True)
            weighted = (top[:, width : width + 1] * result).astype(bfloat)
            for half in range(2):
                at = slice(half * HALF, (half + 1) * HALF)

                @pl.when(2 * tile + half < number)
                def _():
                    source, rows, lanes = place(tile, half)
                    out_buf[source, rows, :] = weighted[at]
                    copy_buf[source, rows, :] = grad_copy[at]
                    product_buf[source, local : local + 1, lanes] = jnp.sum(
                        jnp.where(eye, product[at], 0.0), axis=0, keepdims=True
                    )

            for copy in save_copies(slot, local, meta[4 + local] + tile):
                copy.start()
            return done + 1

        done = lax.fori_loop(0, (number + 1) // 2, one_tile, done)

    def result_copies():
        for source in range(sources):
            yield pltpu.make_async_copy(copy_buf.at[source], grads[source], out_sem.at[0, source])
            yield pltpu.make_async_copy(out_buf.at[source], outs[source], out_sem.at[1, source])

    for source in range(sources):
        copy_buf[source, 2 * cap :, :cap] = pack_rows(product_buf[source])
    for copy in result_copies():
        copy.start()
    for back in (1, 2):

        @pl.when(done >= back)
        def _():
            for copy in save_copies(lax.rem(done - back, 2), 0, 0):
                copy.wait()

    for copy in result_copies():
        copy.wait()


def weight_kernel(heads, meta, save_x, save_g, save_act, save_pre, *refs):
    outs = refs[: 2 * heads]
    grad_in, grad_out, buf_x, buf_g, buf_act, buf_pre, sem = refs[2 * heads :]
    width, hidden = grad_in.shape
    deep, wide = width // heads, hidden // heads
    buffers = (buf_x, buf_g, buf_act, buf_pre)

    def fetch(slot, local, tile):
        at = pl.ds(pl.multiple_of(tile * TILE, TILE), TILE)
        return [
            pltpu.make_async_copy(save.at[local, at, :], buf.at[slot], sem.at[slot, i])
            for i, (save, buf) in enumerate(zip((save_x, save_g, save_act, save_pre), buffers))
        ]

    for local in (1, 0):
        tiles = meta[2 + local]
        grad_in[...] = jnp.zeros_like(grad_in)
        grad_out[...] = jnp.zeros_like(grad_out)

        @pl.when(tiles > 0)
        def _():
            for copy in fetch(0, local, 0):
                copy.start()

        def one_tile(tile, carry):
            slot = lax.rem(tile, 2)

            @pl.when(tile + 1 < tiles)
            def _():
                for copy in fetch(1 - slot, local, tile + 1):
                    copy.start()

            for copy in fetch(slot, local, tile):
                copy.wait()
            for part in range(hidden // width):
                cols = slice(part * width, (part + 1) * width)
                grad_in[:, cols] += dot_tn(buf_x[slot], buf_pre[slot, :, cols])
                grad_out[:, cols] += dot_tn(buf_g[slot], buf_act[slot, :, cols])
            return carry

        lax.fori_loop(0, tiles, one_tile, 0)
        for by_x in range(heads // 2):
            for by_c in range(2):
                head = lax.rem(meta[0] + by_x, heads // 2) * 2 + lax.rem(meta[1] + by_c, 2)
                out = outs[(local * (heads // 2) + by_x) * 2 + by_c]
                for part in range(hidden // width):
                    out[part * deep : (part + 1) * deep, :] = grad_in[
                        pl.ds(pl.multiple_of(head * deep, deep), deep),
                        part * width : (part + 1) * width,
                    ].astype(bfloat)
                block = grad_out[:, pl.ds(pl.multiple_of(head * wide, wide), wide)]
                out[hidden // width * deep :, :] = block.T.astype(bfloat)


def whole_call(kernel, out_shape, scratch=(), micros=1, in_specs=None, out_specs=None, aliases=None):
    specs = {}
    if in_specs is not None:
        specs["in_specs"] = in_specs
    if out_specs is not None:
        specs["out_specs"] = out_specs
    return pl.pallas_call(
        kernel,
        out_shape=out_shape,
        scratch_shapes=scratch,
        input_output_aliases=aliases or {},
        compiler_params=pltpu.CompilerParams(vmem_limit_bytes=VMEM_LIMIT),
        cost_estimate=pl.CostEstimate(
            flops=micros * 1153000000, bytes_accessed=0, transcendentals=0
        ),
        **specs,
    )


class Grid:
    names = ("zh", "zl", "y", "x", "c")

    def __init__(self, mesh):
        experts, heads = mesh.shape["expert"], mesh.shape["head"]
        self.shape = (2, experts // 4, 2, heads // 2, 2)
        self.experts, self.heads = experts, heads
        self.total = experts * heads

    def size(self, name):
        return self.shape[self.names.index(name)]

    def coords(self, linear):
        out = []
        for extent in reversed(self.shape):
            out.append(linear % extent)
            linear = linear // extent
        return dict(zip(self.names, reversed(out)))

    def linear(self, coords):
        at = 0
        for name, extent in zip(self.names, self.shape):
            at = at * extent + coords[name] % extent
        return at

    def me(self, name):
        linear = lax.axis_index("expert") * self.heads + lax.axis_index("head")
        return self.coords(linear)[name]

    def send(self, value, target):
        pairs = [(i, self.linear(target(self.coords(i)))) for i in range(self.total)]
        return lax.ppermute(value, ("expert", "head"), pairs)

    def move(self, value, **by):
        return self.send(value, lambda at: {name: at[name] - by.get(name, 0) for name in at})

    def shift(self, value, name, by):
        return self.move(value, **{name: by})

    def gather(self, value, name):
        extent, own = self.size(name), self.me(name)
        parts = [value] + [self.shift(value, name, by) for by in range(1, extent)]
        if extent == 2:
            return jnp.where(own == 0, jnp.stack(parts), jnp.stack(parts[::-1]))
        return jnp.roll(jnp.stack(parts), own, axis=0)

    def scatter_sum(self, value, name):
        extent, own = self.size(name), self.me(name)
        if extent == 2:
            kept = jnp.where(own == 0, value[0], value[1])
            others = [self.shift(jnp.where(own == 0, value[1], value[0]), name, 1)]
        else:
            value = jnp.roll(value, -own, axis=0)
            kept = value[0]
            others = [self.shift(value[by], name, -by) for by in range(1, extent)]
        total = kept.astype(single)
        for other in others:
            total = total + other.astype(single)
        return total.astype(value.dtype)


def after(value, *others):
    return lax.optimization_barrier((value, *others))[0]


def per_device(
    grid,
    tokens,
    segment_ids,
    task_ids,
    task_table,
    weight_qkv,
    weight_out,
    gain_one,
    gain_two,
    weight_router,
    weight_in,
    weight_hidden,
    cotangent,
):
    expert_count, head_count = grid.experts, grid.heads
    head_index = lax.axis_index("head")
    row_count, model_width = tokens.shape
    cap = 4 * row_count // expert_count
    deep, wide = weight_qkv.shape[1:]
    padded = -(-expert_count // 16) * 16

    pieces = jnp.concatenate([weight_qkv, weight_out.T[None]]).astype(bfloat)
    small = jnp.concatenate(
        [gain_one[None], gain_two[None], weight_router.T]
    ).astype(bfloat).reshape(-1)
    small_rows = -(-small.shape[0] // wide)
    small = jnp.pad(small, (0, small_rows * wide - small.shape[0])).reshape(small_rows, wide)
    packed = jnp.concatenate([pieces.reshape(4 * deep, wide), small])
    packed = grid.gather(grid.gather(packed, "zh"), "zl")
    barely = packed
    packed = grid.gather(packed, "y")
    partly = packed
    smalls = packed.transpose(2, 1, 0, 3, 4).reshape(expert_count, -1)[:, 4 * deep * wide :]
    smalls = smalls[:, : (2 + expert_count) * deep].reshape(expert_count, 2 + expert_count, deep)
    smalls = smalls.transpose(1, 0, 2).reshape(2 + expert_count, model_width)
    gain1, gain2 = smalls[0:1].astype(single), smalls[1:2].astype(single)
    router = jnp.pad(smalls[2:], ((0, padded - expert_count), (0, 0)))
    packed = grid.gather(packed[..., : 4 * deep, :], "x")
    packed = packed.transpose(0, 3, 2, 1, 4, 5).reshape(-1, expert_count, 4, deep, wide)
    packed = packed.transpose(2, 1, 3, 0, 4).reshape(4, model_width, -1)
    if wide % LANES:
        packed = grid.gather(packed, "c").reshape(2, 4, model_width, -1, wide)
        packed = packed.transpose(1, 2, 3, 0, 4).reshape(4, model_width, model_width)
        weights = (packed, packed)
    else:
        weights = (packed, grid.shift(packed, "c", 1))

    own_segments = lax.dynamic_slice_in_dim(segment_ids, head_index * row_count, row_count)
    shape = jax.ShapeDtypeStruct
    vmem, hbm = pl.BlockSpec(memory_space=pltpu.VMEM), pl.BlockSpec(memory_space=pl.ANY)
    smem = pl.BlockSpec(memory_space=pltpu.SMEM)
    table = jnp.pad(task_table.T, ((0, 16 - task_table.shape[1]), (0, 0))).astype(bfloat)
    hidden = weight_in.shape[2]
    deep_in = weight_in.shape[1]
    piece = shape((hidden // model_width * deep_in + weight_hidden.shape[1], model_width), bfloat)
    first, second, slots, other, kept, own_piece = whole_call(
        lambda *refs: routing_kernel(cap, *refs),
        [shape((1, row_count), jnp.int32)] * 2
        + [shape((padded, row_count), single)] * 2
        + [shape((padded, LANES), jnp.int32), piece],
        micros=3,
    )(own_segments[None], task_ids[None], table, weight_in, weight_hidden)
    kept = kept[:, 0]
    segc = own_segments[:, None]
    starts = [min(max(at - SPAN, 0), row_count - WINDOW) for at in range(0, row_count, BLOCK)]
    segw = jnp.stack([own_segments[at : at + WINDOW] for at in starts])

    names = {name: grid.me(name) for name in grid.names}
    extent = grid.size("zl")
    offsets = [(dl, dy) for dl in range(extent) for dy in range(2)]
    offsets.sort(key=lambda by: by[0] * by[1] != 0)
    providers = len(offsets)

    def expert_of(zl, y, local):
        return ((names["zh"] + local) % 2 * extent + zl % extent) * 2 + y % 2

    def meta_of(experts):
        experts = jnp.stack(experts).astype(jnp.int32)
        return jnp.concatenate([experts, kept[experts], names["c"][None]])

    targets = meta_of(
        [expert_of(names["zl"] - dl, names["y"] - dy, k) for dl, dy in offsets for k in range(2)]
    )
    row_parcel = shape((2 * cap, model_width), bfloat)
    parcel = shape((2 * cap + EXTRA, model_width), bfloat)
    cot_parcels = whole_call(
        lambda *refs: cotangent_kernel(cap, *refs),
        [parcel] * providers,
        in_specs=[smem] + [vmem] * 3 + [hbm],
        micros=10,
    )(targets, cotangent, slots, other, partly)
    proj, attn, res, two_low, stat, gate, *row_parcels = whole_call(
        lambda *refs: forward_kernel(cap, head_count, *refs),
        [
            shape((3, row_count, model_width), bfloat),
            shape((row_count, model_width), bfloat),
            shape((row_count, model_width), single),
            shape((row_count, model_width), bfloat),
            shape((row_count, LANES), single),
            shape((padded, row_count), single),
        ]
        + [row_parcel] * providers,
        in_specs=[smem, vmem, hbm, hbm] + [vmem] * 8,
        scratch=[
            pltpu.VMEM((4, model_width, model_width), bfloat),
            pltpu.SemaphoreType.DMA((2, head_count // 2)),
        ],
        micros=28,
    )(targets, tokens, *weights, gain1, gain2, router, segc, segw, first, second, slots)

    pieces = {(0, 0, 0): after(own_piece, cot_parcels[0])}
    pieces[1, 0, 0] = after(grid.shift(after(own_piece, barely), "zh", 1), two_low)
    for by_x in range(1, head_count // 2):
        for local in range(2):
            pieces[local, by_x, 0] = grid.shift(pieces[local, 0, 0], "x", by_x)
    sources = []
    for (dl, dy), *both in zip(offsets, row_parcels, cot_parcels):
        if dl or dy:
            both = [grid.move(value, zl=dl, y=dy) for value in both]
            both[1] = after(both[1], two_low)
        numbers = both[1][2 * cap + 2 : 2 * cap + 6, 0].astype(jnp.int32)
        sources.append((*both, numbers[0::2] + numbers[1::2]))
    for by_x in range(1, head_count // 2):
        pieces[1, by_x, 0] = after(pieces[1, by_x, 0], sources[-1][0])
    for by_x in range(head_count // 2):
        for local in range(2):
            pieces[local, by_x, 1] = grid.shift(pieces[local, by_x, 0], "c", 1)
    piece_keys = [(k, bx, bc) for k in range(2) for bx in range(head_count // 2) for bc in range(2)]
    piece_list = [pieces[key] for key in piece_keys]

    order = [0] + list(range(providers - 1, 0, -1))
    groups = [order[at : at + 2] for at in range(0, providers, 2)]
    save_tiles = sum(-(-len(group) * cap // TILE) for group in groups)
    save_shapes = [
        shape((2, save_tiles * TILE, cols), bfloat)
        for cols in (model_width, model_width, hidden, hidden)
    ]
    own_experts = jnp.stack([expert_of(names["zl"], names["y"], local) for local in range(2)])
    wide_router = jnp.pad(router, ((0, LANES - padded), (0, 0)))
    saved = []
    tiles_before = jnp.zeros((2,), jnp.int32)
    results = {}
    for group in groups:
        count = len(group)
        numbers = jnp.stack([sources[s][2] for s in group], axis=1)
        meta = jnp.concatenate(
            [names["x"][None], names["c"][None], own_experts, tiles_before, numbers.reshape(-1)]
        ).astype(jnp.int32)
        half_tiles = jnp.sum((numbers + HALF - 1) // HALF, axis=1)
        tiles_before = tiles_before + (half_tiles + 1) // 2
        inputs = [meta, wide_router] + [sources[s][part] for part in range(2) for s in group]
        inputs += piece_list + saved
        before = 2 + 2 * count + len(piece_list)
        outs = whole_call(
            lambda *refs, count=count, new=not saved: expert_kernel(count, head_count, new, *refs),
            save_shapes + [parcel] * (2 * count),
            in_specs=[smem, vmem] + [hbm] * (2 * count + len(piece_list) + len(saved)),
            out_specs=[hbm] * (4 + 2 * count),
            aliases={before + i: i for i in range(len(saved))},
            scratch=[
                pltpu.VMEM((2, model_width, hidden), bfloat),
                pltpu.VMEM((2, hidden, model_width), bfloat),
                pltpu.VMEM((count, *row_parcel.shape), bfloat),
                pltpu.VMEM((count, *parcel.shape), bfloat),
                pltpu.VMEM((count, *parcel.shape), bfloat),
                pltpu.VMEM((count, *parcel.shape), bfloat),
                pltpu.VMEM((count, 8, cap), single),
                pltpu.VMEM((TILE, model_width + LANES), single),
                pltpu.VMEM((2, TILE, model_width), bfloat),
                pltpu.VMEM((2, TILE, model_width), bfloat),
                pltpu.VMEM((2, TILE, hidden), bfloat),
                pltpu.VMEM((2, TILE, hidden), bfloat),
                pltpu.SMEM((2, count * cap // HALF + 1), jnp.int32),
                pltpu.SemaphoreType.DMA((2, head_count * (hidden // model_width + 1))),
                pltpu.SemaphoreType.DMA((2, count)),
                pltpu.SemaphoreType.DMA((2, 4)),
                pltpu.SemaphoreType.DMA((2, count)),
            ],
            micros=25,
        )(*inputs)
        saved = list(outs[:4])
        for i, s in enumerate(group):
            results[s] = [outs[4 + i], outs[4 + count + i]]
    out_parcels, grad_parcels = [], []
    for s, (dl, dy) in enumerate(offsets):
        out_part, grad_part = results[s]
        if dl or dy:
            grad_part, out_part = (grid.move(v, zl=-dl, y=-dy) for v in (grad_part, out_part))
        out_parcels.append(out_part)
        grad_parcels.append(grad_part)
    weight_meta = jnp.concatenate([names["x"][None], names["c"][None], tiles_before])
    done = whole_call(
        lambda *refs: weight_kernel(head_count, *refs),
        [piece] * len(piece_keys),
        in_specs=[smem] + [hbm] * 4,
        scratch=[
            pltpu.VMEM((model_width, hidden), single),
            pltpu.VMEM((model_width, hidden), single),
            pltpu.VMEM((2, TILE, model_width), bfloat),
            pltpu.VMEM((2, TILE, model_width), bfloat),
            pltpu.VMEM((2, TILE, hidden), bfloat),
            pltpu.VMEM((2, TILE, hidden), bfloat),
            pltpu.SemaphoreType.DMA((2, 4)),
        ],
        micros=24,
    )(weight_meta.astype(jnp.int32), *saved)
    done = lax.optimization_barrier((*done, *grad_parcels[1:]))
    grad_parcels = grad_parcels[:1] + list(done[len(piece_keys) :])
    grads = dict(zip(piece_keys, done))

    def add(kept, other):
        return (kept.astype(single) + other.astype(single)).astype(bfloat)

    waited = [grads[0, 0, 0]]
    for local in (1, 0):
        for by_x in range(head_count // 2):
            grads[local, by_x, 0] = add(
                grads[local, by_x, 0], grid.shift(grads[local, by_x, 1], "c", -1)
            )
    waited += [grads[1, by_x, 0] for by_x in (0, 1)]
    for local in (1, 0):
        for by_x in range(1, head_count // 2):
            grads[local, 0, 0] = add(
                grads[local, 0, 0], grid.shift(grads[local, by_x, 0], "x", -by_x)
            )
    grad_piece = grads[0, 0, 0].astype(single) + grid.shift(grads[1, 0, 0], "zh", -1).astype(single)
    grad_in_own = grad_piece[: hidden // model_width * deep_in]
    grad_in_own = grad_in_own.reshape(-1, deep_in, model_width).transpose(1, 0, 2)
    grad_in_own = grad_in_own.reshape(1, deep_in, hidden)
    grad_hidden_own = grad_piece[hidden // model_width * deep_in :][None]
    output = whole_call(
        lambda *refs: output_kernel(providers, cap, *refs),
        shape((row_count, model_width), bfloat),
        in_specs=[smem] + [vmem] * (2 + providers),
        micros=8,
    )(targets, res, slots, *out_parcels)

    grad_tokens, grad_w, grad_gain1, grad_gain2, grad_router = whole_call(
        lambda *refs: backward_kernel(providers, cap, head_count, len(waited), *refs),
        (
            shape((row_count, model_width), single),
            shape((4, model_width, model_width), bfloat),
            shape((1, model_width), single),
            shape((1, model_width), single),
            shape((padded, model_width), single),
        ),
        in_specs=[smem] + [vmem] * 7 + [hbm] * 2 + [vmem] * (7 + providers) + [hbm] * len(waited),
        scratch=[
            pltpu.VMEM((padded, row_count), single),
            pltpu.VMEM((row_count, model_width), single),
            pltpu.VMEM((row_count, model_width), bfloat),
            pltpu.VMEM((row_count, model_width), bfloat),
            pltpu.VMEM((3, row_count, model_width), bfloat),
            pltpu.VMEM((row_count, model_width), single),
            pltpu.VMEM((row_count, model_width), single),
            pltpu.VMEM((row_count, model_width), bfloat),
            pltpu.VMEM((4, model_width, model_width), bfloat),
            pltpu.SemaphoreType.DMA((2, head_count // 2)),
        ],
        micros=34,
    )(
        targets,
        tokens, cotangent, res, two_low, proj, attn, stat, *weights, gain1, gain2, router,
        segc, segw, gate, slots, *grad_parcels, *waited,
    )

    pieces = (
        grad_w.reshape(4, expert_count, deep, head_count, wide)
        .transpose(1, 3, 0, 2, 4)
        .reshape(expert_count, head_count, 4 * deep, wide)
    )
    smalls = jnp.concatenate([grad_gain1, grad_gain2, grad_router[:expert_count]]).astype(bfloat)
    smalls = smalls.reshape(2 + expert_count, expert_count, deep).transpose(1, 0, 2)
    smalls = smalls.reshape(expert_count, -1)
    smalls = jnp.pad(smalls, ((0, 0), (0, small_rows * wide - smalls.shape[1])))
    smalls = jnp.broadcast_to(
        smalls.reshape(expert_count, 1, small_rows, wide),
        (expert_count, head_count, small_rows, wide),
    )
    packed = jnp.concatenate([pieces, smalls], axis=2)
    packed = packed.reshape(*grid.shape, 4 * deep + small_rows, wide).transpose(4, 3, 2, 1, 0, 5, 6)
    packed = after(packed, grads[0, 0, 0], *out_parcels[1:3])
    for name in ("c", "x", "y", "zl", "zh"):
        if name == "y":
            packed = after(packed, grad_piece)
        packed = grid.scatter_sum(packed, name)
    pieces = packed[: 4 * deep].reshape(4, deep, wide).astype(single)
    smalls = packed[4 * deep :].reshape(-1)[: (2 + expert_count) * deep].astype(single)
    smalls = smalls.reshape(2 + expert_count, deep)
    return (
        output,
        grad_tokens,
        pieces[:3],
        pieces[3].T,
        smalls[0],
        smalls[1],
        smalls[2:].T,
        grad_in_own,
        grad_hidden_own,
    )


def solution(mesh):
    grid = Grid(mesh)
    placed = (
        P(("expert", "head"), None),
        P("expert"),
        P(),
        P(),
        P(None, "expert", "head"),
        P("head", "expert"),
        P("expert"),
        P("expert"),
        P("expert", None),
        P("expert", "head", None),
        P("expert", "head", None),
        P(("expert", "head"), None),
    )

    def step(*arrays):
        return per_device(grid, *arrays)

    return jax.shard_map(
        step,
        mesh=mesh,
        in_specs=placed,
        out_specs=(
            P(("expert", "head"), None),
            P(("expert", "head"), None),
            P(None, "expert", "head"),
            P("head", "expert"),
            P("expert"),
            P("expert"),
            P("expert", None),
            P("expert", "head", None),
            P("expert", "head", None),
        ),
        check_vma=False,
    )
```

```python
import jax
import jax.numpy as jnp
from jax import lax
from jax.experimental import pallas as pl
from jax.experimental.pallas import tpu as pltpu
from jax.sharding import PartitionSpec as P

HDIM = 64
PACK = 1024
SPAN = 64
BLOCK = 128
WINDOW = BLOCK + 2 * SPAN
CHUNK = 256
LANES = 128
TILE = 256
HALF = 128
EXTRA = 16
ABSENT = -1e6
SCALE = 1153e6 / 8

EPSILON = 1e-05
NEGATIVE = -1e30

bfloat = jnp.bfloat16
single = jnp.float32
VMEM_LIMIT = 56 * 1024 * 1024


def dot_nn(a, b):
    return lax.dot_general(a, b, (((1,), (0,)), ((), ())), preferred_element_type=single)


def dot_nt(a, b):
    return lax.dot_general(a, b, (((1,), (1,)), ((), ())), preferred_element_type=single)


def dot_tn(a, b):
    return lax.dot_general(a, b, (((0,), (0,)), ((), ())), preferred_element_type=single)


def normalise(values):
    centered = values - jnp.mean(values, axis=-1, keepdims=True)
    inverse = lax.rsqrt(jnp.mean(centered * centered, axis=-1, keepdims=True) + EPSILON)
    return centered * inverse, inverse


def norm_pull(grad_normed, scaled, inverse, gain):
    weighted = grad_normed * gain
    return inverse * (
        weighted
        - jnp.mean(weighted, axis=-1, keepdims=True)
        - scaled * jnp.mean(weighted * scaled, axis=-1, keepdims=True)
    )


def split_heads(pair, first_half):
    zero = jnp.zeros_like(pair)
    return jnp.concatenate(
        [jnp.where(first_half, pair, zero), jnp.where(first_half, zero, pair)], axis=0
    )


def window_start(block, rows):
    return pl.multiple_of(jnp.clip(block * BLOCK - SPAN, 0, rows - WINDOW), SPAN)


def fetch_weights(core, own, other, weights, sem):
    copies = []
    if own.shape == weights.shape:
        copies = [pltpu.make_async_copy(own, weights, sem.at[0, 0])]
    else:
        parts_x, parts_y, parts_zl, parts_zh, _, deep, wide = own.shape
        places = [
            (x, y, zl, zh)
            for x in range(parts_x)
            for y in range(parts_y)
            for zl in range(parts_zl)
            for zh in range(parts_zh)
        ]
        for at, (x, y, zl, zh) in enumerate(places):
            row = ((zh * parts_zl + zl) * parts_y + y) * deep
            for i, (ref, half) in enumerate(((own, core), (other, 1 - core))):
                start = pl.multiple_of((2 * x + half) * wide, LANES)
                copies.append(
                    pltpu.make_async_copy(
                        ref.at[x, y, zl, zh],
                        weights.at[:, pl.ds(row, deep), pl.ds(start, wide)],
                        sem.at[i, at],
                    )
                )
    for copy in copies:
        copy.start()
    for copy in copies:
        copy.wait()


def forward_kernel(
    meta, tok, weights_own, weights_other, gain1, gain2, router, segc, segw, first, second,
    proj, attn, res, two, stat, gate, weights_out, weights, sem,
):
    rows, width = tok.shape
    fetch_weights(meta[0], weights_own, weights_other, weights, sem)
    wqkv, wot = weights, weights.at[3]

    def project(step, carry):
        at = pl.ds(pl.multiple_of(step * CHUNK, CHUNK), CHUNK)
        scaled, _ = normalise(tok[at, :].astype(single))
        low = (scaled * gain1[...]).astype(bfloat)
        for part in range(3):
            proj[part, at, :] = dot_nn(low, wqkv[part]).astype(bfloat)
        return carry

    lax.fori_loop(0, rows // CHUNK, project, 0)
    lane = lax.broadcasted_iota(jnp.int32, (BLOCK, LANES), 1)
    first_half = lane < HDIM
    expert = lax.broadcasted_iota(jnp.int32, (router.shape[0], BLOCK), 0)

    def attend(block, carry):
        q_at = pl.ds(pl.multiple_of(block * BLOCK, BLOCK), BLOCK)
        k_at = pl.ds(window_start(block, rows), WINDOW)
        same = (segc[q_at, :] == segw[pl.ds(block, 1), :])[None]
        totals = jnp.zeros((BLOCK, LANES), single)
        for pair in range(width // LANES):
            cols = slice(pair * LANES, (pair + 1) * LANES)
            queries = split_heads(proj[0, q_at, cols] * HDIM**-0.5, first_half)
            scores = dot_nt(queries, proj[1, k_at, cols]).reshape(2, BLOCK, WINDOW)
            scores = jnp.where(same, scores, NEGATIVE)
            peak = jnp.max(scores, axis=-1, keepdims=True)
            exponent = jnp.exp(scores - peak)
            total = jnp.sum(exponent, axis=-1, keepdims=True)
            probs = (exponent * (1.0 / total)).astype(bfloat).reshape(2 * BLOCK, WINDOW)
            out = dot_nn(probs, proj[2, k_at, cols])
            attn[q_at, cols] = jnp.where(first_half, out[:BLOCK], out[BLOCK:]).astype(bfloat)
            log_total = peak + jnp.log(total)
            for half in range(2):
                totals = jnp.where(lane == 2 * pair + half, log_total[half], totals)
        stat[q_at, :] = totals
        residual = tok[q_at, :].astype(single) + dot_nt(attn[q_at, :], wot[...])
        res[q_at, :] = residual
        scaled, _ = normalise(residual)
        low = (scaled * gain2[...]).astype(bfloat)
        two[q_at, :] = low
        logits = dot_nt(router[...], low)
        mark0 = first[:, q_at] == expert
        mark1 = second[:, q_at] == expert
        logit0 = jnp.sum(jnp.where(mark0, logits, 0.0), axis=0, keepdims=True)
        logit1 = jnp.sum(jnp.where(mark1, logits, 0.0), axis=0, keepdims=True)
        top = jnp.maximum(logit0, logit1)
        part0, part1 = jnp.exp(logit0 - top), jnp.exp(logit1 - top)
        scale = 1.0 / (part0 + part1)
        gate[:, q_at] = jnp.where(mark0, part0 * scale, jnp.where(mark1, part1 * scale, 0.0))
        return carry

    lax.fori_loop(0, rows // BLOCK, attend, 0)
    count = gate.shape[0]
    at = rows
    for part in split_two(gate[...]):
        for start in range(0, rows, width):
            two[at : at + count, :] = part[:, start : start + width]
            at += count
    weights_out[...] = weights[...]


def split_two(values):
    high = values.astype(bfloat)
    return high, (values - high.astype(single)).astype(bfloat)


def pack_rows(rows):
    at = lax.broadcasted_iota(jnp.int32, (EXTRA, rows.shape[1]), 0)
    out = jnp.zeros((EXTRA, rows.shape[1]), single)
    for local in range(2):
        high = rows[local : local + 1, :].astype(bfloat).astype(single)
        out = jnp.where(at == 2 * local, high, out)
        out = jnp.where(at == 2 * local + 1, rows[local : local + 1, :] - high, out)
    return out.astype(bfloat)


def unpack_row(packed, local):
    packed = packed.astype(single)
    return packed[2 * local : 2 * local + 1, :] + packed[2 * local + 1 : 2 * local + 2, :]


def routing_kernel(
    cap, segments, tasks, table, weight_in, weight_hidden, cot,
    first, second, route, piece, sent,
):
    rows = segments.shape[1]
    deep, hidden = weight_in.shape[1:]
    width = piece.shape[1]
    for part in range(hidden // width):
        piece[part * deep : (part + 1) * deep, :] = weight_in[
            0, :, part * width : (part + 1) * width
        ].astype(bfloat)
    piece[hidden // width * deep :, :] = weight_hidden[0].astype(bfloat)
    names = lax.broadcasted_iota(jnp.int32, (table.shape[1], tasks.shape[1]), 0)
    experts = dot_nn(table[...], jnp.where(names == tasks[...], 1.0, 0.0).astype(bfloat))
    experts = experts.astype(bfloat)
    chosen = jnp.zeros((table.shape[0], rows), single)
    for start in range(0, tasks.shape[1], 1024):
        size = min(1024, tasks.shape[1] - start)
        at = lax.broadcasted_iota(jnp.int32, (size, rows), 0) + start
        ones = jnp.where(at == segments[...], 1.0, 0.0).astype(bfloat)
        chosen = chosen + dot_nn(experts[:, start : start + size], ones)
    zero, one = chosen[0:1, :], chosen[1:2, :]
    first[...] = zero.astype(jnp.int32)
    second[...] = one.astype(jnp.int32)
    which = lax.broadcasted_iota(jnp.int32, route.shape, 0).astype(single)
    is_first, is_second = which == zero, which == one
    marks = jnp.where(is_first | is_second, 1.0, 0.0)
    earlier = lax.broadcasted_iota(jnp.int32, (rows, rows), 0) < lax.broadcasted_iota(
        jnp.int32, (rows, rows), 1
    )
    places = dot_nn(marks.astype(bfloat), jnp.where(earlier, 1.0, 0.0).astype(bfloat))
    inside = (marks > 0.5) & (places < cap)
    slots = jnp.where(inside, places, ABSENT)
    route[...] = slots
    total = jnp.sum(jnp.where(inside, 1.0, 0.0), axis=1, keepdims=True)
    total = jnp.broadcast_to(total, (route.shape[0], width))
    sent[:rows, :] = cot[...]
    at = rows
    for part in range(2):
        for start in range(0, rows, width):
            sent[at : at + route.shape[0], :] = sixteens(slots[:, start : start + width])[part]
            at += route.shape[0]
    for part in range(2):
        sent[at : at + route.shape[0], :] = sixteens(total)[part]
        at += route.shape[0]


def sixteens(values):
    high = jnp.floor(values * 0.0625) * 16.0
    high = jnp.where(values < 0.0, values, high)
    return high.astype(bfloat), jnp.where(values < 0.0, 0.0, values - high).astype(bfloat)


def output_kernel(providers, cap, meta, res, gate, slots, *refs):
    parcels, out = refs[:providers], refs[providers]
    for step in range(res.shape[0] // CHUNK):
        at = slice(step * CHUNK, (step + 1) * CHUNK)
        out[at, :] = (res[at, :] + returned_rows(parcels, cap, meta, gate, slots, at)).astype(bfloat)


def returned_rows(parcels, cap, meta, gate, slots, at):
    total = 0.0
    for provider, parcel in enumerate(parcels):
        for local in range(2):
            chosen = pl.ds(meta[2 * provider + local], 1)
            ones = onehot(slots[chosen, at], 0, cap, gate[chosen, at])
            total = total + dot_tn(ones, parcel[local * cap : (local + 1) * cap, :])
    return total


def middle_kernel(
    providers, cap, waited, meta,
    cot, res, two, attn, weights, gain2, router, gate, slots,
    *refs,
):
    parcels = refs[:providers]
    (
        grad_res, grad_heads, grad_out, grad_gain2, grad_router,
        products, grad_attn,
    ) = refs[providers + waited :]
    rows, width = cot.shape
    wot = weights.at[3]
    products[...] = jnp.zeros_like(products)
    for provider in range(providers):
        for local in range(2):
            chosen = meta[2 * provider + local]
            ones = onehot(slots[pl.ds(chosen, 1), :], 0, cap)
            moved = dot_nn(parcels[provider][2 * cap :, :cap], ones)
            products[pl.ds(chosen, 1), :] = unpack_row(moved, local)
    gates = gate[...]
    inner_products = products[...]
    grad_logits = gates * (
        inner_products - jnp.sum(gates * inner_products, axis=0, keepdims=True)
    )
    grad_logits = jnp.concatenate(split_two(grad_logits), axis=0)
    router_twice = jnp.concatenate([router[...], router[...]], axis=0)
    count = router.shape[0]
    routed = dot_nn(grad_logits, two[:rows, :])
    grad_router[...] = routed[:count] + routed[count:]
    grad_gain2[...] = jnp.zeros_like(grad_gain2)
    for step in range(rows // CHUNK):
        at = slice(step * CHUNK, (step + 1) * CHUNK)
        scaled, inverse = normalise(res[at, :])
        grad_normed = dot_tn(grad_logits[:, at], router_twice)
        grad_normed = grad_normed + returned_rows(parcels, cap, meta, gate, slots, at)
        grad_gain2[...] += jnp.sum(grad_normed * scaled, axis=0, keepdims=True)
        grad_row = cot[at, :].astype(single) + norm_pull(grad_normed, scaled, inverse, gain2[...])
        grad_res[at, :] = grad_row
        low = grad_row.astype(bfloat)
        grad_attn[at, :] = low
        grad_heads[at, :] = dot_nn(low, wot[...]).astype(bfloat)
    grad_out[...] = dot_tn(grad_attn[...], attn[...]).astype(bfloat)


def backward_kernel(
    heads, core, tok, proj, stat, wqkv, gain1, segc, segw,
    grad_res, grad_heads, grad_out,
    grad_tok, grad_own, other_top, other_rest, grad_gain1,
    grad_proj, grad_key, grad_value, normed, grad_w,
):
    rows, width = tok.shape
    grad_gain1[...] = jnp.zeros_like(grad_gain1)
    grad_key[...] = jnp.zeros_like(grad_key)
    grad_value[...] = jnp.zeros_like(grad_value)
    lane = lax.broadcasted_iota(jnp.int32, (BLOCK, LANES), 1)
    first_half = lane < HDIM

    def attend(block, carry):
        q_at = pl.ds(pl.multiple_of(block * BLOCK, BLOCK), BLOCK)
        k_at = pl.ds(window_start(block, rows), WINDOW)
        same = (segc[q_at, :] == segw[pl.ds(block, 1), :])[None]
        totals = stat[q_at, :]
        for pair in range(width // LANES):
            cols = slice(pair * LANES, (pair + 1) * LANES)
            queries = split_heads(proj[0, q_at, cols] * HDIM**-0.5, first_half)
            keys_block = proj[1, k_at, cols]
            scores = dot_nt(queries, keys_block).reshape(2, BLOCK, WINDOW)
            scores = jnp.where(same, scores, NEGATIVE)
            log_total = jnp.stack(
                [totals[:, 2 * pair : 2 * pair + 1], totals[:, 2 * pair + 1 : 2 * pair + 2]]
            )
            probs = jnp.exp(scores - log_total).reshape(2 * BLOCK, WINDOW)
            heads_low = split_heads(grad_heads[q_at, cols], first_half)
            grad_probs = dot_nt(heads_low, proj[2, k_at, cols])
            delta = jnp.sum(probs * grad_probs, axis=-1, keepdims=True)
            grad_scores = (probs * (grad_probs - delta)).astype(bfloat)
            grad_query = dot_nn(grad_scores, keys_block) * HDIM**-0.5
            grad_proj[0, q_at, cols] = jnp.where(
                first_half, grad_query[:BLOCK], grad_query[BLOCK:]
            ).astype(bfloat)
            grad_key[k_at, cols] += dot_tn(grad_scores, queries)
            grad_value[k_at, cols] += dot_tn(probs.astype(bfloat), heads_low)
        return carry

    lax.fori_loop(0, rows // BLOCK, attend, 0)
    for step in range(rows // CHUNK):
        at = slice(step * CHUNK, (step + 1) * CHUNK)
        grad_proj[1, at, :] = grad_key[at, :].astype(bfloat)
        grad_proj[2, at, :] = grad_value[at, :].astype(bfloat)
        grad_normed = dot_nt(grad_proj[0, at, :], wqkv[0])
        for part in (1, 2):
            grad_normed += dot_nt(grad_proj[part, at, :], wqkv[part])
        scaled, inverse = normalise(tok[at, :].astype(single))
        normed[at, :] = (scaled * gain1[...]).astype(bfloat)
        grad_gain1[...] += jnp.sum(grad_normed * scaled, axis=0, keepdims=True)
        grad_tok[at, :] = grad_res[at, :] + norm_pull(grad_normed, scaled, inverse, gain1[...])
    for part in range(3):
        grad_w[part] = dot_tn(normed[...], grad_proj[part]).astype(bfloat)
    grad_w[3] = grad_out[...]
    if grad_own.shape == grad_w.shape:
        grad_own[...] = grad_w[...]
        other_top[...] = grad_w[:2]
        other_rest[...] = grad_w[2:]
    else:
        wide = width // heads
        for by in range(heads // 2):
            cols = slice(by * wide, (by + 1) * wide)
            start = pl.multiple_of((2 * by + core[0]) * wide, LANES)
            grad_own[:, :, cols] = grad_w[:, :, pl.ds(start, wide)]
            start = pl.multiple_of((2 * by + 1 - core[0]) * wide, LANES)
            other_top[:, :, cols] = grad_w[:2, :, pl.ds(start, wide)]
            other_rest[:, :, cols] = grad_w[2:, :, pl.ds(start, wide)]


def onehot(slots, base, rows, marks=1.0):
    places = lax.broadcasted_iota(jnp.int32, (rows, slots.shape[1]), 0).astype(single)
    return jnp.where(places == slots - base, marks, 0.0).astype(bfloat)


def gelu_both(values):
    square = values * values
    rate = 0.7978845608028654 + 0.035677408136300125 * square
    slope = 0.7978845608028654 + 0.10703222440890037 * square
    bent = jnp.tanh(values * rate)
    half = 0.5 + 0.5 * bent
    return values * half, half + values * (0.5 - 0.5 * (bent * bent)) * slope


def expert_kernel(sources, heads, cap, tokens, count, first, meta, before, *refs):
    refs = list(refs)

    def take(count):
        taken = refs[:count]
        del refs[:count]
        return taken

    rows_in, grads_in = take(sources), take(sources)
    pieces = take(2 * heads)
    if not first:
        take(4)
    saved = take(4)
    outs, grads = take(sources), take(sources)
    (now,) = take(1)
    (
        win, wout, row_all, grad_all, row_buf, grad_buf, gate_buf,
        out_buf, copy_buf, product_buf, now_x, now_g, now_gate,
        st_x, st_g, st_act, st_pre, table, w_sem, in_sem, s_sem, out_sem,
    ) = refs
    width = row_buf.shape[2]
    hidden = wout.shape[1]
    deep, wide = width // heads, hidden // heads
    head_x, head_c = meta[0], meta[1]
    staged = (st_x, st_g, st_act, st_pre)

    def weight_copies(local):
        at = 0
        for by_x in range(heads // 2):
            for by_c in range(2):
                head = lax.rem(head_x + by_x, heads // 2) * 2 + lax.rem(head_c + by_c, 2)
                piece = pieces[(local * (heads // 2) + by_x) * 2 + by_c]
                for part in range(hidden // width):
                    yield pltpu.make_async_copy(
                        piece.at[pl.ds(part * deep, deep), :],
                        win.at[
                            local,
                            pl.ds(pl.multiple_of(head * deep, deep), deep),
                            pl.ds(part * width, width),
                        ],
                        w_sem.at[local, at],
                    )
                    at += 1
                yield pltpu.make_async_copy(
                    piece.at[pl.ds(hidden // width * deep, wide), :],
                    wout.at[local, pl.ds(pl.multiple_of(head * wide, wide), wide), :],
                    w_sem.at[local, at],
                )
                at += 1

    def source_copies():
        for source in range(sources):
            for i, (given, held) in enumerate(((rows_in, row_all), (grads_in, grad_all))):
                yield pltpu.make_async_copy(given[source], held.at[source], in_sem.at[i, source])

    for copy in weight_copies(0):
        copy.start()
    for copy in source_copies():
        copy.start()
    for copy in weight_copies(1):
        copy.start()
    out_buf[...] = jnp.zeros_like(out_buf)
    copy_buf[...] = jnp.zeros_like(copy_buf)
    product_buf[...] = jnp.zeros_like(product_buf)

    def save_copies(slot, local, tile):
        at = pl.ds(pl.multiple_of(tile * TILE, TILE), TILE)
        return [
            pltpu.make_async_copy(stage.at[slot], save.at[local, at, :], s_sem.at[slot, i])
            for i, (stage, save) in enumerate(zip(staged, saved))
        ]

    eye = lax.broadcasted_iota(jnp.int32, (HALF, HALF), 0) == lax.broadcasted_iota(
        jnp.int32, (HALF, HALF), 1
    )
    for copy in source_copies():
        copy.wait()
    step_rows = min(TILE, cap)
    which = lax.broadcasted_iota(jnp.int32, (count, 1), 0)
    numbers, halves = {}, []
    for local in range(2):
        number = 0
        for source in range(sources):
            at = grad_all.shape[1] - 2 * count
            total = grad_all[source, at : at + count, :LANES].astype(single)
            total = total + grad_all[source, at + count :, :LANES].astype(single)
            total = jnp.max(jnp.where(which == meta[2 + local], total, 0.0)).astype(jnp.int32)
            numbers[source, local] = total
            for half in range(cap // HALF):
                table[local, number] = source * (cap // HALF) + half
                number = number + jnp.where(total > half * HALF, 1, 0)
        halves.append(number)
        now[local] = before[local] + (number + 1) // 2
    places = lax.broadcasted_iota(jnp.int32, (step_rows, tokens), 0).astype(single)
    for source in range(sources):
        for local in range(2):
            expert = meta[2 + local]

            def by_token(ref):
                row = []
                for part in range(tokens // width):
                    parts = [
                        ref[source, pl.ds(tokens + (i * (tokens // width) + part) * count, count), :]
                        for i in range(2)
                    ]
                    both = parts[0].astype(single) + parts[1].astype(single)
                    both = jnp.where(which == expert, both, 0.0)
                    row.append(jnp.sum(both, axis=0, keepdims=True))
                return jnp.concatenate(row, axis=1)

            gate_row, slot_row = by_token(row_all), by_token(grad_all)
            for step in range(cap // step_rows):

                @pl.when(numbers[source, local] > step * step_rows)
                def _():
                    at = slice(local * cap + step * step_rows, local * cap + (step + 1) * step_rows)
                    slots = slot_row - step * step_rows
                    ones = jnp.where(places == slots, 1.0, 0.0).astype(bfloat)
                    row_buf[source, at, :] = dot_nn(ones, row_all[source, :tokens, :]).astype(bfloat)
                    grad_buf[source, at, :] = dot_nn(ones, grad_all[source, :tokens, :]).astype(
                        bfloat
                    )
                    gate_buf[source, at, :] = jnp.sum(
                        jnp.where(places == slots, gate_row, 0.0), axis=1, keepdims=True
                    )

    done = 0
    for local in range(2):
        for copy in weight_copies(local):
            copy.wait()
        number = halves[local]

        def place(tile, half):
            entry = table[local, 2 * tile + half]
            step = lax.rem(entry, cap // HALF)
            start = pl.multiple_of(step * HALF, HALF)
            rows = pl.ds(pl.multiple_of(local * cap + start, HALF), HALF)
            return entry // (cap // HALF), rows, pl.ds(start, HALF)

        def one_tile(tile, done):
            slot = lax.rem(done, 2)

            @pl.when(done >= 2)
            def _():
                for copy in save_copies(slot, local, tile):
                    copy.wait()

            for half in range(2):
                at = pl.ds(half * HALF, HALF)

                @pl.when(2 * tile + half < number)
                def _():
                    source, rows, lanes = place(tile, half)
                    now_x[at, :] = row_buf[source, rows, :]
                    now_g[at, :] = grad_buf[source, rows, :]
                    now_gate[at, :] = gate_buf[source, rows, :]

                @pl.when(2 * tile + half >= number)
                def _():
                    now_x[at, :] = jnp.zeros((HALF, width), bfloat)
                    now_g[at, :] = jnp.zeros((HALF, width), bfloat)
                    now_gate[at, :] = jnp.zeros((HALF, 1), single)

            rows_low, grad_low, gate = now_x[...], now_g[...], now_gate[...]
            st_x[slot] = (rows_low.astype(single) * gate).astype(bfloat)
            st_g[slot] = (grad_low.astype(single) * gate).astype(bfloat)
            for part in range(hidden // width):
                cols = slice(part * width, (part + 1) * width)
                pre = dot_nn(rows_low, win[local, :, cols])
                grad_act = dot_nt(grad_low, wout[local, cols, :])
                act, slope = gelu_both(pre)
                st_act[slot, :, cols] = act.astype(bfloat)
                st_pre[slot, :, cols] = (slope * grad_act).astype(bfloat)
            result = dot_nn(st_act[slot], wout[local]).astype(bfloat).astype(single)
            grad_copy = dot_nt(st_pre[slot], win[local]).astype(bfloat)
            product = jnp.sum(grad_low.astype(single) * result, axis=1, keepdims=True)
            result = result.astype(bfloat)
            for half in range(2):
                at = slice(half * HALF, (half + 1) * HALF)

                @pl.when(2 * tile + half < number)
                def _():
                    source, rows, lanes = place(tile, half)
                    out_buf[source, rows, :] = result[at]
                    copy_buf[source, rows, :] = grad_copy[at]
                    product_buf[source, local : local + 1, lanes] = jnp.sum(
                        jnp.where(eye, product[at], 0.0), axis=0, keepdims=True
                    )

            for copy in save_copies(slot, local, before[local] + tile):
                copy.start()
            return done + 1

        done = lax.fori_loop(0, (number + 1) // 2, one_tile, done)

    def result_copies():
        for source in range(sources):
            yield pltpu.make_async_copy(copy_buf.at[source], grads[source], out_sem.at[0, source])
            yield pltpu.make_async_copy(out_buf.at[source], outs[source], out_sem.at[1, source])

    for source in range(sources):
        copy_buf[source, 2 * cap :, :cap] = pack_rows(product_buf[source])
    for copy in result_copies():
        copy.start()
    for back in (1, 2):

        @pl.when(done >= back)
        def _():
            for copy in save_copies(lax.rem(done - back, 2), 0, 0):
                copy.wait()

    for copy in result_copies():
        copy.wait()


def weight_kernel(heads, waited, meta, tiles_saved, save_x, save_g, save_act, save_pre, *refs):
    outs = refs[waited : waited + 2 * heads]
    grad_in, grad_out, buf_x, buf_g, buf_act, buf_pre, sem = refs[waited + 2 * heads :]
    width, hidden = grad_in.shape
    deep, wide = width // heads, hidden // heads
    buffers = (buf_x, buf_g, buf_act, buf_pre)

    def fetch(slot, local, tile):
        at = pl.ds(pl.multiple_of(tile * TILE, TILE), TILE)
        return [
            pltpu.make_async_copy(save.at[local, at, :], buf.at[slot], sem.at[slot, i])
            for i, (save, buf) in enumerate(zip((save_x, save_g, save_act, save_pre), buffers))
        ]

    for local in (1, 0):
        tiles = tiles_saved[local]
        grad_in[...] = jnp.zeros_like(grad_in)
        grad_out[...] = jnp.zeros_like(grad_out)

        @pl.when(tiles > 0)
        def _():
            for copy in fetch(0, local, 0):
                copy.start()

        def one_tile(tile, carry):
            slot = lax.rem(tile, 2)

            @pl.when(tile + 1 < tiles)
            def _():
                for copy in fetch(1 - slot, local, tile + 1):
                    copy.start()

            for copy in fetch(slot, local, tile):
                copy.wait()
            for part in range(hidden // width):
                cols = slice(part * width, (part + 1) * width)
                grad_in[:, cols] += dot_tn(buf_x[slot], buf_pre[slot, :, cols])
                grad_out[:, cols] += dot_tn(buf_g[slot], buf_act[slot, :, cols])
            return carry

        lax.fori_loop(0, tiles, one_tile, 0)
        for by_x in range(heads // 2):
            for by_c in range(2):
                head = lax.rem(meta[0] + by_x, heads // 2) * 2 + lax.rem(meta[1] + by_c, 2)
                out = outs[(local * (heads // 2) + by_x) * 2 + by_c]
                for part in range(hidden // width):
                    out[part * deep : (part + 1) * deep, :] = grad_in[
                        pl.ds(pl.multiple_of(head * deep, deep), deep),
                        part * width : (part + 1) * width,
                    ].astype(bfloat)
                block = grad_out[:, pl.ds(pl.multiple_of(head * wide, wide), wide)]
                out[hidden // width * deep :, :] = block.T.astype(bfloat)


def whole_call(kernel, out_shape, scratch=(), micros=1, in_specs=None, out_specs=None, aliases=None):
    specs = {}
    if in_specs is not None:
        specs["in_specs"] = in_specs
    if out_specs is not None:
        specs["out_specs"] = out_specs
    return pl.pallas_call(
        kernel,
        out_shape=out_shape,
        scratch_shapes=scratch,
        input_output_aliases=aliases or {},
        compiler_params=pltpu.CompilerParams(vmem_limit_bytes=VMEM_LIMIT),
        cost_estimate=pl.CostEstimate(
            flops=int(micros * SCALE), bytes_accessed=0, transcendentals=0
        ),
        **specs,
    )


class Grid:
    names = ("zh", "zl", "y", "x", "c")

    def __init__(self, mesh):
        experts, heads = mesh.shape["expert"], mesh.shape["head"]
        self.shape = (2, experts // 4, 2, heads // 2, 2)
        self.experts, self.heads = experts, heads
        self.total = experts * heads

    def size(self, name):
        return self.shape[self.names.index(name)]

    def coords(self, linear):
        out = []
        for extent in reversed(self.shape):
            out.append(linear % extent)
            linear = linear // extent
        return dict(zip(self.names, reversed(out)))

    def linear(self, coords):
        at = 0
        for name, extent in zip(self.names, self.shape):
            at = at * extent + coords[name] % extent
        return at

    def me(self, name):
        linear = lax.axis_index("expert") * self.heads + lax.axis_index("head")
        return self.coords(linear)[name]

    def send(self, value, target):
        pairs = [(i, self.linear(target(self.coords(i)))) for i in range(self.total)]
        return lax.ppermute(value, ("expert", "head"), pairs)

    def move(self, value, **by):
        return self.send(value, lambda at: {name: at[name] - by.get(name, 0) for name in at})

    def shift(self, value, name, by):
        return self.move(value, **{name: by})

    def exchange(self, value, name, *others):
        stride = self.linear({**dict.fromkeys(self.names, 0), name: 1}) // self.heads
        groups = [[at, at + stride] for at in range(self.experts) if at // stride % 2 == 0]
        both = jnp.broadcast_to(value[None], (2, *value.shape))
        both = lax.all_to_all(
            both, "expert", split_axis=0, concat_axis=0, tiled=True, axis_index_groups=groups
        )
        both = after(both, *others) if others else both
        return jnp.where(self.me(name) == 0, both[1], both[0])

    def gather(self, value, name, *others):
        extent, own = self.size(name), self.me(name)
        parts = [value] + [self.shift(value, name, by) for by in range(1, extent)]
        if others:
            parts[1] = after(parts[1], *others)
        if extent == 2:
            return jnp.where(own == 0, jnp.stack(parts), jnp.stack(parts[::-1]))
        return jnp.roll(jnp.stack(parts), own, axis=0)

    def scatter_sum(self, value, name, *waited):
        extent, own = self.size(name), self.me(name)
        if extent == 2:
            kept = jnp.where(own == 0, value[0], value[1])
            others = [self.shift(jnp.where(own == 0, value[1], value[0]), name, 1)]
        else:
            value = jnp.roll(value, -own, axis=0)
            kept = value[0]
            others = [self.shift(value[by], name, -by) for by in range(1, extent)]
        if waited:
            others[0] = after(others[0], *waited)
        total = kept.astype(single)
        for other in others:
            total = total + other.astype(single)
        return total.astype(value.dtype)


def after(value, *others):
    return lax.optimization_barrier((value, *others))[0]


def per_device(
    grid,
    tokens,
    segment_ids,
    task_ids,
    task_table,
    weight_qkv,
    weight_out,
    gain_one,
    gain_two,
    weight_router,
    weight_in,
    weight_hidden,
    cotangent,
):
    expert_count, head_count = grid.experts, grid.heads
    head_index = lax.axis_index("head")
    row_count, model_width = tokens.shape
    cap = 4 * row_count // expert_count
    deep, wide = weight_qkv.shape[1:]
    padded = -(-expert_count // 16) * 16

    pieces = jnp.concatenate([weight_qkv, weight_out.T[None]]).astype(bfloat)
    small = jnp.concatenate(
        [gain_one[None], gain_two[None], weight_router.T]
    ).astype(bfloat).reshape(-1)
    small_rows = -(-small.shape[0] // wide)
    small = jnp.pad(small, (0, small_rows * wide - small.shape[0])).reshape(small_rows, wide)
    packed = jnp.concatenate([pieces.reshape(4 * deep, wide), small])
    own_segments = lax.dynamic_slice_in_dim(segment_ids, head_index * row_count, row_count)
    shape = jax.ShapeDtypeStruct
    vmem, hbm = pl.BlockSpec(memory_space=pltpu.VMEM), pl.BlockSpec(memory_space=pl.ANY)
    smem = pl.BlockSpec(memory_space=pltpu.SMEM)
    table = jnp.pad(task_table.T, ((0, 16 - task_table.shape[1]), (0, 0))).astype(bfloat)
    hidden = weight_in.shape[2]
    deep_in = weight_in.shape[1]
    piece = shape((hidden // model_width * deep_in + weight_hidden.shape[1], model_width), bfloat)
    route_rows = padded * (2 * (row_count // model_width) + 2)
    first, second, route, own_piece, sent = whole_call(
        lambda *refs: routing_kernel(cap, *refs),
        [shape((1, row_count), jnp.int32)] * 2
        + [
            shape((padded, row_count), single),
            piece,
            shape((row_count + route_rows, model_width), bfloat),
        ],
        micros=3,
    )(own_segments[None], task_ids[None], table, weight_in, weight_hidden, cotangent)
    names = {name: grid.me(name) for name in grid.names}
    extent = grid.size("zl")
    offsets = [(dl, dy) for dl in range(extent) for dy in range(2)]
    offsets.sort(key=lambda by: by[0] * by[1] != 0)
    providers = len(offsets)

    def expert_of(zl, y, local):
        return ((names["zh"] + local) % 2 * extent + zl % extent) * 2 + y % 2

    def ints(*values):
        return jnp.concatenate([jnp.asarray(v, jnp.int32).reshape(-1) for v in values])

    targets = ints(
        *[expert_of(names["zl"] - dl, names["y"] - dy, k) for dl, dy in offsets for k in range(2)],
        names["c"],
    )
    parcel = shape((2 * cap + EXTRA, model_width), bfloat)
    packed = grid.gather(grid.gather(packed, "zh"), "zl")
    nearly = packed
    packed = grid.gather(packed, "y")
    smalls = packed.transpose(2, 1, 0, 3, 4).reshape(expert_count, -1)[:, 4 * deep * wide :]
    smalls = smalls[:, : (2 + expert_count) * deep].reshape(expert_count, 2 + expert_count, deep)
    smalls = smalls.transpose(1, 0, 2).reshape(2 + expert_count, model_width)
    gain1, gain2 = smalls[0:1].astype(single), smalls[1:2].astype(single)
    router = jnp.pad(smalls[2:], ((0, padded - expert_count), (0, 0)))
    packed = grid.gather(packed[..., : 4 * deep, :], "x")
    packed = packed.reshape(*packed.shape[:4], 4, deep, wide)
    if wide % LANES:
        packed = grid.gather(packed, "c").transpose(5, 4, 3, 2, 6, 1, 0, 7)
        packed = packed.reshape(4, model_width, model_width)
        weights = (packed, packed)
    else:
        weights = (packed, grid.shift(packed, "c", 1))

    segc = own_segments[:, None]
    starts = [min(max(at - SPAN, 0), row_count - WINDOW) for at in range(0, row_count, BLOCK)]
    segw = jnp.stack([own_segments[at : at + WINDOW] for at in starts])

    core = ints(names["c"])
    gate_rows = 2 * padded * (row_count // model_width)
    proj, attn, res, two_low, stat, gate, weights = whole_call(
        forward_kernel,
        [
            shape((3, row_count, model_width), bfloat),
            shape((row_count, model_width), bfloat),
            shape((row_count, model_width), single),
            shape((row_count + gate_rows, model_width), bfloat),
            shape((row_count, LANES), single),
            shape((padded, row_count), single),
            shape((4, model_width, model_width), bfloat),
        ],
        in_specs=[smem, vmem, hbm, hbm] + [vmem] * 7,
        scratch=[
            pltpu.VMEM((4, model_width, model_width), bfloat),
            pltpu.SemaphoreType.DMA((2, head_count // 2 * expert_count)),
        ],
        micros=0.2,
    )(core, tokens, *weights, gain1, gain2, router, segc, segw, first, second)

    own_piece = after(own_piece, nearly)
    pieces = {(0, 0, 0): own_piece, (1, 0, 0): grid.exchange(own_piece, "zh")}
    for by_x in range(1, head_count // 2):
        pieces[0, by_x, 0] = grid.shift(own_piece, "x", by_x)
    own_experts = [expert_of(names["zl"], names["y"], local) for local in range(2)]
    sent = after(sent, nearly)
    cots = {(dl, 0): grid.move(sent, zl=dl) if dl else sent for dl in range(extent)}
    cots[0, 1] = grid.move(sent, y=1)
    pieces[1, 0, 0] = after(pieces[1, 0, 0], two_low)
    rows = {(dl, 0): grid.move(two_low, zl=dl) if dl else two_low for dl in range(extent)}
    rows[0, 1] = grid.move(two_low, y=1)
    for dl in range(1, extent):
        cots[dl, 1] = grid.move(cots[dl, 0], y=1)
    for by_x in range(1, head_count // 2):
        piece_x = grid.shift(after(pieces[1, 0, 0], cots[0, 1]), "x", by_x)
        pieces[1, by_x, 0] = after(piece_x, cots[1, 0], rows[0, 1])
    for by_x in range(head_count // 2):
        for local in range(2):
            pieces[local, by_x, 1] = grid.shift(pieces[local, by_x, 0], "c", 1)
    piece_keys = [(k, bx, bc) for k in range(2) for bx in range(head_count // 2) for bc in range(2)]
    piece_list = [pieces[key] for key in piece_keys]

    groups = [[0, 1]] + [[at] for at in range(2, min(4, providers))]
    groups += [list(range(at, min(at + 3, providers))) for at in range(4, providers, 3)]
    save_tiles = sum(-(-len(group) * cap // TILE) for group in groups)
    save_shapes = [
        shape((2, save_tiles * TILE, cols), bfloat)
        for cols in (model_width, model_width, hidden, hidden)
    ]
    saved = []
    tiles_before = jnp.zeros((2,), jnp.int32)
    results = {}
    for group in groups:
        count = len(group)
        keys = [offsets[s] for s in group]
        inputs = [ints(names["x"], names["c"], *own_experts), tiles_before]
        inputs += [rows[key] for key in keys] + [cots[key] for key in keys]
        inputs += piece_list + saved
        before = 2 + 2 * count + len(piece_list)
        outs = whole_call(
            lambda *refs, count=count, new=not saved: expert_kernel(
                count, head_count, cap, row_count, padded, new, *refs
            ),
            save_shapes + [parcel] * (2 * count) + [shape((2,), jnp.int32)],
            in_specs=[smem, smem] + [hbm] * (2 * count + len(piece_list) + len(saved)),
            out_specs=[hbm] * (4 + 2 * count) + [smem],
            aliases={before + i: i for i in range(len(saved))},
            scratch=[
                pltpu.VMEM((2, model_width, hidden), bfloat),
                pltpu.VMEM((2, hidden, model_width), bfloat),
                pltpu.VMEM((count, row_count + gate_rows, model_width), bfloat),
                pltpu.VMEM((count, *sent.shape), bfloat),
                pltpu.VMEM((count, 2 * cap, model_width), bfloat),
                pltpu.VMEM((count, 2 * cap, model_width), bfloat),
                pltpu.VMEM((count, 2 * cap, 1), single),
                pltpu.VMEM((count, *parcel.shape), bfloat),
                pltpu.VMEM((count, *parcel.shape), bfloat),
                pltpu.VMEM((count, 8, cap), single),
                pltpu.VMEM((TILE, model_width), bfloat),
                pltpu.VMEM((TILE, model_width), bfloat),
                pltpu.VMEM((TILE, 1), single),
                pltpu.VMEM((2, TILE, model_width), bfloat),
                pltpu.VMEM((2, TILE, model_width), bfloat),
                pltpu.VMEM((2, TILE, hidden), bfloat),
                pltpu.VMEM((2, TILE, hidden), bfloat),
                pltpu.SMEM((2, count * cap // HALF + 1), jnp.int32),
                pltpu.SemaphoreType.DMA((2, head_count * (hidden // model_width + 1))),
                pltpu.SemaphoreType.DMA((2, count)),
                pltpu.SemaphoreType.DMA((2, 4)),
                pltpu.SemaphoreType.DMA((2, count)),
            ],
            micros=24 * count + 10,
        )(*inputs)
        if not saved:
            for dl in range(1, extent):
                rows[dl, 0] = after(rows[dl, 0], outs[0])
                rows[dl, 1] = grid.move(rows[dl, 0], y=1)
        saved, tiles_before = list(outs[:4]), outs[-1]
        for i, s in enumerate(group):
            results[s] = [outs[4 + i], outs[4 + count + i]]
    out_parcels, grad_parcels = [], []
    for s, (dl, dy) in enumerate(offsets):
        out_part, grad_part = results[s]
        if dl or dy:
            grad_part, out_part = (grid.move(v, zl=-dl, y=-dy) for v in (grad_part, out_part))
        out_parcels.append(out_part)
        grad_parcels.append(grad_part)
    waited = grad_parcels[1 : max(2, providers - 1)]
    done = whole_call(
        lambda *refs: weight_kernel(head_count, len(waited), *refs),
        [piece] * len(piece_keys),
        in_specs=[smem, smem] + [hbm] * (4 + len(waited)),
        scratch=[
            pltpu.VMEM((model_width, hidden), single),
            pltpu.VMEM((model_width, hidden), single),
            pltpu.VMEM((2, TILE, model_width), bfloat),
            pltpu.VMEM((2, TILE, model_width), bfloat),
            pltpu.VMEM((2, TILE, hidden), bfloat),
            pltpu.VMEM((2, TILE, hidden), bfloat),
            pltpu.SemaphoreType.DMA((2, 4)),
        ],
        micros=24,
    )(ints(names["x"], names["c"]), tiles_before, *saved, *waited)
    done = lax.optimization_barrier((*done, *grad_parcels[1:], *out_parcels[1:-1]))
    grad_parcels = grad_parcels[:1] + list(done[len(piece_keys) :][: providers - 1])
    out_parcels[1:-1] = done[len(piece_keys) + providers - 1 :]
    grads = dict(zip(piece_keys, done))

    def add(kept, other):
        return (kept.astype(single) + other.astype(single)).astype(bfloat)

    waited = [grads[0, 0, 0]]
    for local in (1, 0):
        for by_x in range(head_count // 2):
            grads[local, by_x, 0] = add(
                grads[local, by_x, 0], grid.shift(grads[local, by_x, 1], "c", -1)
            )
    waited += [grads[1, by_x, 0] for by_x in (0, 1)]
    output = whole_call(
        lambda *refs: output_kernel(providers, cap, *refs),
        shape((row_count, model_width), bfloat),
        in_specs=[smem] + [vmem] * (3 + providers),
        micros=8,
    )(targets, res, gate, route, *out_parcels)

    grad_res, grad_heads, grad_out, grad_gain2, grad_router = whole_call(
        lambda *refs: middle_kernel(providers, cap, len(waited), *refs),
        (
            shape((row_count, model_width), single),
            shape((row_count, model_width), bfloat),
            shape((model_width, model_width), bfloat),
            shape((1, model_width), single),
            shape((padded, model_width), single),
        ),
        in_specs=[smem] + [vmem] * (9 + providers) + [hbm] * len(waited),
        scratch=[
            pltpu.VMEM((padded, row_count), single),
            pltpu.VMEM((row_count, model_width), bfloat),
        ],
        micros=40,
    )(
        targets, cotangent, res, two_low, attn, weights, gain2, router, gate, route,
        *grad_parcels, *waited,
    )
    for by_x in range(1, head_count // 2):
        other = after(grid.shift(grads[1, by_x, 0], "x", -by_x), grad_gain2)
        grads[1, 0, 0] = add(grads[1, 0, 0], other)
    grad_res = after(grad_res, grads[1, 0, 0], grads[0, 1, 0])
    columns = model_width if wide % LANES else model_width // 2
    grad_tokens, grad_own, other_top, other_rest, grad_gain1 = whole_call(
        lambda *refs: backward_kernel(head_count, *refs),
        (
            shape((row_count, model_width), single),
            shape((4, model_width, columns), bfloat),
            shape((2, model_width, columns), bfloat),
            shape((2, model_width, columns), bfloat),
            shape((1, model_width), single),
        ),
        in_specs=[smem] + [vmem] * 10,
        scratch=[
            pltpu.VMEM((3, row_count, model_width), bfloat),
            pltpu.VMEM((row_count, model_width), single),
            pltpu.VMEM((row_count, model_width), single),
            pltpu.VMEM((row_count, model_width), bfloat),
            pltpu.VMEM((4, model_width, model_width), bfloat),
        ],
        micros=1,
    )(
        core, tokens, proj, stat, weights, gain1, segc, segw, grad_res, grad_heads, grad_out,
    )

    for by_x in range(1, head_count // 2):
        other = after(grid.shift(grads[0, by_x, 0], "x", -by_x), grad_tokens)
        grads[0, 0, 0] = add(grads[0, 0, 0], other)
    other_top = after(other_top, out_parcels[-1])
    smalls = jnp.concatenate([grad_gain1, grad_gain2, grad_router[:expert_count]]).astype(bfloat)
    if wide % LANES:
        packed = grad_own.reshape(4, model_width, -1, 2, wide).transpose(3, 0, 1, 2, 4)
        packed = grid.scatter_sum(packed, "c").reshape(4, model_width, -1)
    else:
        other = [grid.shift(v, "c", 1) for v in (other_top, other_rest)]
        packed = add(grad_own, jnp.concatenate(other))
    packed = packed.reshape(4, model_width, -1, wide).transpose(2, 0, 1, 3)
    packed = grid.scatter_sum(after(packed, grads[0, 0, 0]), "x", output)
    grad_piece = grads[0, 0, 0].astype(single) + grid.exchange(
        grads[1, 0, 0], "zh", packed
    ).astype(single)
    grad_in_own = grad_piece[: hidden // model_width * deep_in]
    grad_in_own = grad_in_own.reshape(-1, deep_in, model_width).transpose(1, 0, 2)
    grad_in_own = grad_in_own.reshape(1, deep_in, hidden)
    grad_hidden_own = grad_piece[hidden // model_width * deep_in :][None]
    for name in ("c", "x"):
        total = smalls.astype(single)
        for by in range(1, grid.size(name)):
            total = total + grid.shift(smalls, name, by).astype(single)
        smalls = total.astype(bfloat)
    smalls = smalls.reshape(2 + expert_count, expert_count, deep).transpose(1, 0, 2)
    smalls = smalls.reshape(expert_count, -1)
    smalls = jnp.pad(smalls, ((0, 0), (0, small_rows * wide - smalls.shape[1])))
    packed = packed.reshape(4, expert_count, deep, wide).transpose(1, 0, 2, 3)
    packed = packed.reshape(expert_count, 4 * deep, wide)
    packed = jnp.concatenate([packed, smalls.reshape(expert_count, small_rows, wide)], axis=1)
    packed = packed.reshape(*grid.shape[:3], 4 * deep + small_rows, wide).transpose(2, 1, 0, 3, 4)
    packed = after(packed, grad_piece)
    for name in ("y", "zl", "zh"):
        packed = grid.scatter_sum(packed, name)
    pieces = packed[: 4 * deep].reshape(4, deep, wide).astype(single)
    smalls = packed[4 * deep :].reshape(-1)[: (2 + expert_count) * deep].astype(single)
    smalls = smalls.reshape(2 + expert_count, deep)
    return (
        output,
        grad_tokens,
        pieces[:3],
        pieces[3].T,
        smalls[0],
        smalls[1],
        smalls[2:].T,
        grad_in_own,
        grad_hidden_own,
    )


def solution(mesh):
    grid = Grid(mesh)
    placed = (
        P(("expert", "head"), None),
        P("expert"),
        P(),
        P(),
        P(None, "expert", "head"),
        P("head", "expert"),
        P("expert"),
        P("expert"),
        P("expert", None),
        P("expert", "head", None),
        P("expert", "head", None),
        P(("expert", "head"), None),
    )

    def step(*arrays):
        return per_device(grid, *arrays)

    return jax.shard_map(
        step,
        mesh=mesh,
        in_specs=placed,
        out_specs=(
            P(("expert", "head"), None),
            P(("expert", "head"), None),
            P(None, "expert", "head"),
            P("head", "expert"),
            P("expert"),
            P("expert"),
            P("expert", None),
            P("expert", "head", None),
            P("expert", "head", None),
        ),
        check_vma=False,
    )
```

```python
import jax
import jax.numpy as jnp
from jax import lax
from jax.experimental import pallas as pl
from jax.experimental.pallas import tpu as pltpu
from jax.sharding import PartitionSpec as P

HDIM = 64
PACK = 1024
SPAN = 64
BLOCK = 128
WINDOW = BLOCK + 2 * SPAN
CHUNK = 256
LANES = 128
TILE = 256
HALF = 128
EXTRA = 16
PART = 256
ABSENT = -1e6
SCALE = 1153e6 / 8

EPSILON = 1e-05
NEGATIVE = -1e30

bfloat = jnp.bfloat16
single = jnp.float32
VMEM_LIMIT = 56 * 1024 * 1024


def dot_nn(a, b):
    return lax.dot_general(a, b, (((1,), (0,)), ((), ())), preferred_element_type=single)


def dot_nt(a, b):
    return lax.dot_general(a, b, (((1,), (1,)), ((), ())), preferred_element_type=single)


def dot_tn(a, b):
    return lax.dot_general(a, b, (((0,), (0,)), ((), ())), preferred_element_type=single)


def normalise(values):
    centered = values - jnp.mean(values, axis=-1, keepdims=True)
    inverse = lax.rsqrt(jnp.mean(centered * centered, axis=-1, keepdims=True) + EPSILON)
    return centered * inverse, inverse


def norm_pull(grad_normed, scaled, inverse, gain):
    weighted = grad_normed * gain
    return inverse * (
        weighted
        - jnp.mean(weighted, axis=-1, keepdims=True)
        - scaled * jnp.mean(weighted * scaled, axis=-1, keepdims=True)
    )


def split_heads(pair, first_half):
    zero = jnp.zeros_like(pair)
    return jnp.concatenate(
        [jnp.where(first_half, pair, zero), jnp.where(first_half, zero, pair)], axis=0
    )


def window_start(block, rows):
    return pl.multiple_of(jnp.clip(block * BLOCK - SPAN, 0, rows - WINDOW), SPAN)


def fetch_weights(core, own, other, weights, sem):
    copies = []
    if own.shape == weights.shape:
        copies = [pltpu.make_async_copy(own, weights, sem.at[0, 0])]
    else:
        parts_x, parts_y, parts_zl, parts_zh, _, deep, wide = own.shape
        places = [
            (x, y, zl, zh)
            for x in range(parts_x)
            for y in range(parts_y)
            for zl in range(parts_zl)
            for zh in range(parts_zh)
        ]
        for at, (x, y, zl, zh) in enumerate(places):
            row = ((zh * parts_zl + zl) * parts_y + y) * deep
            for i, (ref, half) in enumerate(((own, core), (other, 1 - core))):
                start = pl.multiple_of((2 * x + half) * wide, LANES)
                copies.append(
                    pltpu.make_async_copy(
                        ref.at[x, y, zl, zh],
                        weights.at[:, pl.ds(row, deep), pl.ds(start, wide)],
                        sem.at[i, at],
                    )
                )
    for copy in copies:
        copy.start()
    for copy in copies:
        copy.wait()


def forward_kernel(
    meta, tok, weights_own, weights_other, gain1, gain2, router, segc, segw, first, second,
    proj_out, attn_out, res_out, two_out, stat_out, gate, weights_out,
    proj, attn, res, two, stat, weights, sem, out_sem,
):
    rows, width = tok.shape
    fetch_weights(meta[0], weights_own, weights_other, weights, sem)
    wqkv, wot = weights, weights.at[3]
    leaving = [pltpu.make_async_copy(weights, weights_out, out_sem.at[0, 0])]
    leaving[0].start()

    def project(step, carry):
        at = pl.ds(pl.multiple_of(step * CHUNK, CHUNK), CHUNK)
        scaled, _ = normalise(tok[at, :].astype(single))
        low = (scaled * gain1[...]).astype(bfloat)
        for part in range(3):
            proj[part, at, :] = dot_nn(low, wqkv[part]).astype(bfloat)
        return carry

    lax.fori_loop(0, rows // CHUNK, project, 0)
    leaving.append(pltpu.make_async_copy(proj, proj_out, out_sem.at[0, 1]))
    leaving[1].start()

    def block_copies(block):
        at = pl.ds(pl.multiple_of(block * BLOCK, BLOCK), BLOCK)
        return [
            pltpu.make_async_copy(held.at[at, :], out.at[at, :], out_sem.at[1 + i, block])
            for i, (held, out) in enumerate(
                ((attn, attn_out), (res, res_out), (two, two_out), (stat, stat_out))
            )
        ]

    lane = lax.broadcasted_iota(jnp.int32, (BLOCK, LANES), 1)
    first_half = lane < HDIM
    expert = lax.broadcasted_iota(jnp.int32, (router.shape[0], BLOCK), 0)

    def attend(block, carry):
        q_at = pl.ds(pl.multiple_of(block * BLOCK, BLOCK), BLOCK)
        k_at = pl.ds(window_start(block, rows), WINDOW)
        same = (segc[q_at, :] == segw[pl.ds(block, 1), :])[None]
        totals = jnp.zeros((BLOCK, LANES), single)
        for pair in range(width // LANES):
            cols = slice(pair * LANES, (pair + 1) * LANES)
            queries = split_heads(proj[0, q_at, cols] * HDIM**-0.5, first_half)
            scores = dot_nt(queries, proj[1, k_at, cols]).reshape(2, BLOCK, WINDOW)
            scores = jnp.where(same, scores, NEGATIVE)
            peak = jnp.max(scores, axis=-1, keepdims=True)
            exponent = jnp.exp(scores - peak)
            total = jnp.sum(exponent, axis=-1, keepdims=True)
            probs = (exponent * (1.0 / total)).astype(bfloat).reshape(2 * BLOCK, WINDOW)
            out = dot_nn(probs, proj[2, k_at, cols])
            attn[q_at, cols] = jnp.where(first_half, out[:BLOCK], out[BLOCK:]).astype(bfloat)
            log_total = peak + jnp.log(total)
            for half in range(2):
                totals = jnp.where(lane == 2 * pair + half, log_total[half], totals)
        stat[q_at, :] = totals
        residual = tok[q_at, :].astype(single) + dot_nt(attn[q_at, :], wot[...])
        res[q_at, :] = residual
        scaled, _ = normalise(residual)
        low = (scaled * gain2[...]).astype(bfloat)
        two[q_at, :] = low
        logits = dot_nt(router[...], low)
        mark0 = first[:, q_at] == expert
        mark1 = second[:, q_at] == expert
        logit0 = jnp.sum(jnp.where(mark0, logits, 0.0), axis=0, keepdims=True)
        logit1 = jnp.sum(jnp.where(mark1, logits, 0.0), axis=0, keepdims=True)
        top = jnp.maximum(logit0, logit1)
        part0, part1 = jnp.exp(logit0 - top), jnp.exp(logit1 - top)
        scale = 1.0 / (part0 + part1)
        gate[:, q_at] = jnp.where(mark0, part0 * scale, jnp.where(mark1, part1 * scale, 0.0))
        for copy in block_copies(block):
            copy.start()
        return carry

    lax.fori_loop(0, rows // BLOCK, attend, 0)
    count = gate.shape[0]
    at = rows
    for part in split_two(gate[...]):
        for start in range(0, rows, width):
            two[at : at + count, :] = part[:, start : start + width]
            at += count
    rest = pl.ds(rows, two.shape[0] - rows)
    leaving.append(
        pltpu.make_async_copy(two.at[rest, :], two_out.at[rest, :], out_sem.at[0, 2])
    )
    leaving[2].start()
    for copy in leaving:
        copy.wait()

    def settle(block, carry):
        for copy in block_copies(block):
            copy.wait()
        return carry

    lax.fori_loop(0, rows // BLOCK, settle, 0)


def split_two(values):
    high = values.astype(bfloat)
    return high, (values - high.astype(single)).astype(bfloat)


def pack_rows(rows):
    at = lax.broadcasted_iota(jnp.int32, (EXTRA, rows.shape[1]), 0)
    out = jnp.zeros((EXTRA, rows.shape[1]), single)
    for local in range(2):
        high = rows[local : local + 1, :].astype(bfloat).astype(single)
        out = jnp.where(at == 2 * local, high, out)
        out = jnp.where(at == 2 * local + 1, rows[local : local + 1, :] - high, out)
    return out.astype(bfloat)


def unpack_row(packed, local):
    packed = packed.astype(single)
    return packed[2 * local : 2 * local + 1, :] + packed[2 * local + 1 : 2 * local + 2, :]


def routing_kernel(
    cap, segments, tasks, table, weight_in, weight_hidden, cot,
    first, second, route, piece, sent,
):
    rows = segments.shape[1]
    deep, hidden = weight_in.shape[1:]
    width = piece.shape[1]
    for part in range(hidden // width):
        piece[part * deep : (part + 1) * deep, :] = weight_in[
            0, :, part * width : (part + 1) * width
        ].astype(bfloat)
    piece[hidden // width * deep :, :] = weight_hidden[0].astype(bfloat)
    names = lax.broadcasted_iota(jnp.int32, (table.shape[1], tasks.shape[1]), 0)
    experts = dot_nn(table[...], jnp.where(names == tasks[...], 1.0, 0.0).astype(bfloat))
    experts = experts.astype(bfloat)
    chosen = jnp.zeros((table.shape[0], rows), single)
    for start in range(0, tasks.shape[1], 1024):
        size = min(1024, tasks.shape[1] - start)
        at = lax.broadcasted_iota(jnp.int32, (size, rows), 0) + start
        ones = jnp.where(at == segments[...], 1.0, 0.0).astype(bfloat)
        chosen = chosen + dot_nn(experts[:, start : start + size], ones)
    zero, one = chosen[0:1, :], chosen[1:2, :]
    first[...] = zero.astype(jnp.int32)
    second[...] = one.astype(jnp.int32)
    which = lax.broadcasted_iota(jnp.int32, route.shape, 0).astype(single)
    is_first, is_second = which == zero, which == one
    marks = jnp.where(is_first | is_second, 1.0, 0.0)
    earlier = lax.broadcasted_iota(jnp.int32, (rows, rows), 0) < lax.broadcasted_iota(
        jnp.int32, (rows, rows), 1
    )
    places = dot_nn(marks.astype(bfloat), jnp.where(earlier, 1.0, 0.0).astype(bfloat))
    inside = (marks > 0.5) & (places < cap)
    slots = jnp.where(inside, places, ABSENT)
    route[...] = slots
    total = jnp.sum(jnp.where(inside, 1.0, 0.0), axis=1, keepdims=True)
    total = jnp.broadcast_to(total, (route.shape[0], width))
    sent[:rows, :] = cot[...]
    at = rows
    for part in range(2):
        for start in range(0, rows, width):
            sent[at : at + route.shape[0], :] = sixteens(slots[:, start : start + width])[part]
            at += route.shape[0]
    for part in range(2):
        sent[at : at + route.shape[0], :] = sixteens(total)[part]
        at += route.shape[0]


def sixteens(values):
    high = jnp.floor(values * 0.0625) * 16.0
    high = jnp.where(values < 0.0, values, high)
    return high.astype(bfloat), jnp.where(values < 0.0, 0.0, values - high).astype(bfloat)


def output_kernel(providers, cap, meta, res, gate, slots, *refs):
    parcels, out = refs[:providers], refs[providers]
    for step in range(res.shape[0] // CHUNK):
        at = slice(step * CHUNK, (step + 1) * CHUNK)
        out[at, :] = (res[at, :] + returned_rows(parcels, cap, meta, gate, slots, at)).astype(bfloat)


def returned_rows(parcels, cap, meta, gate, slots, at):
    total = 0.0
    for provider, parcel in enumerate(parcels):
        for local in range(2):
            chosen = pl.ds(meta[2 * provider + local], 1)
            ones = onehot(slots[chosen, at], 0, cap, gate[chosen, at])
            total = total + dot_tn(ones, parcel[local * cap : (local + 1) * cap, :])
    return total


def middle_kernel(
    providers, cap, waited, meta,
    cot_in, res_in, two_in, attn_in, weights_in, gain2, router, gate, slots,
    *refs,
):
    parcels = refs[:providers]
    (
        res_left, heads_left, grad_out, grad_gain2, grad_router,
        products, grad_attn, grad_res, grad_heads, cot, res, two, attn, wot, parcel_bufs, sem, out_sem,
    ) = refs[providers + waited :]
    rows, width = cot.shape
    two_rows = two_in.at[pl.ds(0, rows), :]
    arriving = [
        pltpu.make_async_copy(given, held, sem.at[i])
        for i, (given, held) in enumerate(
            [(parcel, parcel_bufs.at[at]) for at, parcel in enumerate(parcels)]
            + [(res_in, res), (cot_in, cot), (weights_in.at[3], wot), (two_rows, two), (attn_in, attn)]
        )
    ]
    for copy in arriving:
        copy.start()
    parcels = [parcel_bufs.at[at] for at in range(providers)]
    for copy in arriving[:providers]:
        copy.wait()
    products[...] = jnp.zeros_like(products)
    for provider in range(providers):
        for local in range(2):
            chosen = meta[2 * provider + local]
            ones = onehot(slots[pl.ds(chosen, 1), :], 0, cap)
            moved = dot_nn(parcels[provider][2 * cap :, :cap], ones)
            products[pl.ds(chosen, 1), :] = unpack_row(moved, local)
    gates = gate[...]
    inner_products = products[...]
    grad_logits = gates * (
        inner_products - jnp.sum(gates * inner_products, axis=0, keepdims=True)
    )
    grad_logits = jnp.concatenate(split_two(grad_logits), axis=0)
    router_twice = jnp.concatenate([router[...], router[...]], axis=0)
    count = router.shape[0]
    grad_gain2[...] = jnp.zeros_like(grad_gain2)
    for copy in arriving[providers : providers + 3]:
        copy.wait()
    leaving = []
    for step in range(rows // CHUNK):
        at = slice(step * CHUNK, (step + 1) * CHUNK)
        scaled, inverse = normalise(res[at, :])
        grad_normed = dot_tn(grad_logits[:, at], router_twice)
        grad_normed = grad_normed + returned_rows(parcels, cap, meta, gate, slots, at)
        grad_gain2[...] += jnp.sum(grad_normed * scaled, axis=0, keepdims=True)
        grad_row = cot[at, :].astype(single) + norm_pull(grad_normed, scaled, inverse, gain2[...])
        grad_res[at, :] = grad_row
        low = grad_row.astype(bfloat)
        grad_attn[at, :] = low
        grad_heads[at, :] = dot_nn(low, wot[...]).astype(bfloat)
        part = pl.ds(step * CHUNK, CHUNK)
        for i, (held, out) in enumerate(((grad_res, res_left), (grad_heads, heads_left))):
            leaving.append(
                pltpu.make_async_copy(held.at[part, :], out.at[part, :], out_sem.at[i, step])
            )
            leaving[-1].start()
    for copy in arriving[providers + 3 :]:
        copy.wait()
    routed = dot_nn(grad_logits, two[...])
    grad_router[...] = routed[:count] + routed[count:]
    grad_out[...] = dot_tn(grad_attn[...], attn[...]).astype(bfloat)
    for copy in leaving:
        copy.wait()


def backward_kernel(
    heads, core, gain1, segc, segw,
    proj_in, heads_in, stat_in, tok_in, res_in, weights_in, out_in,
    tok_left, grad_own, other_top, other_rest, grad_gain1,
    grad_proj, grad_key, grad_value, normed, grad_w,
    proj, grad_heads, stat, tok, grad_res, wqkv, grad_tok, sem, out_sem,
):
    rows, width = tok.shape
    arriving = [
        pltpu.make_async_copy(given, held, sem.at[i])
        for i, (given, held) in enumerate(
            (
                (proj_in, proj), (heads_in, grad_heads), (stat_in, stat), (tok_in, tok),
                (res_in, grad_res), (weights_in.at[pl.ds(0, 3)], wqkv), (out_in, grad_w.at[3]),
            )
        )
    ]
    for copy in arriving:
        copy.start()
    grad_gain1[...] = jnp.zeros_like(grad_gain1)
    grad_key[...] = jnp.zeros_like(grad_key)
    grad_value[...] = jnp.zeros_like(grad_value)
    for copy in arriving[:3]:
        copy.wait()
    lane = lax.broadcasted_iota(jnp.int32, (BLOCK, LANES), 1)
    first_half = lane < HDIM

    def attend(block, carry):
        q_at = pl.ds(pl.multiple_of(block * BLOCK, BLOCK), BLOCK)
        k_at = pl.ds(window_start(block, rows), WINDOW)
        same = (segc[q_at, :] == segw[pl.ds(block, 1), :])[None]
        totals = stat[q_at, :]
        for pair in range(width // LANES):
            cols = slice(pair * LANES, (pair + 1) * LANES)
            queries = split_heads(proj[0, q_at, cols] * HDIM**-0.5, first_half)
            keys_block = proj[1, k_at, cols]
            scores = dot_nt(queries, keys_block).reshape(2, BLOCK, WINDOW)
            scores = jnp.where(same, scores, NEGATIVE)
            log_total = jnp.stack(
                [totals[:, 2 * pair : 2 * pair + 1], totals[:, 2 * pair + 1 : 2 * pair + 2]]
            )
            probs = jnp.exp(scores - log_total).reshape(2 * BLOCK, WINDOW)
            heads_low = split_heads(grad_heads[q_at, cols], first_half)
            grad_probs = dot_nt(heads_low, proj[2, k_at, cols])
            delta = jnp.sum(probs * grad_probs, axis=-1, keepdims=True)
            grad_scores = (probs * (grad_probs - delta)).astype(bfloat)
            grad_query = dot_nn(grad_scores, keys_block) * HDIM**-0.5
            grad_proj[0, q_at, cols] = jnp.where(
                first_half, grad_query[:BLOCK], grad_query[BLOCK:]
            ).astype(bfloat)
            grad_key[k_at, cols] += dot_tn(grad_scores, queries)
            grad_value[k_at, cols] += dot_tn(probs.astype(bfloat), heads_low)
        return carry

    lax.fori_loop(0, rows // BLOCK, attend, 0)
    for copy in arriving[3:]:
        copy.wait()
    leaving = []
    for step in range(rows // CHUNK):
        at = slice(step * CHUNK, (step + 1) * CHUNK)
        grad_proj[1, at, :] = grad_key[at, :].astype(bfloat)
        grad_proj[2, at, :] = grad_value[at, :].astype(bfloat)
        grad_normed = dot_nt(grad_proj[0, at, :], wqkv[0])
        for part in (1, 2):
            grad_normed += dot_nt(grad_proj[part, at, :], wqkv[part])
        scaled, inverse = normalise(tok[at, :].astype(single))
        normed[at, :] = (scaled * gain1[...]).astype(bfloat)
        grad_gain1[...] += jnp.sum(grad_normed * scaled, axis=0, keepdims=True)
        grad_tok[at, :] = grad_res[at, :] + norm_pull(grad_normed, scaled, inverse, gain1[...])
        part = pl.ds(step * CHUNK, CHUNK)
        leaving.append(
            pltpu.make_async_copy(grad_tok.at[part, :], tok_left.at[part, :], out_sem.at[step])
        )
        leaving[-1].start()
    for part in range(3):
        grad_w[part] = dot_tn(normed[...], grad_proj[part]).astype(bfloat)
    if grad_own.shape == grad_w.shape:
        grad_own[...] = grad_w[...]
        other_top[...] = grad_w[:2]
        other_rest[...] = grad_w[2:]
    else:
        wide = width // heads
        for by in range(heads // 2):
            cols = slice(by * wide, (by + 1) * wide)
            start = pl.multiple_of((2 * by + core[0]) * wide, LANES)
            grad_own[:, :, cols] = grad_w[:, :, pl.ds(start, wide)]
            start = pl.multiple_of((2 * by + 1 - core[0]) * wide, LANES)
            other_top[:, :, cols] = grad_w[:2, :, pl.ds(start, wide)]
            other_rest[:, :, cols] = grad_w[2:, :, pl.ds(start, wide)]
    for copy in leaving:
        copy.wait()


def onehot(slots, base, rows, marks=1.0):
    places = lax.broadcasted_iota(jnp.int32, (rows, slots.shape[1]), 0).astype(single)
    return jnp.where(places == slots - base, marks, 0.0).astype(bfloat)


def gelu_both(values):
    bent = values * (0.7978845608028654 + 0.035677408136300125 * (values * values))
    half = 0.5 * jnp.tanh(bent) + 0.5
    steep = 6.0 * bent - 3.1915382432114616 * values
    return values * half, half * (1.0 + (1.0 - half) * steep)


def expert_kernel(sources, heads, cap, tokens, count, first, meta, before, *refs):
    refs = list(refs)

    def take(count):
        taken = refs[:count]
        del refs[:count]
        return taken

    rows_in, grads_in = take(sources), take(sources)
    pieces = take(2 * heads)
    if not first:
        take(4)
    saved = take(4)
    outs, grads = take(sources), take(sources)
    (now,) = take(1)
    (
        win, wout, row_all, grad_all, row_buf, grad_buf, gate_buf,
        out_buf, copy_buf, product_buf, now_x, now_g, now_gate,
        st_x, st_g, st_act, st_pre, table, w_sem, in_sem, s_sem, out_sem,
    ) = refs
    width = row_buf.shape[2]
    hidden = wout.shape[1]
    deep, wide = width // heads, hidden // heads
    head_x, head_c = meta[0], meta[1]
    staged = (st_x, st_g, st_act, st_pre)

    def weight_copies(local):
        at = 0
        for by_x in range(heads // 2):
            for by_c in range(2):
                head = lax.rem(head_x + by_x, heads // 2) * 2 + lax.rem(head_c + by_c, 2)
                piece = pieces[(local * (heads // 2) + by_x) * 2 + by_c]
                for part in range(hidden // width):
                    yield pltpu.make_async_copy(
                        piece.at[pl.ds(part * deep, deep), :],
                        win.at[
                            local,
                            pl.ds(pl.multiple_of(head * deep, deep), deep),
                            pl.ds(part * width, width),
                        ],
                        w_sem.at[local, at],
                    )
                    at += 1
                yield pltpu.make_async_copy(
                    piece.at[pl.ds(hidden // width * deep, wide), :],
                    wout.at[local, pl.ds(pl.multiple_of(head * wide, wide), wide), :],
                    w_sem.at[local, at],
                )
                at += 1

    def source_copies():
        for source in range(sources):
            for i, (given, held) in enumerate(((rows_in, row_all), (grads_in, grad_all))):
                yield pltpu.make_async_copy(given[source], held.at[source], in_sem.at[i, source])

    for copy in source_copies():
        copy.start()
    for local in range(2):
        for copy in weight_copies(local):
            copy.start()
    out_buf[...] = jnp.zeros_like(out_buf)
    copy_buf[...] = jnp.zeros_like(copy_buf)
    product_buf[...] = jnp.zeros_like(product_buf)

    def save_copies(slot, local, tile):
        at = pl.ds(pl.multiple_of(tile * TILE, TILE), TILE)
        return [
            pltpu.make_async_copy(stage.at[slot], save.at[local, at, :], s_sem.at[slot, i])
            for i, (stage, save) in enumerate(zip(staged, saved))
        ]

    eye = lax.broadcasted_iota(jnp.int32, (HALF, HALF), 0) == lax.broadcasted_iota(
        jnp.int32, (HALF, HALF), 1
    )
    for copy in source_copies():
        copy.wait()
    step_rows = min(TILE, cap)
    which = lax.broadcasted_iota(jnp.int32, (count, 1), 0)
    numbers, halves = {}, []
    for local in range(2):
        number = 0
        for source in range(sources):
            at = grad_all.shape[1] - 2 * count
            total = grad_all[source, at : at + count, :LANES].astype(single)
            total = total + grad_all[source, at + count :, :LANES].astype(single)
            total = jnp.max(jnp.where(which == meta[2 + local], total, 0.0)).astype(jnp.int32)
            numbers[source, local] = total
            for half in range(cap // HALF):
                table[local, number] = source * (cap // HALF) + half
                number = number + jnp.where(total > half * HALF, 1, 0)
        halves.append(number)
        now[local] = before[local] + (number + 1) // 2
    places = lax.broadcasted_iota(jnp.int32, (step_rows, tokens), 0).astype(single)
    for source in range(sources):
        for local in range(2):
            expert = meta[2 + local]

            def by_token(ref):
                row = []
                for part in range(tokens // width):
                    parts = [
                        ref[source, pl.ds(tokens + (i * (tokens // width) + part) * count, count), :]
                        for i in range(2)
                    ]
                    both = parts[0].astype(single) + parts[1].astype(single)
                    both = jnp.where(which == expert, both, 0.0)
                    row.append(jnp.sum(both, axis=0, keepdims=True))
                return jnp.concatenate(row, axis=1)

            gate_row, slot_row = by_token(row_all), by_token(grad_all)
            for step in range(cap // step_rows):

                @pl.when(numbers[source, local] > step * step_rows)
                def _():
                    at = slice(local * cap + step * step_rows, local * cap + (step + 1) * step_rows)
                    slots = slot_row - step * step_rows
                    ones = jnp.where(places == slots, 1.0, 0.0).astype(bfloat)
                    row_buf[source, at, :] = dot_nn(ones, row_all[source, :tokens, :]).astype(bfloat)
                    grad_buf[source, at, :] = dot_nn(ones, grad_all[source, :tokens, :]).astype(
                        bfloat
                    )
                    gate_buf[source, at, :] = jnp.sum(
                        jnp.where(places == slots, gate_row, 0.0), axis=1, keepdims=True
                    )

    done = 0
    for local in range(2):
        for copy in weight_copies(local):
            copy.wait()
        number = halves[local]

        def place(tile, half):
            entry = table[local, 2 * tile + half]
            step = lax.rem(entry, cap // HALF)
            start = pl.multiple_of(step * HALF, HALF)
            rows = pl.ds(pl.multiple_of(local * cap + start, HALF), HALF)
            return entry // (cap // HALF), rows, pl.ds(start, HALF)

        def one_tile(tile, done):
            slot = lax.rem(done, 2)

            @pl.when(done >= 2)
            def _():
                for copy in save_copies(slot, local, tile):
                    copy.wait()

            for half in range(2):
                at = pl.ds(half * HALF, HALF)

                @pl.when(2 * tile + half < number)
                def _():
                    source, rows, lanes = place(tile, half)
                    now_x[at, :] = row_buf[source, rows, :]
                    now_g[at, :] = grad_buf[source, rows, :]
                    now_gate[at, :] = gate_buf[source, rows, :]

                @pl.when(2 * tile + half >= number)
                def _():
                    now_x[at, :] = jnp.zeros((HALF, width), bfloat)
                    now_g[at, :] = jnp.zeros((HALF, width), bfloat)
                    now_gate[at, :] = jnp.zeros((HALF, 1), single)

            rows_low, grad_low, gate = now_x[...], now_g[...], now_gate[...]
            st_x[slot] = (rows_low.astype(single) * gate).astype(bfloat)
            st_g[slot] = (grad_low.astype(single) * gate).astype(bfloat)
            for start in range(0, hidden, PART):
                cols = slice(start, start + PART)
                pre = dot_nn(rows_low, win[local, :, cols])
                grad_act = dot_nt(grad_low, wout[local, cols, :])
                act, slope = gelu_both(pre)
                st_act[slot, :, cols] = act.astype(bfloat)
                st_pre[slot, :, cols] = (slope * grad_act).astype(bfloat)
            result = dot_nn(st_act[slot], wout[local]).astype(bfloat).astype(single)
            grad_copy = dot_nt(st_pre[slot], win[local]).astype(bfloat)
            product = jnp.sum(grad_low.astype(single) * result, axis=1, keepdims=True)
            result = result.astype(bfloat)
            for half in range(2):
                at = slice(half * HALF, (half + 1) * HALF)

                @pl.when(2 * tile + half < number)
                def _():
                    source, rows, lanes = place(tile, half)
                    out_buf[source, rows, :] = result[at]
                    copy_buf[source, rows, :] = grad_copy[at]
                    product_buf[source, local : local + 1, lanes] = jnp.sum(
                        jnp.where(eye, product[at], 0.0), axis=0, keepdims=True
                    )

            for copy in save_copies(slot, local, before[local] + tile):
                copy.start()
            return done + 1

        done = lax.fori_loop(0, (number + 1) // 2, one_tile, done)

    def result_copies():
        for source in range(sources):
            yield pltpu.make_async_copy(copy_buf.at[source], grads[source], out_sem.at[0, source])
            yield pltpu.make_async_copy(out_buf.at[source], outs[source], out_sem.at[1, source])

    for source in range(sources):
        copy_buf[source, 2 * cap :, :cap] = pack_rows(product_buf[source])
    for copy in result_copies():
        copy.start()
    for back in (1, 2):

        @pl.when(done >= back)
        def _():
            for copy in save_copies(lax.rem(done - back, 2), 0, 0):
                copy.wait()

    for copy in result_copies():
        copy.wait()


def weight_kernel(heads, waited, meta, tiles_saved, save_x, save_g, save_act, save_pre, *refs):
    refs = list(refs[waited:])
    outs = [
        [refs.pop(0) for _ in range(2 if local and by_x and by_c else 1)]
        for local in range(2)
        for by_x in range(heads // 2)
        for by_c in range(2)
    ]
    grad_in, grad_out, buf_x, buf_g, buf_act, buf_pre, sem = refs
    width, hidden = grad_in.shape
    deep, wide = width // heads, hidden // heads
    buffers = (buf_x, buf_g, buf_act, buf_pre)

    def fetch(slot, local, tile):
        at = pl.ds(pl.multiple_of(tile * TILE, TILE), TILE)
        return [
            pltpu.make_async_copy(save.at[local, at, :], buf.at[slot], sem.at[slot, i])
            for i, (save, buf) in enumerate(zip((save_x, save_g, save_act, save_pre), buffers))
        ]

    for local in (1, 0):
        tiles = tiles_saved[local]
        grad_in[...] = jnp.zeros_like(grad_in)
        grad_out[...] = jnp.zeros_like(grad_out)

        @pl.when(tiles > 0)
        def _():
            for copy in fetch(0, local, 0):
                copy.start()

        def one_tile(tile, carry):
            slot = lax.rem(tile, 2)

            @pl.when(tile + 1 < tiles)
            def _():
                for copy in fetch(1 - slot, local, tile + 1):
                    copy.start()

            for copy in fetch(slot, local, tile):
                copy.wait()
            for part in range(hidden // width):
                cols = slice(part * width, (part + 1) * width)
                grad_in[:, cols] += dot_tn(buf_x[slot], buf_pre[slot, :, cols])
                grad_out[:, cols] += dot_tn(buf_g[slot], buf_act[slot, :, cols])
            return carry

        lax.fori_loop(0, tiles, one_tile, 0)
        for by_x in range(heads // 2):
            for by_c in range(2):
                head = lax.rem(meta[0] + by_x, heads // 2) * 2 + lax.rem(meta[1] + by_c, 2)
                out, *rest = outs[(local * (heads // 2) + by_x) * 2 + by_c]
                for part in range(hidden // width):
                    out[part * deep : (part + 1) * deep, :] = grad_in[
                        pl.ds(pl.multiple_of(head * deep, deep), deep),
                        part * width : (part + 1) * width,
                    ].astype(bfloat)
                block = grad_out[:, pl.ds(pl.multiple_of(head * wide, wide), wide)]
                if rest:
                    rest[0][...] = block.T.astype(bfloat)
                else:
                    out[hidden // width * deep :, :] = block.T.astype(bfloat)


def whole_call(kernel, out_shape, scratch=(), micros=1, in_specs=None, out_specs=None, aliases=None):
    specs = {}
    if in_specs is not None:
        specs["in_specs"] = in_specs
    if out_specs is not None:
        specs["out_specs"] = out_specs
    return pl.pallas_call(
        kernel,
        out_shape=out_shape,
        scratch_shapes=scratch,
        input_output_aliases=aliases or {},
        compiler_params=pltpu.CompilerParams(vmem_limit_bytes=VMEM_LIMIT),
        cost_estimate=pl.CostEstimate(
            flops=int(micros * SCALE), bytes_accessed=0, transcendentals=0
        ),
        **specs,
    )


class Grid:
    names = ("zh", "zl", "y", "x", "c")

    def __init__(self, mesh):
        experts, heads = mesh.shape["expert"], mesh.shape["head"]
        self.shape = (2, experts // 4, 2, heads // 2, 2)
        self.experts, self.heads = experts, heads
        self.total = experts * heads

    def size(self, name):
        return self.shape[self.names.index(name)]

    def coords(self, linear):
        out = []
        for extent in reversed(self.shape):
            out.append(linear % extent)
            linear = linear // extent
        return dict(zip(self.names, reversed(out)))

    def linear(self, coords):
        at = 0
        for name, extent in zip(self.names, self.shape):
            at = at * extent + coords[name] % extent
        return at

    def me(self, name):
        linear = lax.axis_index("expert") * self.heads + lax.axis_index("head")
        return self.coords(linear)[name]

    def send(self, value, target):
        pairs = [(i, self.linear(target(self.coords(i)))) for i in range(self.total)]
        return lax.ppermute(value, ("expert", "head"), pairs)

    def move(self, value, **by):
        return self.send(value, lambda at: {name: at[name] - by.get(name, 0) for name in at})

    def shift(self, value, name, by):
        return self.move(value, **{name: by})

    def exchange(self, value, name, *others):
        stride = self.linear({**dict.fromkeys(self.names, 0), name: 1}) // self.heads
        groups = [[at, at + stride] for at in range(self.experts) if at // stride % 2 == 0]
        both = jnp.broadcast_to(value[None], (2, *value.shape))
        both = lax.all_to_all(
            both, "expert", split_axis=0, concat_axis=0, tiled=True, axis_index_groups=groups
        )
        both = after(both, *others) if others else both
        return jnp.where(self.me(name) == 0, both[1], both[0])

    def gather(self, value, name, *others):
        extent, own = self.size(name), self.me(name)
        parts = [value] + [self.shift(value, name, by) for by in range(1, extent)]
        if others:
            parts[1] = after(parts[1], *others)
        if extent == 2:
            return jnp.where(own == 0, jnp.stack(parts), jnp.stack(parts[::-1]))
        return jnp.roll(jnp.stack(parts), own, axis=0)

    def scatter_sum(self, value, name, *waited):
        extent, own = self.size(name), self.me(name)
        if extent == 2:
            kept = jnp.where(own == 0, value[0], value[1])
            others = [self.shift(jnp.where(own == 0, value[1], value[0]), name, 1)]
        else:
            value = jnp.roll(value, -own, axis=0)
            kept = value[0]
            others = [self.shift(value[by], name, -by) for by in range(1, extent)]
        if waited:
            others[0] = after(others[0], *waited)
        total = kept.astype(single)
        for other in others:
            total = total + other.astype(single)
        return total.astype(value.dtype)


def after(value, *others):
    return lax.optimization_barrier((value, *others))[0]


def per_device(
    grid,
    tokens,
    segment_ids,
    task_ids,
    task_table,
    weight_qkv,
    weight_out,
    gain_one,
    gain_two,
    weight_router,
    weight_in,
    weight_hidden,
    cotangent,
):
    expert_count, head_count = grid.experts, grid.heads
    head_index = lax.axis_index("head")
    row_count, model_width = tokens.shape
    cap = 4 * row_count // expert_count
    deep, wide = weight_qkv.shape[1:]
    padded = -(-expert_count // 16) * 16

    pieces = jnp.concatenate([weight_qkv, weight_out.T[None]]).astype(bfloat)
    small = jnp.concatenate(
        [gain_one[None], gain_two[None], weight_router.T]
    ).astype(bfloat).reshape(-1)
    small_rows = -(-small.shape[0] // wide)
    small = jnp.pad(small, (0, small_rows * wide - small.shape[0])).reshape(small_rows, wide)
    packed = jnp.concatenate([pieces.reshape(4 * deep, wide), small])
    own_segments = lax.dynamic_slice_in_dim(segment_ids, head_index * row_count, row_count)
    shape = jax.ShapeDtypeStruct
    vmem, hbm = pl.BlockSpec(memory_space=pltpu.VMEM), pl.BlockSpec(memory_space=pl.ANY)
    smem = pl.BlockSpec(memory_space=pltpu.SMEM)
    table = jnp.pad(task_table.T, ((0, 16 - task_table.shape[1]), (0, 0))).astype(bfloat)
    hidden = weight_in.shape[2]
    deep_in = weight_in.shape[1]
    piece = shape((hidden // model_width * deep_in + weight_hidden.shape[1], model_width), bfloat)
    route_rows = padded * (2 * (row_count // model_width) + 2)
    first, second, route, own_piece, sent = whole_call(
        lambda *refs: routing_kernel(cap, *refs),
        [shape((1, row_count), jnp.int32)] * 2
        + [
            shape((padded, row_count), single),
            piece,
            shape((row_count + route_rows, model_width), bfloat),
        ],
        micros=3,
    )(own_segments[None], task_ids[None], table, weight_in, weight_hidden, cotangent)
    names = {name: grid.me(name) for name in grid.names}
    extent = grid.size("zl")
    offsets = [(dl, dy) for dl in range(extent) for dy in range(2)]
    offsets.sort(key=lambda by: by[0] * by[1] != 0)
    providers = len(offsets)

    def expert_of(zl, y, local):
        return ((names["zh"] + local) % 2 * extent + zl % extent) * 2 + y % 2

    def ints(*values):
        return jnp.concatenate([jnp.asarray(v, jnp.int32).reshape(-1) for v in values])

    targets = ints(
        *[expert_of(names["zl"] - dl, names["y"] - dy, k) for dl, dy in offsets for k in range(2)],
        names["c"],
    )
    parcel = shape((2 * cap + EXTRA, model_width), bfloat)
    packed = grid.gather(grid.gather(packed, "zh"), "zl")
    nearly = packed
    packed = grid.gather(packed, "y")
    smalls = packed.transpose(2, 1, 0, 3, 4).reshape(expert_count, -1)[:, 4 * deep * wide :]
    smalls = smalls[:, : (2 + expert_count) * deep].reshape(expert_count, 2 + expert_count, deep)
    smalls = smalls.transpose(1, 0, 2).reshape(2 + expert_count, model_width)
    gain1, gain2 = smalls[0:1].astype(single), smalls[1:2].astype(single)
    router = jnp.pad(smalls[2:], ((0, padded - expert_count), (0, 0)))
    packed = grid.gather(packed[..., : 4 * deep, :], "x")
    packed = packed.reshape(*packed.shape[:4], 4, deep, wide)
    if wide % LANES:
        packed = grid.gather(packed, "c").transpose(5, 4, 3, 2, 6, 1, 0, 7)
        packed = packed.reshape(4, model_width, model_width)
        weights = (packed, packed)
    else:
        weights = (packed, grid.shift(packed, "c", 1))

    segc = own_segments[:, None]
    starts = [min(max(at - SPAN, 0), row_count - WINDOW) for at in range(0, row_count, BLOCK)]
    segw = jnp.stack([own_segments[at : at + WINDOW] for at in starts])

    core = ints(names["c"])
    gate_rows = 2 * padded * (row_count // model_width)
    proj, attn, res, two_low, stat, gate, weights = whole_call(
        forward_kernel,
        [
            shape((3, row_count, model_width), bfloat),
            shape((row_count, model_width), bfloat),
            shape((row_count, model_width), single),
            shape((row_count + gate_rows, model_width), bfloat),
            shape((row_count, LANES), single),
            shape((padded, row_count), single),
            shape((4, model_width, model_width), bfloat),
        ],
        in_specs=[smem, vmem, hbm, hbm] + [vmem] * 7,
        out_specs=[hbm] * 5 + [vmem, hbm],
        scratch=[
            pltpu.VMEM((3, row_count, model_width), bfloat),
            pltpu.VMEM((row_count, model_width), bfloat),
            pltpu.VMEM((row_count, model_width), single),
            pltpu.VMEM((row_count + gate_rows, model_width), bfloat),
            pltpu.VMEM((row_count, LANES), single),
            pltpu.VMEM((4, model_width, model_width), bfloat),
            pltpu.SemaphoreType.DMA((2, head_count // 2 * expert_count)),
            pltpu.SemaphoreType.DMA((5, max(4, row_count // BLOCK))),
        ],
        micros=0.2,
    )(core, tokens, *weights, gain1, gain2, router, segc, segw, first, second)

    own_piece = after(own_piece, nearly)
    pieces = {(0, 0, 0): own_piece, (1, 0, 0): grid.exchange(own_piece, "zh")}
    for by_x in range(1, head_count // 2):
        pieces[0, by_x, 0] = grid.shift(own_piece, "x", by_x)
    own_experts = [expert_of(names["zl"], names["y"], local) for local in range(2)]
    sent = after(sent, nearly)
    cots = {(dl, 0): grid.move(sent, zl=dl) if dl else sent for dl in range(extent)}
    cots[0, 1] = grid.move(sent, y=1)
    pieces[1, 0, 0] = after(pieces[1, 0, 0], two_low)
    rows = {(dl, 0): grid.move(two_low, zl=dl) if dl else two_low for dl in range(extent)}
    rows[0, 1] = grid.move(two_low, y=1)
    for dl in range(1, extent):
        rows[dl, 1] = grid.move(two_low, zl=dl, y=1)
        cots[dl, 1] = grid.move(cots[dl, 0], y=1)
    for by_x in range(1, head_count // 2):
        piece_x = grid.shift(after(pieces[1, 0, 0], cots[0, 1]), "x", by_x)
        pieces[1, by_x, 0] = after(piece_x, cots[1, 0], rows[0, 1])
    for by_x in range(head_count // 2):
        for local in range(2):
            pieces[local, by_x, 1] = grid.shift(pieces[local, by_x, 0], "c", 1)
    piece_keys = [(k, bx, bc) for k in range(2) for bx in range(head_count // 2) for bc in range(2)]
    piece_list = [pieces[key] for key in piece_keys]

    groups = [[0, 1]] + [[at] for at in range(2, min(4, providers))]
    groups += [list(range(at, min(at + 3, providers))) for at in range(4, providers, 3)]
    save_tiles = sum(-(-len(group) * cap // TILE) for group in groups)
    save_shapes = [
        shape((2, save_tiles * TILE, cols), bfloat)
        for cols in (model_width, model_width, hidden, hidden)
    ]
    saved = []
    tiles_before = jnp.zeros((2,), jnp.int32)
    results = {}
    for group in groups:
        count = len(group)
        keys = [offsets[s] for s in group]
        inputs = [ints(names["x"], names["c"], *own_experts), tiles_before]
        inputs += [rows[key] for key in keys] + [cots[key] for key in keys]
        inputs += piece_list + saved
        before = 2 + 2 * count + len(piece_list)
        outs = whole_call(
            lambda *refs, count=count, new=not saved: expert_kernel(
                count, head_count, cap, row_count, padded, new, *refs
            ),
            save_shapes + [parcel] * (2 * count) + [shape((2,), jnp.int32)],
            in_specs=[smem, smem] + [hbm] * (2 * count + len(piece_list) + len(saved)),
            out_specs=[hbm] * (4 + 2 * count) + [smem],
            aliases={before + i: i for i in range(len(saved))},
            scratch=[
                pltpu.VMEM((2, model_width, hidden), bfloat),
                pltpu.VMEM((2, hidden, model_width), bfloat),
                pltpu.VMEM((count, row_count + gate_rows, model_width), bfloat),
                pltpu.VMEM((count, *sent.shape), bfloat),
                pltpu.VMEM((count, 2 * cap, model_width), bfloat),
                pltpu.VMEM((count, 2 * cap, model_width), bfloat),
                pltpu.VMEM((count, 2 * cap, 1), single),
                pltpu.VMEM((count, *parcel.shape), bfloat),
                pltpu.VMEM((count, *parcel.shape), bfloat),
                pltpu.VMEM((count, 8, cap), single),
                pltpu.VMEM((TILE, model_width), bfloat),
                pltpu.VMEM((TILE, model_width), bfloat),
                pltpu.VMEM((TILE, 1), single),
                pltpu.VMEM((2, TILE, model_width), bfloat),
                pltpu.VMEM((2, TILE, model_width), bfloat),
                pltpu.VMEM((2, TILE, hidden), bfloat),
                pltpu.VMEM((2, TILE, hidden), bfloat),
                pltpu.SMEM((2, count * cap // HALF + 1), jnp.int32),
                pltpu.SemaphoreType.DMA((2, head_count * (hidden // model_width + 1))),
                pltpu.SemaphoreType.DMA((2, count)),
                pltpu.SemaphoreType.DMA((2, 4)),
                pltpu.SemaphoreType.DMA((2, count)),
            ],
            micros=16 if saved else 58,
        )(*inputs)
        if not saved:
            for dl in range(1, extent):
                rows[dl, 0] = after(rows[dl, 0], outs[0])
        saved, tiles_before = list(outs[:4]), outs[-1]
        for i, s in enumerate(group):
            results[s] = [outs[4 + i], outs[4 + count + i]]
    out_parcels, grad_parcels = [], []
    for s, (dl, dy) in enumerate(offsets):
        out_part, grad_part = results[s]
        if dl and dy:
            grad_part = after(grad_part, *grad_parcels[1:])
        if dl or dy:
            grad_part = grid.move(grad_part, zl=-dl, y=-dy)
            if dl:
                out_part = after(out_part, saved[0])
            if not (dl and dy):
                out_part = grid.move(out_part, zl=-dl, y=-dy)
        out_parcels.append(out_part)
        grad_parcels.append(grad_part)
    waited = []
    halves = [
        shape((hidden // model_width * deep_in, model_width), bfloat),
        shape((weight_hidden.shape[1], model_width), bfloat),
    ]
    done = whole_call(
        lambda *refs: weight_kernel(head_count, len(waited), *refs),
        [s for key in piece_keys for s in (halves if all(key) else [piece])],
        in_specs=[smem, smem] + [hbm] * (4 + len(waited)),
        scratch=[
            pltpu.VMEM((model_width, hidden), single),
            pltpu.VMEM((model_width, hidden), single),
            pltpu.VMEM((2, TILE, model_width), bfloat),
            pltpu.VMEM((2, TILE, model_width), bfloat),
            pltpu.VMEM((2, TILE, hidden), bfloat),
            pltpu.VMEM((2, TILE, hidden), bfloat),
            pltpu.SemaphoreType.DMA((2, 4)),
        ],
        micros=1,
    )(ints(names["x"], names["c"]), tiles_before, *saved, *waited)
    done, grad_parcels, out_parcels[1] = lax.optimization_barrier(
        (done, grad_parcels, out_parcels[1])
    )
    out_parcels = [
        grid.move(after(value, done[0]), zl=-dl, y=-dy) if dl and dy else value
        for value, (dl, dy) in zip(out_parcels, offsets)
    ]
    done = list(done)
    grads = {
        key: [done.pop(0) for _ in halves] if all(key) else done.pop(0) for key in piece_keys
    }

    def add(kept, other):
        return (kept.astype(single) + other.astype(single)).astype(bfloat)

    crossed = {}
    for key in piece_keys:
        if key[2] == 0:
            other = grads[key[0], key[1], 1]
            parts = other if isinstance(other, list) else [other]
            parts = [grid.shift(part, "c", -1) for part in parts]
            crossed[key] = jnp.concatenate(parts) if len(parts) > 1 else parts[0]
    for by_x in range(1, head_count // 2):
        grads[1, by_x, 0] = add(grads[1, by_x, 0], crossed.pop((1, by_x, 0)))
    waited = []
    output = whole_call(
        lambda *refs: output_kernel(providers, cap, *refs),
        shape((row_count, model_width), bfloat),
        in_specs=[smem] + [vmem] * (3 + providers),
        micros=8,
    )(targets, res, gate, route, *out_parcels)

    grad_res, grad_heads, grad_out, grad_gain2, grad_router = whole_call(
        lambda *refs: middle_kernel(providers, cap, len(waited), *refs),
        (
            shape((row_count, model_width), single),
            shape((row_count, model_width), bfloat),
            shape((model_width, model_width), bfloat),
            shape((1, model_width), single),
            shape((padded, model_width), single),
        ),
        in_specs=[smem] + [hbm] * 5 + [vmem] * 4 + [hbm] * (providers + len(waited)),
        out_specs=[hbm] * 2 + [vmem] * 3,
        scratch=[
            pltpu.VMEM((padded, row_count), single),
            pltpu.VMEM((row_count, model_width), bfloat),
            pltpu.VMEM((row_count, model_width), single),
            pltpu.VMEM((row_count, model_width), bfloat),
            pltpu.VMEM((row_count, model_width), bfloat),
            pltpu.VMEM((row_count, model_width), single),
            pltpu.VMEM((row_count, model_width), bfloat),
            pltpu.VMEM((row_count, model_width), bfloat),
            pltpu.VMEM((model_width, model_width), bfloat),
            pltpu.VMEM((providers, *parcel.shape), bfloat),
            pltpu.SemaphoreType.DMA((providers + 5,)),
            pltpu.SemaphoreType.DMA((2, row_count // CHUNK)),
        ],
        micros=4,
    )(
        targets, cotangent, res, two_low, attn, weights, gain2, router, gate, route,
        *grad_parcels, *waited,
    )
    for key, other in crossed.items():
        grads[key] = add(grads[key], after(other, grad_gain2))
    for by_x in range(1, head_count // 2):
        other = after(grid.shift(grads[1, by_x, 0], "x", -by_x), grad_gain2)
        grads[1, 0, 0] = add(grads[1, 0, 0], other)
    grad_res = after(grad_res, grads[1, 0, 0], grads[0, 1, 0], *out_parcels[2:-1])
    columns = model_width if wide % LANES else model_width // 2
    grad_tokens, grad_own, other_top, other_rest, grad_gain1 = whole_call(
        lambda *refs: backward_kernel(head_count, *refs),
        (
            shape((row_count, model_width), single),
            shape((4, model_width, columns), bfloat),
            shape((2, model_width, columns), bfloat),
            shape((2, model_width, columns), bfloat),
            shape((1, model_width), single),
        ),
        in_specs=[smem] + [vmem] * 3 + [hbm] * 7,
        out_specs=[hbm] + [vmem] * 4,
        scratch=[
            pltpu.VMEM((3, row_count, model_width), bfloat),
            pltpu.VMEM((row_count, model_width), single),
            pltpu.VMEM((row_count, model_width), single),
            pltpu.VMEM((row_count, model_width), bfloat),
            pltpu.VMEM((4, model_width, model_width), bfloat),
            pltpu.VMEM((3, row_count, model_width), bfloat),
            pltpu.VMEM((row_count, model_width), bfloat),
            pltpu.VMEM((row_count, LANES), single),
            pltpu.VMEM((row_count, model_width), bfloat),
            pltpu.VMEM((row_count, model_width), single),
            pltpu.VMEM((3, model_width, model_width), bfloat),
            pltpu.VMEM((row_count, model_width), single),
            pltpu.SemaphoreType.DMA((7,)),
            pltpu.SemaphoreType.DMA((row_count // CHUNK,)),
        ],
        micros=1,
    )(
        core, gain1, segc, segw, proj, grad_heads, stat, tokens, grad_res, weights, grad_out,
    )

    for by_x in range(1, head_count // 2):
        other = after(grid.shift(grads[0, by_x, 0], "x", -by_x), grad_tokens)
        grads[0, 0, 0] = add(grads[0, 0, 0], other)
    other_top = after(other_top, *out_parcels[3:])
    smalls = jnp.concatenate([grad_gain1, grad_gain2, grad_router[:expert_count]]).astype(bfloat)
    if wide % LANES:
        packed = grad_own.reshape(4, model_width, -1, 2, wide).transpose(3, 0, 1, 2, 4)
        packed = grid.scatter_sum(packed, "c").reshape(4, model_width, -1)
    else:
        other = [grid.shift(v, "c", 1) for v in (other_top, other_rest)]
        packed = add(grad_own, jnp.concatenate(other))
    packed = packed.reshape(4, model_width, -1, wide).transpose(2, 0, 1, 3)
    packed = grid.scatter_sum(after(packed, grads[0, 0, 0]), "x", output)
    grad_piece = grads[0, 0, 0].astype(single) + grid.exchange(
        grads[1, 0, 0], "zh", packed
    ).astype(single)
    grad_in_own = grad_piece[: hidden // model_width * deep_in]
    grad_in_own = grad_in_own.reshape(-1, deep_in, model_width).transpose(1, 0, 2)
    grad_in_own = grad_in_own.reshape(1, deep_in, hidden)
    grad_hidden_own = grad_piece[hidden // model_width * deep_in :][None]
    for name in ("c", "x"):
        total = smalls.astype(single)
        for by in range(1, grid.size(name)):
            total = total + grid.shift(smalls, name, by).astype(single)
        smalls = total.astype(bfloat)
    smalls = smalls.reshape(2 + expert_count, expert_count, deep).transpose(1, 0, 2)
    smalls = smalls.reshape(expert_count, -1)
    smalls = jnp.pad(smalls, ((0, 0), (0, small_rows * wide - smalls.shape[1])))
    packed = packed.reshape(4, expert_count, deep, wide).transpose(1, 0, 2, 3)
    packed = packed.reshape(expert_count, 4 * deep, wide)
    packed = jnp.concatenate([packed, smalls.reshape(expert_count, small_rows, wide)], axis=1)
    packed = packed.reshape(*grid.shape[:3], 4 * deep + small_rows, wide).transpose(2, 1, 0, 3, 4)
    packed = after(packed, grad_piece)
    for name in ("y", "zl", "zh"):
        packed = grid.scatter_sum(packed, name)
    pieces = packed[: 4 * deep].reshape(4, deep, wide).astype(single)
    smalls = packed[4 * deep :].reshape(-1)[: (2 + expert_count) * deep].astype(single)
    smalls = smalls.reshape(2 + expert_count, deep)
    return (
        output,
        grad_tokens,
        pieces[:3],
        pieces[3].T,
        smalls[0],
        smalls[1],
        smalls[2:].T,
        grad_in_own,
        grad_hidden_own,
    )


def solution(mesh):
    grid = Grid(mesh)
    placed = (
        P(("expert", "head"), None),
        P("expert"),
        P(),
        P(),
        P(None, "expert", "head"),
        P("head", "expert"),
        P("expert"),
        P("expert"),
        P("expert", None),
        P("expert", "head", None),
        P("expert", "head", None),
        P(("expert", "head"), None),
    )

    def step(*arrays):
        return per_device(grid, *arrays)

    return jax.shard_map(
        step,
        mesh=mesh,
        in_specs=placed,
        out_specs=(
            P(("expert", "head"), None),
            P(("expert", "head"), None),
            P(None, "expert", "head"),
            P("head", "expert"),
            P("expert"),
            P("expert"),
            P("expert", None),
            P("expert", "head", None),
            P("expert", "head", None),
        ),
        check_vma=False,
    )
```

```python
import jax
import jax.numpy as jnp
from jax import lax
from jax.experimental import pallas as pl
from jax.experimental.pallas import tpu as pltpu
from jax.sharding import PartitionSpec as P

HDIM = 64
PACK = 1024
SPAN = 64
BLOCK = 128
WINDOW = BLOCK + 2 * SPAN
CHUNK = 256
LANES = 128
TILE = 256
HALF = 64
EXTRA = 16
PART = 256
ABSENT = -1e6
SCALE = 1153e6 / 8

EPSILON = 1e-05
NEGATIVE = -1e30

bfloat = jnp.bfloat16
single = jnp.float32
VMEM_LIMIT = 56 * 1024 * 1024


def dot_nn(a, b):
    return lax.dot_general(a, b, (((1,), (0,)), ((), ())), preferred_element_type=single)


def dot_nt(a, b):
    return lax.dot_general(a, b, (((1,), (1,)), ((), ())), preferred_element_type=single)


def dot_tn(a, b):
    return lax.dot_general(a, b, (((0,), (0,)), ((), ())), preferred_element_type=single)


def normalise(values):
    centered = values - jnp.mean(values, axis=-1, keepdims=True)
    inverse = lax.rsqrt(jnp.mean(centered * centered, axis=-1, keepdims=True) + EPSILON)
    return centered * inverse, inverse


def norm_pull(grad_normed, scaled, inverse, gain):
    weighted = grad_normed * gain
    return inverse * (
        weighted
        - jnp.mean(weighted, axis=-1, keepdims=True)
        - scaled * jnp.mean(weighted * scaled, axis=-1, keepdims=True)
    )


def split_heads(pair, first_half):
    zero = jnp.zeros_like(pair)
    return jnp.concatenate(
        [jnp.where(first_half, pair, zero), jnp.where(first_half, zero, pair)], axis=0
    )


def window_start(block, rows):
    return pl.multiple_of(jnp.clip(block * BLOCK - SPAN, 0, rows - WINDOW), SPAN)


def fetch_weights(core, own, other, weights, sem):
    copies = []
    if own.shape == weights.shape:
        copies = [pltpu.make_async_copy(own, weights, sem.at[0, 0])]
    else:
        parts_x, parts_y, parts_zl, parts_zh, _, deep, wide = own.shape
        places = [
            (x, y, zl, zh)
            for x in range(parts_x)
            for y in range(parts_y)
            for zl in range(parts_zl)
            for zh in range(parts_zh)
        ]
        for at, (x, y, zl, zh) in enumerate(places):
            row = ((zh * parts_zl + zl) * parts_y + y) * deep
            for i, (ref, half) in enumerate(((own, core), (other, 1 - core))):
                start = pl.multiple_of((2 * x + half) * wide, LANES)
                copies.append(
                    pltpu.make_async_copy(
                        ref.at[x, y, zl, zh],
                        weights.at[:, pl.ds(row, deep), pl.ds(start, wide)],
                        sem.at[i, at],
                    )
                )
    for copy in copies:
        copy.start()
    for copy in copies:
        copy.wait()


def forward_kernel(
    meta, tok, weights_own, weights_other, gain1, gain2, router, segc, segw, first, second,
    proj_out, attn_out, res_out, two_out, stat_out, gate, weights_out,
    proj, attn, res, two, stat, weights, sem, out_sem,
):
    rows, width = tok.shape
    fetch_weights(meta[0], weights_own, weights_other, weights, sem)
    wqkv, wot = weights, weights.at[3]
    leaving = [pltpu.make_async_copy(weights, weights_out, out_sem.at[0, 0])]
    leaving[0].start()

    def project(step, carry):
        at = pl.ds(pl.multiple_of(step * CHUNK, CHUNK), CHUNK)
        scaled, _ = normalise(tok[at, :].astype(single))
        low = (scaled * gain1[...]).astype(bfloat)
        for part in range(3):
            proj[part, at, :] = dot_nn(low, wqkv[part]).astype(bfloat)
        return carry

    lax.fori_loop(0, rows // CHUNK, project, 0)
    leaving.append(pltpu.make_async_copy(proj, proj_out, out_sem.at[0, 1]))
    leaving[1].start()

    def block_copies(block):
        at = pl.ds(pl.multiple_of(block * BLOCK, BLOCK), BLOCK)
        return [
            pltpu.make_async_copy(held.at[at, :], out.at[at, :], out_sem.at[1 + i, block])
            for i, (held, out) in enumerate(
                ((attn, attn_out), (res, res_out), (two, two_out), (stat, stat_out))
            )
        ]

    lane = lax.broadcasted_iota(jnp.int32, (BLOCK, LANES), 1)
    first_half = lane < HDIM
    expert = lax.broadcasted_iota(jnp.int32, (router.shape[0], BLOCK), 0)

    def attend(block, carry):
        q_at = pl.ds(pl.multiple_of(block * BLOCK, BLOCK), BLOCK)
        k_at = pl.ds(window_start(block, rows), WINDOW)
        same = (segc[q_at, :] == segw[pl.ds(block, 1), :])[None]
        totals = jnp.zeros((BLOCK, LANES), single)
        for pair in range(width // LANES):
            cols = slice(pair * LANES, (pair + 1) * LANES)
            queries = split_heads(proj[0, q_at, cols] * HDIM**-0.5, first_half)
            scores = dot_nt(queries, proj[1, k_at, cols]).reshape(2, BLOCK, WINDOW)
            scores = jnp.where(same, scores, NEGATIVE)
            peak = jnp.max(scores, axis=-1, keepdims=True)
            exponent = jnp.exp(scores - peak)
            total = jnp.sum(exponent, axis=-1, keepdims=True)
            probs = (exponent * (1.0 / total)).astype(bfloat).reshape(2 * BLOCK, WINDOW)
            out = dot_nn(probs, proj[2, k_at, cols])
            attn[q_at, cols] = jnp.where(first_half, out[:BLOCK], out[BLOCK:]).astype(bfloat)
            log_total = peak + jnp.log(total)
            for half in range(2):
                totals = jnp.where(lane == 2 * pair + half, log_total[half], totals)
        stat[q_at, :] = totals
        residual = tok[q_at, :].astype(single) + dot_nt(attn[q_at, :], wot[...])
        res[q_at, :] = residual
        scaled, _ = normalise(residual)
        low = (scaled * gain2[...]).astype(bfloat)
        two[q_at, :] = low
        logits = dot_nt(router[...], low)
        mark0 = first[:, q_at] == expert
        mark1 = second[:, q_at] == expert
        logit0 = jnp.sum(jnp.where(mark0, logits, 0.0), axis=0, keepdims=True)
        logit1 = jnp.sum(jnp.where(mark1, logits, 0.0), axis=0, keepdims=True)
        top = jnp.maximum(logit0, logit1)
        part0, part1 = jnp.exp(logit0 - top), jnp.exp(logit1 - top)
        scale = 1.0 / (part0 + part1)
        gate[:, q_at] = jnp.where(mark0, part0 * scale, jnp.where(mark1, part1 * scale, 0.0))
        for copy in block_copies(block):
            copy.start()
        return carry

    lax.fori_loop(0, rows // BLOCK, attend, 0)
    count = gate.shape[0]
    at = rows
    for part in split_two(gate[...]):
        for start in range(0, rows, width):
            two[at : at + count, :] = part[:, start : start + width]
            at += count
    rest = pl.ds(rows, two.shape[0] - rows)
    leaving.append(
        pltpu.make_async_copy(two.at[rest, :], two_out.at[rest, :], out_sem.at[0, 2])
    )
    leaving[2].start()
    for copy in leaving:
        copy.wait()

    def settle(block, carry):
        for copy in block_copies(block):
            copy.wait()
        return carry

    lax.fori_loop(0, rows // BLOCK, settle, 0)


def split_two(values):
    high = values.astype(bfloat)
    return high, (values - high.astype(single)).astype(bfloat)


def pack_rows(rows):
    at = lax.broadcasted_iota(jnp.int32, (EXTRA, rows.shape[1]), 0)
    out = jnp.zeros((EXTRA, rows.shape[1]), single)
    for local in range(2):
        high = rows[local : local + 1, :].astype(bfloat).astype(single)
        out = jnp.where(at == 2 * local, high, out)
        out = jnp.where(at == 2 * local + 1, rows[local : local + 1, :] - high, out)
    return out.astype(bfloat)


def unpack_row(packed, local):
    packed = packed.astype(single)
    return packed[2 * local : 2 * local + 1, :] + packed[2 * local + 1 : 2 * local + 2, :]


def routing_kernel(
    cap, segments, tasks, table, weight_in, weight_hidden, cot,
    first, second, route, piece, sent,
):
    rows = segments.shape[1]
    deep, hidden = weight_in.shape[1:]
    width = piece.shape[1]
    for part in range(hidden // width):
        piece[part * deep : (part + 1) * deep, :] = weight_in[
            0, :, part * width : (part + 1) * width
        ].astype(bfloat)
    piece[hidden // width * deep :, :] = weight_hidden[0].astype(bfloat)
    names = lax.broadcasted_iota(jnp.int32, (table.shape[1], tasks.shape[1]), 0)
    experts = dot_nn(table[...], jnp.where(names == tasks[...], 1.0, 0.0).astype(bfloat))
    experts = experts.astype(bfloat)
    chosen = jnp.zeros((table.shape[0], rows), single)
    for start in range(0, tasks.shape[1], 1024):
        size = min(1024, tasks.shape[1] - start)
        at = lax.broadcasted_iota(jnp.int32, (size, rows), 0) + start
        ones = jnp.where(at == segments[...], 1.0, 0.0).astype(bfloat)
        chosen = chosen + dot_nn(experts[:, start : start + size], ones)
    zero, one = chosen[0:1, :], chosen[1:2, :]
    first[...] = zero.astype(jnp.int32)
    second[...] = one.astype(jnp.int32)
    which = lax.broadcasted_iota(jnp.int32, route.shape, 0).astype(single)
    is_first, is_second = which == zero, which == one
    marks = jnp.where(is_first | is_second, 1.0, 0.0)
    earlier = lax.broadcasted_iota(jnp.int32, (rows, rows), 0) < lax.broadcasted_iota(
        jnp.int32, (rows, rows), 1
    )
    places = dot_nn(marks.astype(bfloat), jnp.where(earlier, 1.0, 0.0).astype(bfloat))
    inside = (marks > 0.5) & (places < cap)
    slots = jnp.where(inside, places, ABSENT)
    route[...] = slots
    total = jnp.sum(jnp.where(inside, 1.0, 0.0), axis=1, keepdims=True)
    total = jnp.broadcast_to(total, (route.shape[0], width))
    sent[:rows, :] = cot[...]
    at = rows
    for part in range(2):
        for start in range(0, rows, width):
            sent[at : at + route.shape[0], :] = sixteens(slots[:, start : start + width])[part]
            at += route.shape[0]
    for part in range(2):
        sent[at : at + route.shape[0], :] = sixteens(total)[part]
        at += route.shape[0]


def sixteens(values):
    high = jnp.floor(values * 0.0625) * 16.0
    high = jnp.where(values < 0.0, values, high)
    return high.astype(bfloat), jnp.where(values < 0.0, 0.0, values - high).astype(bfloat)


def output_kernel(providers, cap, meta, res, gate, slots, *refs):
    parcels, out = refs[:providers], refs[providers]
    for step in range(res.shape[0] // CHUNK):
        at = slice(step * CHUNK, (step + 1) * CHUNK)
        out[at, :] = (res[at, :] + returned_rows(parcels, cap, meta, gate, slots, at)).astype(bfloat)


def returned_rows(parcels, cap, meta, gate, slots, at):
    total = 0.0
    for provider, parcel in enumerate(parcels):
        for local in range(2):
            chosen = pl.ds(meta[2 * provider + local], 1)
            ones = onehot(slots[chosen, at], 0, cap, gate[chosen, at])
            total = total + dot_tn(ones, parcel[local * cap : (local + 1) * cap, :])
    return total


def middle_kernel(
    providers, cap, waited, meta,
    cot_in, res_in, two_in, attn_in, weights_in, gain2, router, gate, slots,
    *refs,
):
    parcels = refs[:providers]
    (
        res_left, heads_left, grad_out, grad_gain2, grad_router,
        products, grad_attn, grad_res, grad_heads, cot, res, two, attn, wot, parcel_bufs, sem, out_sem,
    ) = refs[providers + waited :]
    rows, width = cot.shape
    two_rows = two_in.at[pl.ds(0, rows), :]
    arriving = [
        pltpu.make_async_copy(given, held, sem.at[i])
        for i, (given, held) in enumerate(
            [(parcel, parcel_bufs.at[at]) for at, parcel in enumerate(parcels)]
            + [(res_in, res), (cot_in, cot), (weights_in.at[3], wot), (two_rows, two), (attn_in, attn)]
        )
    ]
    for copy in arriving:
        copy.start()
    parcels = [parcel_bufs.at[at] for at in range(providers)]
    for copy in arriving[:providers]:
        copy.wait()
    products[...] = jnp.zeros_like(products)
    for provider in range(providers):
        for local in range(2):
            chosen = meta[2 * provider + local]
            ones = onehot(slots[pl.ds(chosen, 1), :], 0, cap)
            moved = dot_nn(parcels[provider][2 * cap :, :cap], ones)
            products[pl.ds(chosen, 1), :] = unpack_row(moved, local)
    gates = gate[...]
    inner_products = products[...]
    grad_logits = gates * (
        inner_products - jnp.sum(gates * inner_products, axis=0, keepdims=True)
    )
    grad_logits = jnp.concatenate(split_two(grad_logits), axis=0)
    router_twice = jnp.concatenate([router[...], router[...]], axis=0)
    count = router.shape[0]
    grad_gain2[...] = jnp.zeros_like(grad_gain2)
    for copy in arriving[providers : providers + 3]:
        copy.wait()
    leaving = []
    for step in range(rows // CHUNK):
        at = slice(step * CHUNK, (step + 1) * CHUNK)
        scaled, inverse = normalise(res[at, :])
        grad_normed = dot_tn(grad_logits[:, at], router_twice)
        grad_normed = grad_normed + returned_rows(parcels, cap, meta, gate, slots, at)
        grad_gain2[...] += jnp.sum(grad_normed * scaled, axis=0, keepdims=True)
        grad_row = cot[at, :].astype(single) + norm_pull(grad_normed, scaled, inverse, gain2[...])
        grad_res[at, :] = grad_row
        low = grad_row.astype(bfloat)
        grad_attn[at, :] = low
        grad_heads[at, :] = dot_nn(low, wot[...]).astype(bfloat)
        part = pl.ds(step * CHUNK, CHUNK)
        for i, (held, out) in enumerate(((grad_res, res_left), (grad_heads, heads_left))):
            leaving.append(
                pltpu.make_async_copy(held.at[part, :], out.at[part, :], out_sem.at[i, step])
            )
            leaving[-1].start()
    for copy in arriving[providers + 3 :]:
        copy.wait()
    routed = dot_nn(grad_logits, two[...])
    grad_router[...] = routed[:count] + routed[count:]
    grad_out[...] = dot_tn(grad_attn[...], attn[...]).astype(bfloat)
    for copy in leaving:
        copy.wait()


def backward_kernel(
    heads, core, gain1, segc, segw,
    proj_in, heads_in, stat_in, tok_in, res_in, weights_in, out_in,
    tok_left, grad_own, other_top, other_rest, grad_gain1,
    grad_proj, grad_key, grad_value, normed, grad_w,
    proj, grad_heads, stat, tok, grad_res, wqkv, grad_tok, sem, out_sem,
):
    rows, width = tok.shape
    arriving = [
        pltpu.make_async_copy(given, held, sem.at[i])
        for i, (given, held) in enumerate(
            (
                (proj_in, proj), (heads_in, grad_heads), (stat_in, stat), (tok_in, tok),
                (res_in, grad_res), (weights_in.at[pl.ds(0, 3)], wqkv), (out_in, grad_w.at[3]),
            )
        )
    ]
    for copy in arriving:
        copy.start()
    grad_gain1[...] = jnp.zeros_like(grad_gain1)
    grad_key[...] = jnp.zeros_like(grad_key)
    grad_value[...] = jnp.zeros_like(grad_value)
    for copy in arriving[:3]:
        copy.wait()
    lane = lax.broadcasted_iota(jnp.int32, (BLOCK, LANES), 1)
    first_half = lane < HDIM

    def attend(block, carry):
        q_at = pl.ds(pl.multiple_of(block * BLOCK, BLOCK), BLOCK)
        k_at = pl.ds(window_start(block, rows), WINDOW)
        same = (segc[q_at, :] == segw[pl.ds(block, 1), :])[None]
        totals = stat[q_at, :]
        for pair in range(width // LANES):
            cols = slice(pair * LANES, (pair + 1) * LANES)
            queries = split_heads(proj[0, q_at, cols] * HDIM**-0.5, first_half)
            keys_block = proj[1, k_at, cols]
            scores = dot_nt(queries, keys_block).reshape(2, BLOCK, WINDOW)
            scores = jnp.where(same, scores, NEGATIVE)
            log_total = jnp.stack(
                [totals[:, 2 * pair : 2 * pair + 1], totals[:, 2 * pair + 1 : 2 * pair + 2]]
            )
            probs = jnp.exp(scores - log_total).reshape(2 * BLOCK, WINDOW)
            heads_low = split_heads(grad_heads[q_at, cols], first_half)
            grad_probs = dot_nt(heads_low, proj[2, k_at, cols])
            delta = jnp.sum(probs * grad_probs, axis=-1, keepdims=True)
            grad_scores = (probs * (grad_probs - delta)).astype(bfloat)
            grad_query = dot_nn(grad_scores, keys_block) * HDIM**-0.5
            grad_proj[0, q_at, cols] = jnp.where(
                first_half, grad_query[:BLOCK], grad_query[BLOCK:]
            ).astype(bfloat)
            grad_key[k_at, cols] += dot_tn(grad_scores, queries)
            grad_value[k_at, cols] += dot_tn(probs.astype(bfloat), heads_low)
        return carry

    lax.fori_loop(0, rows // BLOCK, attend, 0)
    for copy in arriving[3:]:
        copy.wait()
    leaving = []
    for step in range(rows // CHUNK):
        at = slice(step * CHUNK, (step + 1) * CHUNK)
        grad_proj[1, at, :] = grad_key[at, :].astype(bfloat)
        grad_proj[2, at, :] = grad_value[at, :].astype(bfloat)
        grad_normed = dot_nt(grad_proj[0, at, :], wqkv[0])
        for part in (1, 2):
            grad_normed += dot_nt(grad_proj[part, at, :], wqkv[part])
        scaled, inverse = normalise(tok[at, :].astype(single))
        normed[at, :] = (scaled * gain1[...]).astype(bfloat)
        grad_gain1[...] += jnp.sum(grad_normed * scaled, axis=0, keepdims=True)
        grad_tok[at, :] = grad_res[at, :] + norm_pull(grad_normed, scaled, inverse, gain1[...])
        part = pl.ds(step * CHUNK, CHUNK)
        leaving.append(
            pltpu.make_async_copy(grad_tok.at[part, :], tok_left.at[part, :], out_sem.at[step])
        )
        leaving[-1].start()
    for part in range(3):
        grad_w[part] = dot_tn(normed[...], grad_proj[part]).astype(bfloat)
    if grad_own.shape == grad_w.shape:
        grad_own[...] = grad_w[...]
        other_top[...] = grad_w[:2]
        other_rest[...] = grad_w[2:]
    else:
        wide = width // heads
        for by in range(heads // 2):
            cols = slice(by * wide, (by + 1) * wide)
            start = pl.multiple_of((2 * by + core[0]) * wide, LANES)
            grad_own[:, :, cols] = grad_w[:, :, pl.ds(start, wide)]
            start = pl.multiple_of((2 * by + 1 - core[0]) * wide, LANES)
            other_top[:, :, cols] = grad_w[:2, :, pl.ds(start, wide)]
            other_rest[:, :, cols] = grad_w[2:, :, pl.ds(start, wide)]
    for copy in leaving:
        copy.wait()


def onehot(slots, base, rows, marks=1.0):
    places = lax.broadcasted_iota(jnp.int32, (rows, slots.shape[1]), 0).astype(single)
    return jnp.where(places == slots - base, marks, 0.0).astype(bfloat)


def gelu_both(values):
    bent = values * (0.7978845608028654 + 0.035677408136300125 * (values * values))
    half = 0.5 * jnp.tanh(bent) + 0.5
    steep = 6.0 * bent - 3.1915382432114616 * values
    return values * half, half * (1.0 + (1.0 - half) * steep)


def expert_kernel(work, heads, cap, tokens, count, fresh, first, meta, before, *refs):
    refs = list(refs)
    sources = len(work)
    needed = sorted({local for locals_of in work for local in locals_of})

    def take(count):
        taken = refs[:count]
        del refs[:count]
        return taken

    rows_in, grads_in = take(sources), take(sources)
    carried = [] if fresh else take(2)
    pieces = take(len(needed) * heads)
    if not first:
        take(4)
    saved = take(4)
    outs, grads = take(sources), take(sources)
    (now,) = take(1)
    (
        win, wout, row_all, grad_all, row_buf, grad_buf, gate_buf,
        out_buf, copy_buf, product_buf, now_x, now_g, now_gate,
        st_x, st_g, st_act, st_pre, table, w_sem, in_sem, s_sem, out_sem,
    ) = refs
    width = row_buf.shape[2]
    hidden = wout.shape[1]
    deep, wide = width // heads, hidden // heads
    head_x, head_c = meta[0], meta[1]
    staged = (st_x, st_g, st_act, st_pre)

    def weight_copies(local):
        at = 0
        for by_x in range(heads // 2):
            for by_c in range(2):
                head = lax.rem(head_x + by_x, heads // 2) * 2 + lax.rem(head_c + by_c, 2)
                piece = pieces[(needed.index(local) * (heads // 2) + by_x) * 2 + by_c]
                for part in range(hidden // width):
                    yield pltpu.make_async_copy(
                        piece.at[pl.ds(part * deep, deep), :],
                        win.at[
                            local,
                            pl.ds(pl.multiple_of(head * deep, deep), deep),
                            pl.ds(part * width, width),
                        ],
                        w_sem.at[local, at],
                    )
                    at += 1
                yield pltpu.make_async_copy(
                    piece.at[pl.ds(hidden // width * deep, wide), :],
                    wout.at[local, pl.ds(pl.multiple_of(head * wide, wide), wide), :],
                    w_sem.at[local, at],
                )
                at += 1

    def source_copies():
        for source in range(sources):
            for i, (given, held) in enumerate(((rows_in, row_all), (grads_in, grad_all))):
                yield pltpu.make_async_copy(given[source], held.at[source], in_sem.at[i, source])

    for copy in source_copies():
        copy.start()
    for local in needed:
        for copy in weight_copies(local):
            copy.start()
    carry_copies = [
        pltpu.make_async_copy(given, held.at[0], out_sem.at[i, 0])
        for i, (given, held) in enumerate(zip(carried, (out_buf, copy_buf)))
    ]
    for copy in carry_copies:
        copy.start()
    for source in range(0 if fresh else 1, sources):
        out_buf[source] = jnp.zeros_like(out_buf[source])
        copy_buf[source] = jnp.zeros_like(copy_buf[source])
    product_buf[...] = jnp.zeros_like(product_buf)

    def save_copies(slot, local, tile):
        at = pl.ds(pl.multiple_of(tile * TILE, TILE), TILE)
        return [
            pltpu.make_async_copy(stage.at[slot], save.at[local, at, :], s_sem.at[slot, i])
            for i, (stage, save) in enumerate(zip(staged, saved))
        ]

    eye = lax.broadcasted_iota(jnp.int32, (HALF, HALF), 0) == lax.broadcasted_iota(
        jnp.int32, (HALF, HALF), 1
    )
    for copy in source_copies():
        copy.wait()
    step_rows = min(TILE, cap)
    which = lax.broadcasted_iota(jnp.int32, (count, 1), 0)
    numbers, halves = {}, []
    for local in range(2):
        number = 0
        for source in range(sources):
            if local not in work[source]:
                continue
            at = grad_all.shape[1] - 2 * count
            total = grad_all[source, at : at + count, :LANES].astype(single)
            total = total + grad_all[source, at + count :, :LANES].astype(single)
            total = jnp.max(jnp.where(which == meta[2 + local], total, 0.0)).astype(jnp.int32)
            numbers[source, local] = total
            for half in range(cap // HALF):
                table[local, number] = source * (cap // HALF) + half
                number = number + jnp.where(total > half * HALF, 1, 0)
        halves.append(number)
        now[local] = before[local] + (number + TILE // HALF - 1) // (TILE // HALF)
    places = lax.broadcasted_iota(jnp.int32, (step_rows, tokens), 0).astype(single)
    for source in range(sources):
        for local in work[source]:
            expert = meta[2 + local]

            def by_token(ref):
                row = []
                for part in range(tokens // width):
                    parts = [
                        ref[source, pl.ds(tokens + (i * (tokens // width) + part) * count, count), :]
                        for i in range(2)
                    ]
                    both = parts[0].astype(single) + parts[1].astype(single)
                    both = jnp.where(which == expert, both, 0.0)
                    row.append(jnp.sum(both, axis=0, keepdims=True))
                return jnp.concatenate(row, axis=1)

            gate_row, slot_row = by_token(row_all), by_token(grad_all)
            for step in range(cap // step_rows):

                @pl.when(numbers[source, local] > step * step_rows)
                def _():
                    at = slice(local * cap + step * step_rows, local * cap + (step + 1) * step_rows)
                    slots = slot_row - step * step_rows
                    ones = jnp.where(places == slots, 1.0, 0.0).astype(bfloat)
                    row_buf[source, at, :] = dot_nn(ones, row_all[source, :tokens, :]).astype(bfloat)
                    grad_buf[source, at, :] = dot_nn(ones, grad_all[source, :tokens, :]).astype(
                        bfloat
                    )
                    gate_buf[source, at, :] = jnp.sum(
                        jnp.where(places == slots, gate_row, 0.0), axis=1, keepdims=True
                    )

    for copy in carry_copies:
        copy.wait()
    if not fresh:
        for local in range(2):
            if local not in work[0]:
                row = unpack_row(copy_buf[0, 2 * cap :, :cap], local)
                for step in range(cap // HALF):
                    at = local * (cap // HALF) + step
                    product_buf[0, at : at + 1, :] = row[:, step * HALF : (step + 1) * HALF]
    done = 0
    for local in needed:
        for copy in weight_copies(local):
            copy.wait()
        number = halves[local]

        def place(tile, half):
            entry = table[local, (TILE // HALF) * tile + half]
            step = lax.rem(entry, cap // HALF)
            rows = pl.ds(pl.multiple_of(local * cap + step * HALF, HALF), HALF)
            return entry // (cap // HALF), rows, pl.ds(local * (cap // HALF) + step, 1)

        def one_tile(tile, done):
            slot = lax.rem(done, 2)

            @pl.when(done >= 2)
            def _():
                for copy in save_copies(slot, local, tile):
                    copy.wait()

            for half in range(TILE // HALF):
                at = pl.ds(half * HALF, HALF)

                @pl.when((TILE // HALF) * tile + half < number)
                def _():
                    source, rows, lanes = place(tile, half)
                    now_x[at, :] = row_buf[source, rows, :]
                    now_g[at, :] = grad_buf[source, rows, :]
                    now_gate[at, :] = gate_buf[source, rows, :]

                @pl.when((TILE // HALF) * tile + half >= number)
                def _():
                    now_x[at, :] = jnp.zeros((HALF, width), bfloat)
                    now_g[at, :] = jnp.zeros((HALF, width), bfloat)
                    now_gate[at, :] = jnp.zeros((HALF, 1), single)

            rows_low, grad_low, gate = now_x[...], now_g[...], now_gate[...]
            st_x[slot] = (rows_low.astype(single) * gate).astype(bfloat)
            st_g[slot] = (grad_low.astype(single) * gate).astype(bfloat)
            for start in range(0, hidden, PART):
                cols = slice(start, start + PART)
                pre = dot_nn(rows_low, win[local, :, cols])
                grad_act = dot_nt(grad_low, wout[local, cols, :])
                act, slope = gelu_both(pre)
                st_act[slot, :, cols] = act.astype(bfloat)
                st_pre[slot, :, cols] = (slope * grad_act).astype(bfloat)
            result = dot_nn(st_act[slot], wout[local]).astype(bfloat).astype(single)
            grad_copy = dot_nt(st_pre[slot], win[local]).astype(bfloat)
            product = jnp.sum(grad_low.astype(single) * result, axis=1, keepdims=True)
            result = result.astype(bfloat)
            for half in range(TILE // HALF):
                at = slice(half * HALF, (half + 1) * HALF)

                @pl.when((TILE // HALF) * tile + half < number)
                def _():
                    source, rows, lanes = place(tile, half)
                    out_buf[source, rows, :] = result[at]
                    copy_buf[source, rows, :] = grad_copy[at]
                    product_buf[source, lanes, :] = jnp.sum(
                        jnp.where(eye, product[at], 0.0), axis=0, keepdims=True
                    )

            for copy in save_copies(slot, local, before[local] + tile):
                copy.start()
            return done + 1

        done = lax.fori_loop(
            0, (number + TILE // HALF - 1) // (TILE // HALF), one_tile, done
        )

    def result_copies():
        for source in range(sources):
            yield pltpu.make_async_copy(copy_buf.at[source], grads[source], out_sem.at[0, source])
            yield pltpu.make_async_copy(out_buf.at[source], outs[source], out_sem.at[1, source])

    for source in range(sources):
        rows = []
        for local in range(2):
            at = range(local * (cap // HALF), (local + 1) * (cap // HALF))
            rows.append(jnp.concatenate([product_buf[source, i : i + 1, :] for i in at], axis=1))
        copy_buf[source, 2 * cap :, :cap] = pack_rows(jnp.concatenate(rows, axis=0))
    for copy in result_copies():
        copy.start()
    for back in (1, 2):

        @pl.when(done >= back)
        def _():
            for copy in save_copies(lax.rem(done - back, 2), 0, 0):
                copy.wait()

    for copy in result_copies():
        copy.wait()


def weight_kernel(heads, waited, meta, tiles_saved, save_x, save_g, save_act, save_pre, *refs):
    refs = list(refs[waited:])
    outs = [
        [refs.pop(0) for _ in range(2 if local and by_x and by_c else 1)]
        for local in range(2)
        for by_x in range(heads // 2)
        for by_c in range(2)
    ]
    grad_in, grad_out, buf_x, buf_g, buf_act, buf_pre, sem = refs
    width, hidden = grad_in.shape
    deep, wide = width // heads, hidden // heads
    buffers = (buf_x, buf_g, buf_act, buf_pre)

    def fetch(slot, local, tile):
        at = pl.ds(pl.multiple_of(tile * TILE, TILE), TILE)
        return [
            pltpu.make_async_copy(save.at[local, at, :], buf.at[slot], sem.at[slot, i])
            for i, (save, buf) in enumerate(zip((save_x, save_g, save_act, save_pre), buffers))
        ]

    for local in (1, 0):
        tiles = tiles_saved[local]
        grad_in[...] = jnp.zeros_like(grad_in)
        grad_out[...] = jnp.zeros_like(grad_out)

        @pl.when(tiles > 0)
        def _():
            for copy in fetch(0, local, 0):
                copy.start()

        def one_tile(tile, carry):
            slot = lax.rem(tile, 2)

            @pl.when(tile + 1 < tiles)
            def _():
                for copy in fetch(1 - slot, local, tile + 1):
                    copy.start()

            for copy in fetch(slot, local, tile):
                copy.wait()
            for part in range(hidden // width):
                cols = slice(part * width, (part + 1) * width)
                grad_in[:, cols] += dot_tn(buf_x[slot], buf_pre[slot, :, cols])
                grad_out[:, cols] += dot_tn(buf_g[slot], buf_act[slot, :, cols])
            return carry

        lax.fori_loop(0, tiles, one_tile, 0)
        for by_x in range(heads // 2):
            for by_c in range(2):
                head = lax.rem(meta[0] + by_x, heads // 2) * 2 + lax.rem(meta[1] + by_c, 2)
                out, *rest = outs[(local * (heads // 2) + by_x) * 2 + by_c]
                for part in range(hidden // width):
                    out[part * deep : (part + 1) * deep, :] = grad_in[
                        pl.ds(pl.multiple_of(head * deep, deep), deep),
                        part * width : (part + 1) * width,
                    ].astype(bfloat)
                block = grad_out[:, pl.ds(pl.multiple_of(head * wide, wide), wide)]
                if rest:
                    rest[0][...] = block.T.astype(bfloat)
                else:
                    out[hidden // width * deep :, :] = block.T.astype(bfloat)


def whole_call(kernel, out_shape, scratch=(), micros=1, in_specs=None, out_specs=None, aliases=None):
    specs = {}
    if in_specs is not None:
        specs["in_specs"] = in_specs
    if out_specs is not None:
        specs["out_specs"] = out_specs
    return pl.pallas_call(
        kernel,
        out_shape=out_shape,
        scratch_shapes=scratch,
        input_output_aliases=aliases or {},
        compiler_params=pltpu.CompilerParams(vmem_limit_bytes=VMEM_LIMIT),
        cost_estimate=pl.CostEstimate(
            flops=int(micros * SCALE), bytes_accessed=0, transcendentals=0
        ),
        **specs,
    )


class Grid:
    names = ("zh", "zl", "y", "x", "c")

    def __init__(self, mesh):
        experts, heads = mesh.shape["expert"], mesh.shape["head"]
        self.shape = (2, experts // 4, 2, heads // 2, 2)
        self.experts, self.heads = experts, heads
        self.total = experts * heads

    def size(self, name):
        return self.shape[self.names.index(name)]

    def coords(self, linear):
        out = []
        for extent in reversed(self.shape):
            out.append(linear % extent)
            linear = linear // extent
        return dict(zip(self.names, reversed(out)))

    def linear(self, coords):
        at = 0
        for name, extent in zip(self.names, self.shape):
            at = at * extent + coords[name] % extent
        return at

    def me(self, name):
        linear = lax.axis_index("expert") * self.heads + lax.axis_index("head")
        return self.coords(linear)[name]

    def send(self, value, target):
        pairs = [(i, self.linear(target(self.coords(i)))) for i in range(self.total)]
        return lax.ppermute(value, ("expert", "head"), pairs)

    def move(self, value, **by):
        return self.send(value, lambda at: {name: at[name] - by.get(name, 0) for name in at})

    def shift(self, value, name, by):
        return self.move(value, **{name: by})

    def exchange(self, value, name, *others):
        stride = self.linear({**dict.fromkeys(self.names, 0), name: 1}) // self.heads
        groups = [[at, at + stride] for at in range(self.experts) if at // stride % 2 == 0]
        both = jnp.broadcast_to(value[None], (2, *value.shape))
        both = lax.all_to_all(
            both, "expert", split_axis=0, concat_axis=0, tiled=True, axis_index_groups=groups
        )
        both = after(both, *others) if others else both
        return jnp.where(self.me(name) == 0, both[1], both[0])

    def gather(self, value, name, *others):
        extent, own = self.size(name), self.me(name)
        parts = [value] + [self.shift(value, name, by) for by in range(1, extent)]
        if others:
            parts[1] = after(parts[1], *others)
        if extent == 2:
            return jnp.where(own == 0, jnp.stack(parts), jnp.stack(parts[::-1]))
        return jnp.roll(jnp.stack(parts), own, axis=0)

    def scatter_sum(self, value, name, *waited):
        extent, own = self.size(name), self.me(name)
        if extent == 2:
            kept = jnp.where(own == 0, value[0], value[1])
            others = [self.shift(jnp.where(own == 0, value[1], value[0]), name, 1)]
        else:
            value = jnp.roll(value, -own, axis=0)
            kept = value[0]
            others = [self.shift(value[by], name, -by) for by in range(1, extent)]
        if waited:
            others[0] = after(others[0], *waited)
        total = kept.astype(single)
        for other in others:
            total = total + other.astype(single)
        return total.astype(value.dtype)


def after(value, *others):
    return lax.optimization_barrier((value, *others))[0]


def per_device(
    grid,
    tokens,
    segment_ids,
    task_ids,
    task_table,
    weight_qkv,
    weight_out,
    gain_one,
    gain_two,
    weight_router,
    weight_in,
    weight_hidden,
    cotangent,
):
    expert_count, head_count = grid.experts, grid.heads
    head_index = lax.axis_index("head")
    row_count, model_width = tokens.shape
    cap = 4 * row_count // expert_count
    deep, wide = weight_qkv.shape[1:]
    padded = -(-expert_count // 16) * 16

    pieces = jnp.concatenate([weight_qkv, weight_out.T[None]]).astype(bfloat)
    small = jnp.concatenate(
        [gain_one[None], gain_two[None], weight_router.T]
    ).astype(bfloat).reshape(-1)
    small_rows = -(-small.shape[0] // wide)
    small = jnp.pad(small, (0, small_rows * wide - small.shape[0])).reshape(small_rows, wide)
    packed = jnp.concatenate([pieces.reshape(4 * deep, wide), small])
    own_segments = lax.dynamic_slice_in_dim(segment_ids, head_index * row_count, row_count)
    shape = jax.ShapeDtypeStruct
    vmem, hbm = pl.BlockSpec(memory_space=pltpu.VMEM), pl.BlockSpec(memory_space=pl.ANY)
    smem = pl.BlockSpec(memory_space=pltpu.SMEM)
    table = jnp.pad(task_table.T, ((0, 16 - task_table.shape[1]), (0, 0))).astype(bfloat)
    hidden = weight_in.shape[2]
    deep_in = weight_in.shape[1]
    piece = shape((hidden // model_width * deep_in + weight_hidden.shape[1], model_width), bfloat)
    route_rows = padded * (2 * (row_count // model_width) + 2)
    first, second, route, own_piece, sent = whole_call(
        lambda *refs: routing_kernel(cap, *refs),
        [shape((1, row_count), jnp.int32)] * 2
        + [
            shape((padded, row_count), single),
            piece,
            shape((row_count + route_rows, model_width), bfloat),
        ],
        micros=3,
    )(own_segments[None], task_ids[None], table, weight_in, weight_hidden, cotangent)
    names = {name: grid.me(name) for name in grid.names}
    extent = grid.size("zl")
    offsets = [(dl, dy) for dl in range(extent) for dy in range(2)]
    offsets.sort(key=lambda by: by[0] * by[1] != 0)
    providers = len(offsets)

    def expert_of(zl, y, local):
        return ((names["zh"] + local) % 2 * extent + zl % extent) * 2 + y % 2

    def ints(*values):
        return jnp.concatenate([jnp.asarray(v, jnp.int32).reshape(-1) for v in values])

    targets = ints(
        *[expert_of(names["zl"] - dl, names["y"] - dy, k) for dl, dy in offsets for k in range(2)],
        names["c"],
    )
    parcel = shape((2 * cap + EXTRA, model_width), bfloat)
    packed = grid.gather(grid.gather(packed, "zh"), "zl")
    nearly = packed
    packed = grid.gather(packed, "y")
    smalls = packed.transpose(2, 1, 0, 3, 4).reshape(expert_count, -1)[:, 4 * deep * wide :]
    smalls = smalls[:, : (2 + expert_count) * deep].reshape(expert_count, 2 + expert_count, deep)
    smalls = smalls.transpose(1, 0, 2).reshape(2 + expert_count, model_width)
    gain1, gain2 = smalls[0:1].astype(single), smalls[1:2].astype(single)
    router = jnp.pad(smalls[2:], ((0, padded - expert_count), (0, 0)))
    packed = grid.gather(packed[..., : 4 * deep, :], "x")
    packed = packed.reshape(*packed.shape[:4], 4, deep, wide)
    if wide % LANES:
        packed = grid.gather(packed, "c").transpose(5, 4, 3, 2, 6, 1, 0, 7)
        packed = packed.reshape(4, model_width, model_width)
        weights = (packed, packed)
    else:
        weights = (packed, grid.shift(packed, "c", 1))

    segc = own_segments[:, None]
    starts = [min(max(at - SPAN, 0), row_count - WINDOW) for at in range(0, row_count, BLOCK)]
    segw = jnp.stack([own_segments[at : at + WINDOW] for at in starts])

    core = ints(names["c"])
    gate_rows = 2 * padded * (row_count // model_width)
    proj, attn, res, two_low, stat, gate, weights = whole_call(
        forward_kernel,
        [
            shape((3, row_count, model_width), bfloat),
            shape((row_count, model_width), bfloat),
            shape((row_count, model_width), single),
            shape((row_count + gate_rows, model_width), bfloat),
            shape((row_count, LANES), single),
            shape((padded, row_count), single),
            shape((4, model_width, model_width), bfloat),
        ],
        in_specs=[smem, vmem, hbm, hbm] + [vmem] * 7,
        out_specs=[hbm] * 5 + [vmem, hbm],
        scratch=[
            pltpu.VMEM((3, row_count, model_width), bfloat),
            pltpu.VMEM((row_count, model_width), bfloat),
            pltpu.VMEM((row_count, model_width), single),
            pltpu.VMEM((row_count + gate_rows, model_width), bfloat),
            pltpu.VMEM((row_count, LANES), single),
            pltpu.VMEM((4, model_width, model_width), bfloat),
            pltpu.SemaphoreType.DMA((2, head_count // 2 * expert_count)),
            pltpu.SemaphoreType.DMA((5, max(4, row_count // BLOCK))),
        ],
        micros=0.2,
    )(core, tokens, *weights, gain1, gain2, router, segc, segw, first, second)

    own_piece = after(own_piece, nearly)
    pieces = {(0, 0, 0): own_piece, (1, 0, 0): grid.exchange(own_piece, "zh")}
    for by_x in range(1, head_count // 2):
        pieces[0, by_x, 0] = grid.shift(own_piece, "x", by_x)
    own_experts = [expert_of(names["zl"], names["y"], local) for local in range(2)]
    sent = after(sent, nearly)
    cots = {(dl, 0): grid.move(sent, zl=dl) if dl else sent for dl in range(extent)}
    cots[0, 1] = grid.move(sent, y=1)
    pieces[1, 0, 0] = after(pieces[1, 0, 0], two_low)
    rows = {(dl, 0): grid.move(two_low, zl=dl) if dl else two_low for dl in range(extent)}
    rows[0, 1] = grid.move(two_low, y=1)
    for dl in range(1, extent):
        rows[dl, 1] = grid.move(two_low, zl=dl, y=1)
        cots[dl, 1] = grid.move(cots[dl, 0], y=1)
    for by_x in range(1, head_count // 2):
        pieces[1, by_x, 0] = grid.shift(after(pieces[1, 0, 0], cots[0, 1]), "x", by_x)
    for by_x in range(head_count // 2):
        pieces[0, by_x, 0] = after(pieces[0, by_x, 0], two_low)
        pieces[0, by_x, 1] = grid.shift(pieces[0, by_x, 0], "c", 1)
    piece_keys = [(k, bx, bc) for k in range(2) for bx in range(head_count // 2) for bc in range(2)]

    calls = [{0: (0,)}, {0: (1,), 1: (0, 1)}] + [{at: (0, 1)} for at in range(2, min(4, providers))]
    for at in range(4, providers, 3):
        calls.append({s: (0, 1) for s in range(at, min(at + 3, providers))})
    save_tiles = sum(-(-len(call) * cap // TILE) for call in calls)
    save_shapes = [
        shape((2, save_tiles * TILE, cols), bfloat)
        for cols in (model_width, model_width, hidden, hidden)
    ]
    saved = []
    tiles_before = jnp.zeros((2,), jnp.int32)
    results = {}
    left = len(calls)
    for call in calls:
        left -= 1
        group = list(call)
        count = len(group)
        needed = sorted({local for work in call.values() for local in work})
        carried = [results[s] for s in group if s in results]
        carried = [value for both in carried for value in both]
        held_pieces = [pieces[key] for key in piece_keys if key[0] in needed]
        keys = [offsets[s] for s in group]
        inputs = [ints(names["x"], names["c"], *own_experts), tiles_before]
        inputs += [rows[key] for key in keys] + [cots[key] for key in keys]
        inputs += carried + held_pieces + saved
        before = 2 + 2 * count + len(carried) + len(held_pieces)
        outs = whole_call(
            lambda *refs, work=tuple(call.values()), fresh=not carried, new=not saved: expert_kernel(
                work, head_count, cap, row_count, padded, fresh, new, *refs
            ),
            save_shapes + [parcel] * (2 * count) + [shape((2,), jnp.int32)],
            in_specs=[smem, smem]
            + [hbm] * (2 * count + len(carried) + len(held_pieces) + len(saved)),
            out_specs=[hbm] * (4 + 2 * count) + [smem],
            aliases={before + i: i for i in range(len(saved))},
            scratch=[
                pltpu.VMEM((2, model_width, hidden), bfloat),
                pltpu.VMEM((2, hidden, model_width), bfloat),
                pltpu.VMEM((count, row_count + gate_rows, model_width), bfloat),
                pltpu.VMEM((count, *sent.shape), bfloat),
                pltpu.VMEM((count, 2 * cap, model_width), bfloat),
                pltpu.VMEM((count, 2 * cap, model_width), bfloat),
                pltpu.VMEM((count, 2 * cap, 1), single),
                pltpu.VMEM((count, *parcel.shape), bfloat),
                pltpu.VMEM((count, *parcel.shape), bfloat),
                pltpu.VMEM((count, 2 * cap // HALF, HALF), single),
                pltpu.VMEM((TILE, model_width), bfloat),
                pltpu.VMEM((TILE, model_width), bfloat),
                pltpu.VMEM((TILE, 1), single),
                pltpu.VMEM((2, TILE, model_width), bfloat),
                pltpu.VMEM((2, TILE, model_width), bfloat),
                pltpu.VMEM((2, TILE, hidden), bfloat),
                pltpu.VMEM((2, TILE, hidden), bfloat),
                pltpu.SMEM((2, count * cap // HALF + 1), jnp.int32),
                pltpu.SemaphoreType.DMA((2, head_count * (hidden // model_width + 1))),
                pltpu.SemaphoreType.DMA((2, count)),
                pltpu.SemaphoreType.DMA((2, 4)),
                pltpu.SemaphoreType.DMA((2, count)),
            ],
            micros=(8, 40)[len(saved) // 4] if left > len(calls) - 3 else 16,
        )(*inputs)
        if not saved:
            near = ((0, 1), (1, 0))
            held = lax.optimization_barrier(
                (pieces, rows[0, 1], [cots[key] for key in near], outs[0])
            )
            pieces, rows[0, 1] = dict(held[0]), held[1]
            cots.update(zip(near, held[2]))
            for by_x in range(1, head_count // 2):
                ready = after(pieces[1, by_x, 0], cots[1, 0], rows[0, 1])
                pieces[1, by_x, 0] = ready
            for by_x in range(head_count // 2):
                pieces[1, by_x, 1] = grid.shift(pieces[1, by_x, 0], "c", 1)
        if len(calls) - left == 2:
            for dl in range(1, extent):
                rows[dl, 0] = after(rows[dl, 0], outs[0])
        saved, tiles_before = list(outs[:4]), outs[-1]
        for i, s in enumerate(group):
            results[s] = [outs[4 + i], outs[4 + count + i]]
    out_parcels, grad_parcels = [], []
    for s, (dl, dy) in enumerate(offsets):
        out_part, grad_part = results[s]
        if dl and dy:
            grad_part = after(grad_part, *grad_parcels[1:])
        if dl or dy:
            grad_part = grid.move(grad_part, zl=-dl, y=-dy)
            out_part = after(out_part, saved[0])
            if not (dl and dy):
                out_part = grid.move(out_part, zl=-dl, y=-dy)
        out_parcels.append(out_part)
        grad_parcels.append(grad_part)
    waited = []
    halves = [
        shape((hidden // model_width * deep_in, model_width), bfloat),
        shape((weight_hidden.shape[1], model_width), bfloat),
    ]
    done = whole_call(
        lambda *refs: weight_kernel(head_count, len(waited), *refs),
        [s for key in piece_keys for s in (halves if all(key) else [piece])],
        in_specs=[smem, smem] + [hbm] * (4 + len(waited)),
        scratch=[
            pltpu.VMEM((model_width, hidden), single),
            pltpu.VMEM((model_width, hidden), single),
            pltpu.VMEM((2, TILE, model_width), bfloat),
            pltpu.VMEM((2, TILE, model_width), bfloat),
            pltpu.VMEM((2, TILE, hidden), bfloat),
            pltpu.VMEM((2, TILE, hidden), bfloat),
            pltpu.SemaphoreType.DMA((2, 4)),
        ],
        micros=1,
    )(ints(names["x"], names["c"]), tiles_before, *saved, *waited)
    done, grad_parcels = lax.optimization_barrier((done, grad_parcels))
    out_parcels = [
        grid.move(after(value, done[0]), zl=-dl, y=-dy) if dl and dy else value
        for value, (dl, dy) in zip(out_parcels, offsets)
    ]
    done = list(done)
    grads = {
        key: [done.pop(0) for _ in halves] if all(key) else done.pop(0) for key in piece_keys
    }

    def add(kept, other):
        return (kept.astype(single) + other.astype(single)).astype(bfloat)

    crossed = {}
    for key in piece_keys:
        if key[2] == 0:
            other = grads[key[0], key[1], 1]
            parts = other if isinstance(other, list) else [other]
            parts = [grid.shift(part, "c", -1) for part in parts]
            crossed[key] = jnp.concatenate(parts) if len(parts) > 1 else parts[0]
    for by_x in range(1, head_count // 2):
        grads[1, by_x, 0] = add(grads[1, by_x, 0], crossed.pop((1, by_x, 0)))
    waited = []
    output = whole_call(
        lambda *refs: output_kernel(providers, cap, *refs),
        shape((row_count, model_width), bfloat),
        in_specs=[smem] + [vmem] * (3 + providers),
        micros=8,
    )(targets, res, gate, route, *out_parcels)

    grad_res, grad_heads, grad_out, grad_gain2, grad_router = whole_call(
        lambda *refs: middle_kernel(providers, cap, len(waited), *refs),
        (
            shape((row_count, model_width), single),
            shape((row_count, model_width), bfloat),
            shape((model_width, model_width), bfloat),
            shape((1, model_width), single),
            shape((padded, model_width), single),
        ),
        in_specs=[smem] + [hbm] * 5 + [vmem] * 4 + [hbm] * (providers + len(waited)),
        out_specs=[hbm] * 2 + [vmem] * 3,
        scratch=[
            pltpu.VMEM((padded, row_count), single),
            pltpu.VMEM((row_count, model_width), bfloat),
            pltpu.VMEM((row_count, model_width), single),
            pltpu.VMEM((row_count, model_width), bfloat),
            pltpu.VMEM((row_count, model_width), bfloat),
            pltpu.VMEM((row_count, model_width), single),
            pltpu.VMEM((row_count, model_width), bfloat),
            pltpu.VMEM((row_count, model_width), bfloat),
            pltpu.VMEM((model_width, model_width), bfloat),
            pltpu.VMEM((providers, *parcel.shape), bfloat),
            pltpu.SemaphoreType.DMA((providers + 5,)),
            pltpu.SemaphoreType.DMA((2, row_count // CHUNK)),
        ],
        micros=4,
    )(
        targets, cotangent, res, two_low, attn, weights, gain2, router, gate, route,
        *grad_parcels, *waited,
    )
    for key, other in crossed.items():
        grads[key] = add(grads[key], after(other, grad_gain2))
    for by_x in range(1, head_count // 2):
        other = after(grid.shift(grads[1, by_x, 0], "x", -by_x), grad_gain2)
        grads[1, 0, 0] = add(grads[1, 0, 0], other)
    grad_res = after(grad_res, grads[1, 0, 0], grads[0, 1, 0], *out_parcels[1:-1])
    columns = model_width if wide % LANES else model_width // 2
    grad_tokens, grad_own, other_top, other_rest, grad_gain1 = whole_call(
        lambda *refs: backward_kernel(head_count, *refs),
        (
            shape((row_count, model_width), single),
            shape((4, model_width, columns), bfloat),
            shape((2, model_width, columns), bfloat),
            shape((2, model_width, columns), bfloat),
            shape((1, model_width), single),
        ),
        in_specs=[smem] + [vmem] * 3 + [hbm] * 7,
        out_specs=[hbm] + [vmem] * 4,
        scratch=[
            pltpu.VMEM((3, row_count, model_width), bfloat),
            pltpu.VMEM((row_count, model_width), single),
            pltpu.VMEM((row_count, model_width), single),
            pltpu.VMEM((row_count, model_width), bfloat),
            pltpu.VMEM((4, model_width, model_width), bfloat),
            pltpu.VMEM((3, row_count, model_width), bfloat),
            pltpu.VMEM((row_count, model_width), bfloat),
            pltpu.VMEM((row_count, LANES), single),
            pltpu.VMEM((row_count, model_width), bfloat),
            pltpu.VMEM((row_count, model_width), single),
            pltpu.VMEM((3, model_width, model_width), bfloat),
            pltpu.VMEM((row_count, model_width), single),
            pltpu.SemaphoreType.DMA((7,)),
            pltpu.SemaphoreType.DMA((row_count // CHUNK,)),
        ],
        micros=1,
    )(
        core, gain1, segc, segw, proj, grad_heads, stat, tokens, grad_res, weights, grad_out,
    )

    for by_x in range(1, head_count // 2):
        other = after(grid.shift(grads[0, by_x, 0], "x", -by_x), grad_tokens)
        grads[0, 0, 0] = add(grads[0, 0, 0], other)
    smalls = jnp.concatenate([grad_gain1, grad_gain2, grad_router[:expert_count]]).astype(bfloat)
    ahead = [grads[0, 0, 0], *out_parcels[3:]]
    if wide % LANES or grid.size("x") != 2:
        if wide % LANES:
            packed = grad_own.reshape(4, model_width, -1, 2, wide).transpose(3, 0, 1, 2, 4)
            packed = grid.scatter_sum(packed, "c").reshape(4, model_width, -1)
        else:
            other = [grid.shift(v, "c", 1) for v in (other_top, other_rest)]
            packed = add(grad_own, jnp.concatenate(other))
        packed = packed.reshape(4, model_width, -1, wide).transpose(2, 0, 1, 3)
        packed = grid.scatter_sum(after(packed, *ahead), "x", output)
    else:
        other = [grid.shift(v, "c", 1) for v in (other_top, other_rest)]
        other = lax.optimization_barrier((*other, *ahead))[:2]

        def columns_of(x):
            def pick(value):
                return jnp.where(x == 0, value[..., :wide], value[..., wide:]).astype(single)

            both = zip((grad_own[:2], grad_own[2:]), other)
            return jnp.concatenate([pick(kept) + pick(crossed_in) for kept, crossed_in in both])

        got = grid.shift(columns_of(1 - names["x"]).astype(bfloat), "x", 1)
        packed = columns_of(names["x"]) + after(got, output).astype(single)
        packed = packed.astype(bfloat)
    grad_piece = grads[0, 0, 0].astype(single) + grid.exchange(
        grads[1, 0, 0], "zh", packed
    ).astype(single)
    grad_in_own = grad_piece[: hidden // model_width * deep_in]
    grad_in_own = grad_in_own.reshape(-1, deep_in, model_width).transpose(1, 0, 2)
    grad_in_own = grad_in_own.reshape(1, deep_in, hidden)
    grad_hidden_own = grad_piece[hidden // model_width * deep_in :][None]
    for name in ("c", "x"):
        total = smalls.astype(single)
        for by in range(1, grid.size(name)):
            total = total + grid.shift(smalls, name, by).astype(single)
        smalls = total.astype(bfloat)
    smalls = smalls.reshape(2 + expert_count, expert_count, deep).transpose(1, 0, 2)
    smalls = smalls.reshape(expert_count, -1)
    smalls = jnp.pad(smalls, ((0, 0), (0, small_rows * wide - smalls.shape[1])))
    packed = packed.reshape(4, expert_count, deep, wide).transpose(1, 0, 2, 3)
    packed = packed.reshape(expert_count, 4 * deep, wide)
    packed = jnp.concatenate([packed, smalls.reshape(expert_count, small_rows, wide)], axis=1)
    packed = packed.reshape(*grid.shape[:3], 4 * deep + small_rows, wide).transpose(2, 1, 0, 3, 4)
    packed = after(packed, grad_piece)
    for name in ("y", "zl", "zh"):
        packed = grid.scatter_sum(packed, name)
    pieces = packed[: 4 * deep].reshape(4, deep, wide).astype(single)
    smalls = packed[4 * deep :].reshape(-1)[: (2 + expert_count) * deep].astype(single)
    smalls = smalls.reshape(2 + expert_count, deep)
    return (
        output,
        grad_tokens,
        pieces[:3],
        pieces[3].T,
        smalls[0],
        smalls[1],
        smalls[2:].T,
        grad_in_own,
        grad_hidden_own,
    )


def solution(mesh):
    grid = Grid(mesh)
    placed = (
        P(("expert", "head"), None),
        P("expert"),
        P(),
        P(),
        P(None, "expert", "head"),
        P("head", "expert"),
        P("expert"),
        P("expert"),
        P("expert", None),
        P("expert", "head", None),
        P("expert", "head", None),
        P(("expert", "head"), None),
    )

    def step(*arrays):
        return per_device(grid, *arrays)

    return jax.shard_map(
        step,
        mesh=mesh,
        in_specs=placed,
        out_specs=(
            P(("expert", "head"), None),
            P(("expert", "head"), None),
            P(None, "expert", "head"),
            P("head", "expert"),
            P("expert"),
            P("expert"),
            P("expert", None),
            P("expert", "head", None),
            P("expert", "head", None),
        ),
        check_vma=False,
    )
```

```python
import jax
import jax.numpy as jnp
from jax import lax
from jax.experimental import pallas as pl
from jax.experimental.pallas import tpu as pltpu
from jax.sharding import PartitionSpec as P

HDIM = 64
PACK = 1024
SPAN = 64
BLOCK = 128
WINDOW = BLOCK + 2 * SPAN
CHUNK = 256
LANES = 128
TILE = 256
HALF = 64
EXTRA = 16
PART = 256
ABSENT = -1e6
SCALE = 1153e6 / 8

EPSILON = 1e-05
NEGATIVE = -1e30

bfloat = jnp.bfloat16
single = jnp.float32
VMEM_LIMIT = 56 * 1024 * 1024


def dot_nn(a, b):
    return lax.dot_general(a, b, (((1,), (0,)), ((), ())), preferred_element_type=single)


def dot_nt(a, b):
    return lax.dot_general(a, b, (((1,), (1,)), ((), ())), preferred_element_type=single)


def dot_tn(a, b):
    return lax.dot_general(a, b, (((0,), (0,)), ((), ())), preferred_element_type=single)


def normalise(values):
    centered = values - jnp.mean(values, axis=-1, keepdims=True)
    inverse = lax.rsqrt(jnp.mean(centered * centered, axis=-1, keepdims=True) + EPSILON)
    return centered * inverse, inverse


def norm_pull(grad_normed, scaled, inverse, gain):
    weighted = grad_normed * gain
    return inverse * (
        weighted
        - jnp.mean(weighted, axis=-1, keepdims=True)
        - scaled * jnp.mean(weighted * scaled, axis=-1, keepdims=True)
    )


def split_heads(pair, first_half):
    zero = jnp.zeros_like(pair)
    return jnp.concatenate(
        [jnp.where(first_half, pair, zero), jnp.where(first_half, zero, pair)], axis=0
    )


def segment_bias(segc, segr, q_at, k_at):
    bias = jnp.where(segc[k_at, :] == segr[:, q_at], 0.0, NEGATIVE)
    return jnp.concatenate([bias, bias], axis=1)


def window_start(block, rows):
    return pl.multiple_of(jnp.clip(block * BLOCK - SPAN, 0, rows - WINDOW), SPAN)


def fetch_weights(core, own, other, weights, sem):
    copies = []
    if own.shape == weights.shape:
        copies = [pltpu.make_async_copy(own, weights, sem.at[0, 0])]
    else:
        parts_x, parts_y, parts_zl, parts_zh, _, deep, wide = own.shape
        places = [
            (x, y, zl, zh)
            for x in range(parts_x)
            for y in range(parts_y)
            for zl in range(parts_zl)
            for zh in range(parts_zh)
        ]
        for at, (x, y, zl, zh) in enumerate(places):
            row = ((zh * parts_zl + zl) * parts_y + y) * deep
            for i, (ref, half) in enumerate(((own, core), (other, 1 - core))):
                start = pl.multiple_of((2 * x + half) * wide, LANES)
                copies.append(
                    pltpu.make_async_copy(
                        ref.at[x, y, zl, zh],
                        weights.at[:, pl.ds(row, deep), pl.ds(start, wide)],
                        sem.at[i, at],
                    )
                )
    for copy in copies:
        copy.start()
    for copy in copies:
        copy.wait()


def forward_kernel(
    meta, tok, weights_own, weights_other, gain1, gain2, router, segc, segr, first, second,
    proj_out, attn_out, res_out, two_out, stat_out, gate, weights_out,
    proj, attn, res, two, stat, weights, sem, out_sem,
):
    rows, width = tok.shape
    fetch_weights(meta[0], weights_own, weights_other, weights, sem)
    wqkv, wot = weights, weights.at[3]
    leaving = [pltpu.make_async_copy(weights, weights_out, out_sem.at[0, 0])]
    leaving[0].start()

    def project(step, carry):
        at = pl.ds(pl.multiple_of(step * CHUNK, CHUNK), CHUNK)
        scaled, _ = normalise(tok[at, :].astype(single))
        low = (scaled * gain1[...]).astype(bfloat)
        for part in range(3):
            proj[part, at, :] = dot_nn(low, wqkv[part]).astype(bfloat)
        return carry

    lax.fori_loop(0, rows // CHUNK, project, 0)
    leaving.append(pltpu.make_async_copy(proj, proj_out, out_sem.at[0, 1]))
    leaving[1].start()

    def block_copies(block):
        at = pl.ds(pl.multiple_of(block * BLOCK, BLOCK), BLOCK)
        return [
            pltpu.make_async_copy(held.at[at, :], out.at[at, :], out_sem.at[1 + i, block])
            for i, (held, out) in enumerate(
                ((attn, attn_out), (res, res_out), (two, two_out))
            )
        ]

    lane = lax.broadcasted_iota(jnp.int32, (BLOCK, LANES), 1)
    first_half = lane < HDIM
    expert = lax.broadcasted_iota(jnp.int32, (router.shape[0], BLOCK), 0)

    def attend(block, carry):
        q_at = pl.ds(pl.multiple_of(block * BLOCK, BLOCK), BLOCK)
        k_at = pl.ds(window_start(block, rows), WINDOW)
        bias = segment_bias(segc, segr, q_at, k_at)
        for pair in range(width // LANES):
            cols = slice(pair * LANES, (pair + 1) * LANES)
            queries = split_heads(proj[0, q_at, cols] * HDIM**-0.5, first_half)
            scores = dot_nt(proj[1, k_at, cols], queries) + bias
            peak = jnp.max(scores, axis=0, keepdims=True)
            exponent = jnp.exp(scores - peak)
            total = jnp.sum(exponent, axis=0, keepdims=True)
            probs = (exponent * (1.0 / total)).astype(bfloat)
            out = dot_tn(probs, proj[2, k_at, cols])
            attn[q_at, cols] = jnp.where(first_half, out[:BLOCK], out[BLOCK:]).astype(bfloat)
            log_total = peak + jnp.log(total)
            stat[2 * pair : 2 * pair + 1, q_at] = log_total[:, :BLOCK]
            stat[2 * pair + 1 : 2 * pair + 2, q_at] = log_total[:, BLOCK:]
        residual = tok[q_at, :].astype(single) + dot_nt(attn[q_at, :], wot[...])
        res[q_at, :] = residual
        scaled, _ = normalise(residual)
        low = (scaled * gain2[...]).astype(bfloat)
        two[q_at, :] = low
        logits = dot_nt(router[...], low)
        mark0 = first[:, q_at] == expert
        mark1 = second[:, q_at] == expert
        logit0 = jnp.sum(jnp.where(mark0, logits, 0.0), axis=0, keepdims=True)
        logit1 = jnp.sum(jnp.where(mark1, logits, 0.0), axis=0, keepdims=True)
        top = jnp.maximum(logit0, logit1)
        part0, part1 = jnp.exp(logit0 - top), jnp.exp(logit1 - top)
        scale = 1.0 / (part0 + part1)
        gate[:, q_at] = jnp.where(mark0, part0 * scale, jnp.where(mark1, part1 * scale, 0.0))
        for copy in block_copies(block):
            copy.start()
        return carry

    lax.fori_loop(0, rows // BLOCK, attend, 0)
    count = gate.shape[0]
    at = rows
    for part in split_two(gate[...]):
        for start in range(0, rows, width):
            two[at : at + count, :] = part[:, start : start + width]
            at += count
    leaving.append(pltpu.make_async_copy(stat, stat_out, out_sem.at[0, 3]))
    leaving[2].start()
    rest = pl.ds(rows, two.shape[0] - rows)
    leaving.append(
        pltpu.make_async_copy(two.at[rest, :], two_out.at[rest, :], out_sem.at[0, 2])
    )
    leaving[3].start()
    for copy in leaving:
        copy.wait()

    def settle(block, carry):
        for copy in block_copies(block):
            copy.wait()
        return carry

    lax.fori_loop(0, rows // BLOCK, settle, 0)


def split_two(values):
    high = values.astype(bfloat)
    return high, (values - high.astype(single)).astype(bfloat)


def pack_rows(rows):
    at = lax.broadcasted_iota(jnp.int32, (EXTRA, rows.shape[1]), 0)
    out = jnp.zeros((EXTRA, rows.shape[1]), single)
    for local in range(2):
        high = rows[local : local + 1, :].astype(bfloat).astype(single)
        out = jnp.where(at == 2 * local, high, out)
        out = jnp.where(at == 2 * local + 1, rows[local : local + 1, :] - high, out)
    return out.astype(bfloat)


def unpack_row(packed, local):
    packed = packed.astype(single)
    return packed[2 * local : 2 * local + 1, :] + packed[2 * local + 1 : 2 * local + 2, :]


def routing_kernel(
    cap, segments, tasks, table, weight_in, weight_hidden, cot,
    first, second, route, piece, sent,
):
    rows = segments.shape[1]
    deep, hidden = weight_in.shape[1:]
    width = piece.shape[1]
    for part in range(hidden // width):
        piece[part * deep : (part + 1) * deep, :] = weight_in[
            0, :, part * width : (part + 1) * width
        ].astype(bfloat)
    piece[hidden // width * deep :, :] = weight_hidden[0].astype(bfloat)
    names = lax.broadcasted_iota(jnp.int32, (table.shape[1], tasks.shape[1]), 0)
    experts = dot_nn(table[...], jnp.where(names == tasks[...], 1.0, 0.0).astype(bfloat))
    experts = experts.astype(bfloat)
    chosen = jnp.zeros((table.shape[0], rows), single)
    for start in range(0, tasks.shape[1], 1024):
        size = min(1024, tasks.shape[1] - start)
        at = lax.broadcasted_iota(jnp.int32, (size, rows), 0) + start
        ones = jnp.where(at == segments[...], 1.0, 0.0).astype(bfloat)
        chosen = chosen + dot_nn(experts[:, start : start + size], ones)
    zero, one = chosen[0:1, :], chosen[1:2, :]
    first[...] = zero.astype(jnp.int32)
    second[...] = one.astype(jnp.int32)
    which = lax.broadcasted_iota(jnp.int32, route.shape, 0).astype(single)
    is_first, is_second = which == zero, which == one
    marks = jnp.where(is_first | is_second, 1.0, 0.0)
    earlier = lax.broadcasted_iota(jnp.int32, (rows, rows), 0) < lax.broadcasted_iota(
        jnp.int32, (rows, rows), 1
    )
    places = dot_nn(marks.astype(bfloat), jnp.where(earlier, 1.0, 0.0).astype(bfloat))
    inside = (marks > 0.5) & (places < cap)
    slots = jnp.where(inside, places, ABSENT)
    route[...] = slots
    total = jnp.sum(jnp.where(inside, 1.0, 0.0), axis=1, keepdims=True)
    total = jnp.broadcast_to(total, (route.shape[0], width))
    sent[:rows, :] = cot[...]
    at = rows
    for part in range(2):
        for start in range(0, rows, width):
            sent[at : at + route.shape[0], :] = sixteens(slots[:, start : start + width])[part]
            at += route.shape[0]
    for part in range(2):
        sent[at : at + route.shape[0], :] = sixteens(total)[part]
        at += route.shape[0]


def sixteens(values):
    high = jnp.floor(values * 0.0625) * 16.0
    high = jnp.where(values < 0.0, values, high)
    return high.astype(bfloat), jnp.where(values < 0.0, 0.0, values - high).astype(bfloat)


def output_kernel(providers, cap, meta, res, gate, slots, *refs):
    parcels, out = refs[:providers], refs[providers]
    for step in range(res.shape[0] // CHUNK):
        at = slice(step * CHUNK, (step + 1) * CHUNK)
        out[at, :] = (res[at, :] + returned_rows(parcels, cap, meta, gate, slots, at)).astype(bfloat)


def returned_rows(parcels, cap, meta, gate, slots, at):
    total = 0.0
    for provider, parcel in enumerate(parcels):
        for local in range(2):
            chosen = pl.ds(meta[2 * provider + local], 1)
            ones = onehot(slots[chosen, at], 0, cap, gate[chosen, at])
            total = total + dot_tn(ones, parcel[local * cap : (local + 1) * cap, :])
    return total


def middle_kernel(
    providers, cap, waited, meta,
    cot_in, res_in, two_in, attn_in, weights_in, gain2, router, gate, slots,
    *refs,
):
    parcels = refs[:providers]
    (
        res_left, heads_left, grad_out, grad_gain2, grad_router,
        products, grad_attn, grad_res, grad_heads, cot, res, two, attn, wot, parcel_bufs, sem, out_sem,
    ) = refs[providers + waited :]
    rows, width = cot.shape
    two_rows = two_in.at[pl.ds(0, rows), :]
    arriving = [
        pltpu.make_async_copy(given, held, sem.at[i])
        for i, (given, held) in enumerate(
            [(parcel, parcel_bufs.at[at]) for at, parcel in enumerate(parcels)]
            + [(res_in, res), (cot_in, cot), (weights_in.at[3], wot), (two_rows, two), (attn_in, attn)]
        )
    ]
    for copy in arriving:
        copy.start()
    parcels = [parcel_bufs.at[at] for at in range(providers)]
    for copy in arriving[:providers]:
        copy.wait()
    products[...] = jnp.zeros_like(products)
    for provider in range(providers):
        for local in range(2):
            chosen = meta[2 * provider + local]
            ones = onehot(slots[pl.ds(chosen, 1), :], 0, cap)
            moved = dot_nn(parcels[provider][2 * cap :, :cap], ones)
            products[pl.ds(chosen, 1), :] = unpack_row(moved, local)
    gates = gate[...]
    inner_products = products[...]
    grad_logits = gates * (
        inner_products - jnp.sum(gates * inner_products, axis=0, keepdims=True)
    )
    grad_logits = jnp.concatenate(split_two(grad_logits), axis=0)
    router_twice = jnp.concatenate([router[...], router[...]], axis=0)
    count = router.shape[0]
    grad_gain2[...] = jnp.zeros_like(grad_gain2)
    for copy in arriving[providers : providers + 3]:
        copy.wait()
    leaving = []
    for step in range(rows // CHUNK):
        at = slice(step * CHUNK, (step + 1) * CHUNK)
        scaled, inverse = normalise(res[at, :])
        grad_normed = dot_tn(grad_logits[:, at], router_twice)
        grad_normed = grad_normed + returned_rows(parcels, cap, meta, gate, slots, at)
        grad_gain2[...] += jnp.sum(grad_normed * scaled, axis=0, keepdims=True)
        grad_row = cot[at, :].astype(single) + norm_pull(grad_normed, scaled, inverse, gain2[...])
        grad_res[at, :] = grad_row
        low = grad_row.astype(bfloat)
        grad_attn[at, :] = low
        grad_heads[at, :] = dot_nn(low, wot[...]).astype(bfloat)
        part = pl.ds(step * CHUNK, CHUNK)
        for i, (held, out) in enumerate(((grad_res, res_left), (grad_heads, heads_left))):
            leaving.append(
                pltpu.make_async_copy(held.at[part, :], out.at[part, :], out_sem.at[i, step])
            )
            leaving[-1].start()
    for copy in arriving[providers + 3 :]:
        copy.wait()
    routed = dot_nn(grad_logits, two[...])
    grad_router[...] = routed[:count] + routed[count:]
    grad_out[...] = dot_tn(grad_attn[...], attn[...]).astype(bfloat)
    for copy in leaving:
        copy.wait()


def backward_kernel(
    heads, core, gain1, segc, segr,
    proj_in, heads_in, stat_in, tok_in, res_in, weights_in, out_in,
    tok_left, grad_own, other_top, other_rest, grad_gain1,
    grad_proj, grad_key, grad_value, normed, grad_w,
    proj, grad_heads, stat, tok, grad_res, wqkv, grad_tok, sem, out_sem,
):
    rows, width = tok.shape
    arriving = [
        pltpu.make_async_copy(given, held, sem.at[i])
        for i, (given, held) in enumerate(
            (
                (proj_in, proj), (heads_in, grad_heads), (stat_in, stat), (tok_in, tok),
                (res_in, grad_res), (weights_in.at[pl.ds(0, 3)], wqkv), (out_in, grad_w.at[3]),
            )
        )
    ]
    for copy in arriving:
        copy.start()
    grad_gain1[...] = jnp.zeros_like(grad_gain1)
    grad_key[...] = jnp.zeros_like(grad_key)
    grad_value[...] = jnp.zeros_like(grad_value)
    for copy in arriving[:3]:
        copy.wait()
    lane = lax.broadcasted_iota(jnp.int32, (BLOCK, LANES), 1)
    first_half = lane < HDIM

    def attend(block, carry):
        q_at = pl.ds(pl.multiple_of(block * BLOCK, BLOCK), BLOCK)
        k_at = pl.ds(window_start(block, rows), WINDOW)
        bias = segment_bias(segc, segr, q_at, k_at)
        for pair in range(width // LANES):
            cols = slice(pair * LANES, (pair + 1) * LANES)
            queries = split_heads(proj[0, q_at, cols] * HDIM**-0.5, first_half)
            keys_block = proj[1, k_at, cols]
            log_total = jnp.concatenate(
                [stat[2 * pair + half : 2 * pair + half + 1, q_at] for half in range(2)], axis=1
            )
            probs = jnp.exp(dot_nt(keys_block, queries) + bias - log_total)
            heads_low = split_heads(grad_heads[q_at, cols], first_half)
            grad_probs = dot_nt(proj[2, k_at, cols], heads_low)
            delta = jnp.sum(probs * grad_probs, axis=0, keepdims=True)
            grad_scores = (probs * (grad_probs - delta)).astype(bfloat)
            grad_query = dot_tn(grad_scores, keys_block) * HDIM**-0.5
            grad_proj[0, q_at, cols] = jnp.where(
                first_half, grad_query[:BLOCK], grad_query[BLOCK:]
            ).astype(bfloat)
            grad_key[k_at, cols] += dot_nn(grad_scores, queries)
            grad_value[k_at, cols] += dot_nn(probs.astype(bfloat), heads_low)
        return carry

    lax.fori_loop(0, rows // BLOCK, attend, 0)
    for copy in arriving[3:]:
        copy.wait()
    leaving = []
    for step in range(rows // CHUNK):
        at = slice(step * CHUNK, (step + 1) * CHUNK)
        grad_proj[1, at, :] = grad_key[at, :].astype(bfloat)
        grad_proj[2, at, :] = grad_value[at, :].astype(bfloat)
        grad_normed = dot_nt(grad_proj[0, at, :], wqkv[0])
        for part in (1, 2):
            grad_normed += dot_nt(grad_proj[part, at, :], wqkv[part])
        scaled, inverse = normalise(tok[at, :].astype(single))
        normed[at, :] = (scaled * gain1[...]).astype(bfloat)
        grad_gain1[...] += jnp.sum(grad_normed * scaled, axis=0, keepdims=True)
        grad_tok[at, :] = grad_res[at, :] + norm_pull(grad_normed, scaled, inverse, gain1[...])
        part = pl.ds(step * CHUNK, CHUNK)
        leaving.append(
            pltpu.make_async_copy(grad_tok.at[part, :], tok_left.at[part, :], out_sem.at[step])
        )
        leaving[-1].start()
    for part in range(3):
        grad_w[part] = dot_tn(normed[...], grad_proj[part]).astype(bfloat)
    if grad_own.shape == grad_w.shape:
        grad_own[...] = grad_w[...]
        other_top[...] = grad_w[:2]
        other_rest[...] = grad_w[2:]
    else:
        wide = width // heads
        for by in range(heads // 2):
            cols = slice(by * wide, (by + 1) * wide)
            start = pl.multiple_of((2 * by + core[0]) * wide, LANES)
            grad_own[:, :, cols] = grad_w[:, :, pl.ds(start, wide)]
            start = pl.multiple_of((2 * by + 1 - core[0]) * wide, LANES)
            other_top[:, :, cols] = grad_w[:2, :, pl.ds(start, wide)]
            other_rest[:, :, cols] = grad_w[2:, :, pl.ds(start, wide)]
    for copy in leaving:
        copy.wait()


def onehot(slots, base, rows, marks=1.0):
    places = lax.broadcasted_iota(jnp.int32, (rows, slots.shape[1]), 0).astype(single)
    return jnp.where(places == slots - base, marks, 0.0).astype(bfloat)


def gelu_both(values):
    bent = values * (0.7978845608028654 + 0.035677408136300125 * (values * values))
    half = 0.5 * jnp.tanh(bent) + 0.5
    steep = 6.0 * bent - 3.1915382432114616 * values
    return values * half, half * (1.0 + (1.0 - half) * steep)


def expert_kernel(work, heads, cap, tokens, count, fresh, first, meta, before, *refs):
    refs = list(refs)
    sources = len(work)
    needed = sorted({local for locals_of in work for local in locals_of})

    def take(count):
        taken = refs[:count]
        del refs[:count]
        return taken

    rows_in, grads_in = take(sources), take(sources)
    carried = [] if fresh else take(2)
    pieces = take(len(needed) * heads)
    if not first:
        take(4)
    saved = take(4)
    outs, grads = take(sources), take(sources)
    (now,) = take(1)
    (
        win, wout, row_all, grad_all, row_buf, grad_buf, gate_buf,
        out_buf, copy_buf, product_buf, now_x, now_g, now_gate,
        st_x, st_g, st_act, st_pre, table, w_sem, in_sem, s_sem, out_sem,
    ) = refs
    width = row_buf.shape[2]
    hidden = wout.shape[1]
    deep, wide = width // heads, hidden // heads
    head_x, head_c = meta[0], meta[1]
    staged = (st_x, st_g, st_act, st_pre)

    def weight_copies(local):
        at = 0
        for by_x in range(heads // 2):
            for by_c in range(2):
                head = lax.rem(head_x + by_x, heads // 2) * 2 + lax.rem(head_c + by_c, 2)
                piece = pieces[(needed.index(local) * (heads // 2) + by_x) * 2 + by_c]
                for part in range(hidden // width):
                    yield pltpu.make_async_copy(
                        piece.at[pl.ds(part * deep, deep), :],
                        win.at[
                            local,
                            pl.ds(pl.multiple_of(head * deep, deep), deep),
                            pl.ds(part * width, width),
                        ],
                        w_sem.at[local, at],
                    )
                    at += 1
                yield pltpu.make_async_copy(
                    piece.at[pl.ds(hidden // width * deep, wide), :],
                    wout.at[local, pl.ds(pl.multiple_of(head * wide, wide), wide), :],
                    w_sem.at[local, at],
                )
                at += 1

    def source_copies():
        for source in range(sources):
            for i, (given, held) in enumerate(((rows_in, row_all), (grads_in, grad_all))):
                yield pltpu.make_async_copy(given[source], held.at[source], in_sem.at[i, source])

    for copy in source_copies():
        copy.start()
    for local in needed:
        for copy in weight_copies(local):
            copy.start()
    carry_copies = [
        pltpu.make_async_copy(given, held.at[0], out_sem.at[i, 0])
        for i, (given, held) in enumerate(zip(carried, (out_buf, copy_buf)))
    ]
    for copy in carry_copies:
        copy.start()
    for source in range(0 if fresh else 1, sources):
        out_buf[source] = jnp.zeros_like(out_buf[source])
        copy_buf[source] = jnp.zeros_like(copy_buf[source])
    product_buf[...] = jnp.zeros_like(product_buf)

    def save_copies(slot, local, tile):
        at = pl.ds(pl.multiple_of(tile * TILE, TILE), TILE)
        return [
            pltpu.make_async_copy(stage.at[slot], save.at[local, at, :], s_sem.at[slot, i])
            for i, (stage, save) in enumerate(zip(staged, saved))
        ]

    eye = lax.broadcasted_iota(jnp.int32, (HALF, HALF), 0) == lax.broadcasted_iota(
        jnp.int32, (HALF, HALF), 1
    )
    for copy in source_copies():
        copy.wait()
    step_rows = min(TILE, cap)
    which = lax.broadcasted_iota(jnp.int32, (count, 1), 0)
    numbers, halves = {}, []
    for local in range(2):
        number = 0
        for source in range(sources):
            if local not in work[source]:
                continue
            at = grad_all.shape[1] - 2 * count
            total = grad_all[source, at : at + count, :LANES].astype(single)
            total = total + grad_all[source, at + count :, :LANES].astype(single)
            total = jnp.max(jnp.where(which == meta[2 + local], total, 0.0)).astype(jnp.int32)
            numbers[source, local] = total
            for half in range(cap // HALF):
                table[local, number] = source * (cap // HALF) + half
                number = number + jnp.where(total > half * HALF, 1, 0)
        halves.append(number)
        now[local] = before[local] + (number + TILE // HALF - 1) // (TILE // HALF)
    places = lax.broadcasted_iota(jnp.int32, (step_rows, tokens), 0).astype(single)
    for source in range(sources):
        for local in work[source]:
            expert = meta[2 + local]

            def by_token(ref):
                row = []
                for part in range(tokens // width):
                    parts = [
                        ref[source, pl.ds(tokens + (i * (tokens // width) + part) * count, count), :]
                        for i in range(2)
                    ]
                    both = parts[0].astype(single) + parts[1].astype(single)
                    both = jnp.where(which == expert, both, 0.0)
                    row.append(jnp.sum(both, axis=0, keepdims=True))
                return jnp.concatenate(row, axis=1)

            gate_row, slot_row = by_token(row_all), by_token(grad_all)
            for step in range(cap // step_rows):

                @pl.when(numbers[source, local] > step * step_rows)
                def _():
                    at = slice(local * cap + step * step_rows, local * cap + (step + 1) * step_rows)
                    slots = slot_row - step * step_rows
                    ones = jnp.where(places == slots, 1.0, 0.0).astype(bfloat)
                    row_buf[source, at, :] = dot_nn(ones, row_all[source, :tokens, :]).astype(bfloat)
                    grad_buf[source, at, :] = dot_nn(ones, grad_all[source, :tokens, :]).astype(
                        bfloat
                    )
                    gate_buf[source, at, :] = jnp.sum(
                        jnp.where(places == slots, gate_row, 0.0), axis=1, keepdims=True
                    )

    for copy in carry_copies:
        copy.wait()
    if not fresh:
        for local in range(2):
            if local not in work[0]:
                row = unpack_row(copy_buf[0, 2 * cap :, :cap], local)
                for step in range(cap // HALF):
                    at = local * (cap // HALF) + step
                    product_buf[0, at : at + 1, :] = row[:, step * HALF : (step + 1) * HALF]
    done = 0
    for local in needed:
        for copy in weight_copies(local):
            copy.wait()
        number = halves[local]

        def place(tile, half):
            entry = table[local, (TILE // HALF) * tile + half]
            step = lax.rem(entry, cap // HALF)
            rows = pl.ds(pl.multiple_of(local * cap + step * HALF, HALF), HALF)
            return entry // (cap // HALF), rows, pl.ds(local * (cap // HALF) + step, 1)

        def one_tile(tile, done):
            slot = lax.rem(done, 2)

            @pl.when(done >= 2)
            def _():
                for copy in save_copies(slot, local, tile):
                    copy.wait()

            for half in range(TILE // HALF):
                at = pl.ds(half * HALF, HALF)

                @pl.when((TILE // HALF) * tile + half < number)
                def _():
                    source, rows, lanes = place(tile, half)
                    now_x[at, :] = row_buf[source, rows, :]
                    now_g[at, :] = grad_buf[source, rows, :]
                    now_gate[at, :] = gate_buf[source, rows, :]

                @pl.when((TILE // HALF) * tile + half >= number)
                def _():
                    now_x[at, :] = jnp.zeros((HALF, width), bfloat)
                    now_g[at, :] = jnp.zeros((HALF, width), bfloat)
                    now_gate[at, :] = jnp.zeros((HALF, 1), single)

            rows_low, grad_low, gate = now_x[...], now_g[...], now_gate[...]
            st_x[slot] = (rows_low.astype(single) * gate).astype(bfloat)
            st_g[slot] = (grad_low.astype(single) * gate).astype(bfloat)
            for start in range(0, hidden, PART):
                cols = slice(start, start + PART)
                pre = dot_nn(rows_low, win[local, :, cols])
                grad_act = dot_nt(grad_low, wout[local, cols, :])
                act, slope = gelu_both(pre)
                st_act[slot, :, cols] = act.astype(bfloat)
                st_pre[slot, :, cols] = (slope * grad_act).astype(bfloat)
            result = dot_nn(st_act[slot], wout[local]).astype(bfloat).astype(single)
            grad_copy = dot_nt(st_pre[slot], win[local]).astype(bfloat)
            product = jnp.sum(grad_low.astype(single) * result, axis=1, keepdims=True)
            result = result.astype(bfloat)
            for half in range(TILE // HALF):
                at = slice(half * HALF, (half + 1) * HALF)

                @pl.when((TILE // HALF) * tile + half < number)
                def _():
                    source, rows, lanes = place(tile, half)
                    out_buf[source, rows, :] = result[at]
                    copy_buf[source, rows, :] = grad_copy[at]
                    product_buf[source, lanes, :] = jnp.sum(
                        jnp.where(eye, product[at], 0.0), axis=0, keepdims=True
                    )

            for copy in save_copies(slot, local, before[local] + tile):
                copy.start()
            return done + 1

        done = lax.fori_loop(
            0, (number + TILE // HALF - 1) // (TILE // HALF), one_tile, done
        )

    def result_copies():
        for source in range(sources):
            yield pltpu.make_async_copy(copy_buf.at[source], grads[source], out_sem.at[0, source])
            yield pltpu.make_async_copy(out_buf.at[source], outs[source], out_sem.at[1, source])

    for source in range(sources):
        rows = []
        for local in range(2):
            at = range(local * (cap // HALF), (local + 1) * (cap // HALF))
            rows.append(jnp.concatenate([product_buf[source, i : i + 1, :] for i in at], axis=1))
        copy_buf[source, 2 * cap :, :cap] = pack_rows(jnp.concatenate(rows, axis=0))
    for copy in result_copies():
        copy.start()
    for back in (1, 2):

        @pl.when(done >= back)
        def _():
            for copy in save_copies(lax.rem(done - back, 2), 0, 0):
                copy.wait()

    for copy in result_copies():
        copy.wait()


def weight_kernel(heads, waited, meta, tiles_saved, save_x, save_g, save_act, save_pre, *refs):
    refs = list(refs[waited:])
    outs = [
        [refs.pop(0) for _ in range(2 if local and by_x and by_c else 1)]
        for local in range(2)
        for by_x in range(heads // 2)
        for by_c in range(2)
    ]
    grad_in, grad_out, buf_x, buf_g, buf_act, buf_pre, sem = refs
    width, hidden = grad_in.shape
    deep, wide = width // heads, hidden // heads
    buffers = (buf_x, buf_g, buf_act, buf_pre)

    def fetch(slot, local, tile):
        at = pl.ds(pl.multiple_of(tile * TILE, TILE), TILE)
        return [
            pltpu.make_async_copy(save.at[local, at, :], buf.at[slot], sem.at[slot, i])
            for i, (save, buf) in enumerate(zip((save_x, save_g, save_act, save_pre), buffers))
        ]

    for local in (1, 0):
        tiles = tiles_saved[local]
        grad_in[...] = jnp.zeros_like(grad_in)
        grad_out[...] = jnp.zeros_like(grad_out)

        @pl.when(tiles > 0)
        def _():
            for copy in fetch(0, local, 0):
                copy.start()

        def one_tile(tile, carry):
            slot = lax.rem(tile, 2)

            @pl.when(tile + 1 < tiles)
            def _():
                for copy in fetch(1 - slot, local, tile + 1):
                    copy.start()

            for copy in fetch(slot, local, tile):
                copy.wait()
            for part in range(hidden // width):
                cols = slice(part * width, (part + 1) * width)
                grad_in[:, cols] += dot_tn(buf_x[slot], buf_pre[slot, :, cols])
                grad_out[:, cols] += dot_tn(buf_g[slot], buf_act[slot, :, cols])
            return carry

        lax.fori_loop(0, tiles, one_tile, 0)
        for by_x in range(heads // 2):
            for by_c in range(2):
                head = lax.rem(meta[0] + by_x, heads // 2) * 2 + lax.rem(meta[1] + by_c, 2)
                out, *rest = outs[(local * (heads // 2) + by_x) * 2 + by_c]
                for part in range(hidden // width):
                    out[part * deep : (part + 1) * deep, :] = grad_in[
                        pl.ds(pl.multiple_of(head * deep, deep), deep),
                        part * width : (part + 1) * width,
                    ].astype(bfloat)
                block = grad_out[:, pl.ds(pl.multiple_of(head * wide, wide), wide)]
                if rest:
                    rest[0][...] = block.T.astype(bfloat)
                else:
                    out[hidden // width * deep :, :] = block.T.astype(bfloat)


def whole_call(kernel, out_shape, scratch=(), micros=1, in_specs=None, out_specs=None, aliases=None):
    specs = {}
    if in_specs is not None:
        specs["in_specs"] = in_specs
    if out_specs is not None:
        specs["out_specs"] = out_specs
    return pl.pallas_call(
        kernel,
        out_shape=out_shape,
        scratch_shapes=scratch,
        input_output_aliases=aliases or {},
        compiler_params=pltpu.CompilerParams(vmem_limit_bytes=VMEM_LIMIT),
        cost_estimate=pl.CostEstimate(
            flops=int(micros * SCALE), bytes_accessed=0, transcendentals=0
        ),
        **specs,
    )


class Grid:
    names = ("zh", "zl", "y", "x", "c")

    def __init__(self, mesh):
        experts, heads = mesh.shape["expert"], mesh.shape["head"]
        self.shape = (2, experts // 4, 2, heads // 2, 2)
        self.experts, self.heads = experts, heads
        self.total = experts * heads

    def size(self, name):
        return self.shape[self.names.index(name)]

    def coords(self, linear):
        out = []
        for extent in reversed(self.shape):
            out.append(linear % extent)
            linear = linear // extent
        return dict(zip(self.names, reversed(out)))

    def linear(self, coords):
        at = 0
        for name, extent in zip(self.names, self.shape):
            at = at * extent + coords[name] % extent
        return at

    def me(self, name):
        linear = lax.axis_index("expert") * self.heads + lax.axis_index("head")
        return self.coords(linear)[name]

    def send(self, value, target):
        pairs = [(i, self.linear(target(self.coords(i)))) for i in range(self.total)]
        return lax.ppermute(value, ("expert", "head"), pairs)

    def move(self, value, **by):
        return self.send(value, lambda at: {name: at[name] - by.get(name, 0) for name in at})

    def shift(self, value, name, by):
        return self.move(value, **{name: by})

    def exchange(self, value, name, *others):
        stride = self.linear({**dict.fromkeys(self.names, 0), name: 1}) // self.heads
        groups = [[at, at + stride] for at in range(self.experts) if at // stride % 2 == 0]
        both = jnp.broadcast_to(value[None], (2, *value.shape))
        both = lax.all_to_all(
            both, "expert", split_axis=0, concat_axis=0, tiled=True, axis_index_groups=groups
        )
        both = after(both, *others) if others else both
        return jnp.where(self.me(name) == 0, both[1], both[0])

    def gather(self, value, name, *others):
        extent, own = self.size(name), self.me(name)
        parts = [value] + [self.shift(value, name, by) for by in range(1, extent)]
        if others:
            parts[1] = after(parts[1], *others)
        if extent == 2:
            return jnp.where(own == 0, jnp.stack(parts), jnp.stack(parts[::-1]))
        return jnp.roll(jnp.stack(parts), own, axis=0)

    def scatter_sum(self, value, name, *waited):
        extent, own = self.size(name), self.me(name)
        if extent == 2:
            kept = jnp.where(own == 0, value[0], value[1])
            others = [self.shift(jnp.where(own == 0, value[1], value[0]), name, 1)]
        else:
            value = jnp.roll(value, -own, axis=0)
            kept = value[0]
            others = [self.shift(value[by], name, -by) for by in range(1, extent)]
        if waited:
            others[0] = after(others[0], *waited)
        total = kept.astype(single)
        for other in others:
            total = total + other.astype(single)
        return total.astype(value.dtype)


def after(value, *others):
    return lax.optimization_barrier((value, *others))[0]


def per_device(
    grid,
    tokens,
    segment_ids,
    task_ids,
    task_table,
    weight_qkv,
    weight_out,
    gain_one,
    gain_two,
    weight_router,
    weight_in,
    weight_hidden,
    cotangent,
):
    expert_count, head_count = grid.experts, grid.heads
    head_index = lax.axis_index("head")
    row_count, model_width = tokens.shape
    cap = 4 * row_count // expert_count
    deep, wide = weight_qkv.shape[1:]
    padded = -(-expert_count // 16) * 16

    pieces = jnp.concatenate([weight_qkv, weight_out.T[None]]).astype(bfloat)
    small = jnp.concatenate(
        [gain_one[None], gain_two[None], weight_router.T]
    ).astype(bfloat).reshape(-1)
    small_rows = -(-small.shape[0] // wide)
    small = jnp.pad(small, (0, small_rows * wide - small.shape[0])).reshape(small_rows, wide)
    packed = jnp.concatenate([pieces.reshape(4 * deep, wide), small])
    own_segments = lax.dynamic_slice_in_dim(segment_ids, head_index * row_count, row_count)
    shape = jax.ShapeDtypeStruct
    vmem, hbm = pl.BlockSpec(memory_space=pltpu.VMEM), pl.BlockSpec(memory_space=pl.ANY)
    smem = pl.BlockSpec(memory_space=pltpu.SMEM)
    table = jnp.pad(task_table.T, ((0, 16 - task_table.shape[1]), (0, 0))).astype(bfloat)
    hidden = weight_in.shape[2]
    deep_in = weight_in.shape[1]
    piece = shape((hidden // model_width * deep_in + weight_hidden.shape[1], model_width), bfloat)
    route_rows = padded * (2 * (row_count // model_width) + 2)
    first, second, route, own_piece, sent = whole_call(
        lambda *refs: routing_kernel(cap, *refs),
        [shape((1, row_count), jnp.int32)] * 2
        + [
            shape((padded, row_count), single),
            piece,
            shape((row_count + route_rows, model_width), bfloat),
        ],
        micros=3,
    )(own_segments[None], task_ids[None], table, weight_in, weight_hidden, cotangent)
    names = {name: grid.me(name) for name in grid.names}
    extent = grid.size("zl")
    offsets = [(dl, dy) for dl in range(extent) for dy in range(2)]
    offsets.sort(key=lambda by: by[0] * by[1] != 0)
    providers = len(offsets)

    def expert_of(zl, y, local):
        return ((names["zh"] + local) % 2 * extent + zl % extent) * 2 + y % 2

    def ints(*values):
        return jnp.concatenate([jnp.asarray(v, jnp.int32).reshape(-1) for v in values])

    targets = ints(
        *[expert_of(names["zl"] - dl, names["y"] - dy, k) for dl, dy in offsets for k in range(2)],
        names["c"],
    )
    parcel = shape((2 * cap + EXTRA, model_width), bfloat)
    packed = grid.gather(grid.gather(packed, "zh"), "zl")
    nearly = packed
    packed = grid.gather(packed, "y")
    smalls = packed.transpose(2, 1, 0, 3, 4).reshape(expert_count, -1)[:, 4 * deep * wide :]
    smalls = smalls[:, : (2 + expert_count) * deep].reshape(expert_count, 2 + expert_count, deep)
    smalls = smalls.transpose(1, 0, 2).reshape(2 + expert_count, model_width)
    gain1, gain2 = smalls[0:1].astype(single), smalls[1:2].astype(single)
    router = jnp.pad(smalls[2:], ((0, padded - expert_count), (0, 0)))
    packed = grid.gather(packed[..., : 4 * deep, :], "x")
    packed = packed.reshape(*packed.shape[:4], 4, deep, wide)
    if wide % LANES:
        packed = grid.gather(packed, "c").transpose(5, 4, 3, 2, 6, 1, 0, 7)
        packed = packed.reshape(4, model_width, model_width)
        weights = (packed, packed)
    else:
        weights = (packed, grid.shift(packed, "c", 1))

    segc = own_segments[:, None]
    segr = own_segments[None]

    core = ints(names["c"])
    gate_rows = 2 * padded * (row_count // model_width)
    proj, attn, res, two_low, stat, gate, weights = whole_call(
        forward_kernel,
        [
            shape((3, row_count, model_width), bfloat),
            shape((row_count, model_width), bfloat),
            shape((row_count, model_width), single),
            shape((row_count + gate_rows, model_width), bfloat),
            shape((model_width // HDIM, row_count), single),
            shape((padded, row_count), single),
            shape((4, model_width, model_width), bfloat),
        ],
        in_specs=[smem, vmem, hbm, hbm] + [vmem] * 7,
        out_specs=[hbm] * 5 + [vmem, hbm],
        scratch=[
            pltpu.VMEM((3, row_count, model_width), bfloat),
            pltpu.VMEM((row_count, model_width), bfloat),
            pltpu.VMEM((row_count, model_width), single),
            pltpu.VMEM((row_count + gate_rows, model_width), bfloat),
            pltpu.VMEM((model_width // HDIM, row_count), single),
            pltpu.VMEM((4, model_width, model_width), bfloat),
            pltpu.SemaphoreType.DMA((2, head_count // 2 * expert_count)),
            pltpu.SemaphoreType.DMA((5, max(4, row_count // BLOCK))),
        ],
        micros=0.2,
    )(core, tokens, *weights, gain1, gain2, router, segc, segr, first, second)

    own_piece = after(own_piece, nearly)
    pieces = {(0, 0, 0): own_piece, (1, 0, 0): grid.exchange(own_piece, "zh")}
    for by_x in range(1, head_count // 2):
        pieces[0, by_x, 0] = grid.shift(own_piece, "x", by_x)
    own_experts = [expert_of(names["zl"], names["y"], local) for local in range(2)]
    sent = after(sent, nearly)
    cots = {(dl, 0): grid.move(sent, zl=dl) if dl else sent for dl in range(extent)}
    cots[0, 1] = grid.move(sent, y=1)
    pieces[1, 0, 0] = after(pieces[1, 0, 0], two_low)
    rows = {(dl, 0): grid.move(two_low, zl=dl) if dl else two_low for dl in range(extent)}
    rows[0, 1] = grid.move(two_low, y=1)
    for dl in range(1, extent):
        rows[dl, 1] = grid.move(two_low, zl=dl, y=1)
        cots[dl, 1] = grid.move(cots[dl, 0], y=1)
    for by_x in range(1, head_count // 2):
        pieces[1, by_x, 0] = grid.shift(after(pieces[1, 0, 0], cots[0, 1]), "x", by_x)
    for by_x in range(head_count // 2):
        pieces[0, by_x, 0] = after(pieces[0, by_x, 0], two_low)
        pieces[0, by_x, 1] = grid.shift(pieces[0, by_x, 0], "c", 1)
    piece_keys = [(k, bx, bc) for k in range(2) for bx in range(head_count // 2) for bc in range(2)]

    calls = [{0: (0,)}, {0: (1,), 1: (0, 1)}] + [{at: (0, 1)} for at in range(2, min(4, providers))]
    for at in range(4, providers, 3):
        calls.append({s: (0, 1) for s in range(at, min(at + 3, providers))})
    save_tiles = sum(-(-len(call) * cap // TILE) for call in calls)
    save_shapes = [
        shape((2, save_tiles * TILE, cols), bfloat)
        for cols in (model_width, model_width, hidden, hidden)
    ]
    saved = []
    tiles_before = jnp.zeros((2,), jnp.int32)
    results = {}
    left = len(calls)
    for call in calls:
        left -= 1
        group = list(call)
        count = len(group)
        needed = sorted({local for work in call.values() for local in work})
        carried = [results[s] for s in group if s in results]
        carried = [value for both in carried for value in both]
        held_pieces = [pieces[key] for key in piece_keys if key[0] in needed]
        keys = [offsets[s] for s in group]
        inputs = [ints(names["x"], names["c"], *own_experts), tiles_before]
        inputs += [rows[key] for key in keys] + [cots[key] for key in keys]
        inputs += carried + held_pieces + saved
        before = 2 + 2 * count + len(carried) + len(held_pieces)
        outs = whole_call(
            lambda *refs, work=tuple(call.values()), fresh=not carried, new=not saved: expert_kernel(
                work, head_count, cap, row_count, padded, fresh, new, *refs
            ),
            save_shapes + [parcel] * (2 * count) + [shape((2,), jnp.int32)],
            in_specs=[smem, smem]
            + [hbm] * (2 * count + len(carried) + len(held_pieces) + len(saved)),
            out_specs=[hbm] * (4 + 2 * count) + [smem],
            aliases={before + i: i for i in range(len(saved))},
            scratch=[
                pltpu.VMEM((2, model_width, hidden), bfloat),
                pltpu.VMEM((2, hidden, model_width), bfloat),
                pltpu.VMEM((count, row_count + gate_rows, model_width), bfloat),
                pltpu.VMEM((count, *sent.shape), bfloat),
                pltpu.VMEM((count, 2 * cap, model_width), bfloat),
                pltpu.VMEM((count, 2 * cap, model_width), bfloat),
                pltpu.VMEM((count, 2 * cap, 1), single),
                pltpu.VMEM((count, *parcel.shape), bfloat),
                pltpu.VMEM((count, *parcel.shape), bfloat),
                pltpu.VMEM((count, 2 * cap // HALF, HALF), single),
                pltpu.VMEM((TILE, model_width), bfloat),
                pltpu.VMEM((TILE, model_width), bfloat),
                pltpu.VMEM((TILE, 1), single),
                pltpu.VMEM((2, TILE, model_width), bfloat),
                pltpu.VMEM((2, TILE, model_width), bfloat),
                pltpu.VMEM((2, TILE, hidden), bfloat),
                pltpu.VMEM((2, TILE, hidden), bfloat),
                pltpu.SMEM((2, count * cap // HALF + 1), jnp.int32),
                pltpu.SemaphoreType.DMA((2, head_count * (hidden // model_width + 1))),
                pltpu.SemaphoreType.DMA((2, count)),
                pltpu.SemaphoreType.DMA((2, 4)),
                pltpu.SemaphoreType.DMA((2, count)),
            ],
            micros=(8, 40)[len(saved) // 4] if left > len(calls) - 3 else 16,
        )(*inputs)
        if not saved:
            near = ((0, 1), (1, 0))
            held = lax.optimization_barrier(
                (pieces, rows[0, 1], [cots[key] for key in near], outs[0])
            )
            pieces, rows[0, 1] = dict(held[0]), held[1]
            cots.update(zip(near, held[2]))
            for by_x in range(1, head_count // 2):
                ready = after(pieces[1, by_x, 0], cots[1, 0], rows[0, 1])
                pieces[1, by_x, 0] = ready
            for by_x in range(head_count // 2):
                pieces[1, by_x, 1] = grid.shift(pieces[1, by_x, 0], "c", 1)
        if len(calls) - left == 2:
            for dl in range(1, extent):
                rows[dl, 0] = after(rows[dl, 0], outs[0])
        saved, tiles_before = list(outs[:4]), outs[-1]
        for i, s in enumerate(group):
            results[s] = [outs[4 + i], outs[4 + count + i]]
    out_parcels, grad_parcels = [], []
    for s, (dl, dy) in enumerate(offsets):
        out_part, grad_part = results[s]
        if dl and dy:
            grad_part = after(grad_part, *grad_parcels[1:])
        if dl or dy:
            grad_part = grid.move(grad_part, zl=-dl, y=-dy)
            out_part = after(out_part, saved[0])
            if not (dl and dy):
                out_part = grid.move(out_part, zl=-dl, y=-dy)
        out_parcels.append(out_part)
        grad_parcels.append(grad_part)
    waited = []
    halves = [
        shape((hidden // model_width * deep_in, model_width), bfloat),
        shape((weight_hidden.shape[1], model_width), bfloat),
    ]
    done = whole_call(
        lambda *refs: weight_kernel(head_count, len(waited), *refs),
        [s for key in piece_keys for s in (halves if all(key) else [piece])],
        in_specs=[smem, smem] + [hbm] * (4 + len(waited)),
        scratch=[
            pltpu.VMEM((model_width, hidden), single),
            pltpu.VMEM((model_width, hidden), single),
            pltpu.VMEM((2, TILE, model_width), bfloat),
            pltpu.VMEM((2, TILE, model_width), bfloat),
            pltpu.VMEM((2, TILE, hidden), bfloat),
            pltpu.VMEM((2, TILE, hidden), bfloat),
            pltpu.SemaphoreType.DMA((2, 4)),
        ],
        micros=1,
    )(ints(names["x"], names["c"]), tiles_before, *saved, *waited)
    done, grad_parcels = lax.optimization_barrier((done, grad_parcels))
    out_parcels = [
        grid.move(after(value, done[0]), zl=-dl, y=-dy) if dl and dy else value
        for value, (dl, dy) in zip(out_parcels, offsets)
    ]
    done = list(done)
    grads = {
        key: [done.pop(0) for _ in halves] if all(key) else done.pop(0) for key in piece_keys
    }

    def add(kept, other):
        return (kept.astype(single) + other.astype(single)).astype(bfloat)

    crossed = {}
    for key in piece_keys:
        if key[2] == 0:
            other = grads[key[0], key[1], 1]
            parts = other if isinstance(other, list) else [other]
            parts = [grid.shift(part, "c", -1) for part in parts]
            crossed[key] = jnp.concatenate(parts) if len(parts) > 1 else parts[0]
    for by_x in range(1, head_count // 2):
        grads[1, by_x, 0] = add(grads[1, by_x, 0], crossed.pop((1, by_x, 0)))
    waited = []
    output = whole_call(
        lambda *refs: output_kernel(providers, cap, *refs),
        shape((row_count, model_width), bfloat),
        in_specs=[smem] + [vmem] * (3 + providers),
        micros=8,
    )(targets, res, gate, route, *out_parcels)

    grad_res, grad_heads, grad_out, grad_gain2, grad_router = whole_call(
        lambda *refs: middle_kernel(providers, cap, len(waited), *refs),
        (
            shape((row_count, model_width), single),
            shape((row_count, model_width), bfloat),
            shape((model_width, model_width), bfloat),
            shape((1, model_width), single),
            shape((padded, model_width), single),
        ),
        in_specs=[smem] + [hbm] * 5 + [vmem] * 4 + [hbm] * (providers + len(waited)),
        out_specs=[hbm] * 2 + [vmem] * 3,
        scratch=[
            pltpu.VMEM((padded, row_count), single),
            pltpu.VMEM((row_count, model_width), bfloat),
            pltpu.VMEM((row_count, model_width), single),
            pltpu.VMEM((row_count, model_width), bfloat),
            pltpu.VMEM((row_count, model_width), bfloat),
            pltpu.VMEM((row_count, model_width), single),
            pltpu.VMEM((row_count, model_width), bfloat),
            pltpu.VMEM((row_count, model_width), bfloat),
            pltpu.VMEM((model_width, model_width), bfloat),
            pltpu.VMEM((providers, *parcel.shape), bfloat),
            pltpu.SemaphoreType.DMA((providers + 5,)),
            pltpu.SemaphoreType.DMA((2, row_count // CHUNK)),
        ],
        micros=4,
    )(
        targets, cotangent, res, two_low, attn, weights, gain2, router, gate, route,
        *grad_parcels, *waited,
    )
    for key, other in crossed.items():
        grads[key] = add(grads[key], after(other, grad_gain2))
    for by_x in range(1, head_count // 2):
        other = after(grid.shift(grads[1, by_x, 0], "x", -by_x), grad_gain2)
        grads[1, 0, 0] = add(grads[1, 0, 0], other)
    grad_res = after(grad_res, grads[1, 0, 0], grads[0, 1, 0], *out_parcels[1:-1])
    columns = model_width if wide % LANES else model_width // 2
    grad_tokens, grad_own, other_top, other_rest, grad_gain1 = whole_call(
        lambda *refs: backward_kernel(head_count, *refs),
        (
            shape((row_count, model_width), single),
            shape((4, model_width, columns), bfloat),
            shape((2, model_width, columns), bfloat),
            shape((2, model_width, columns), bfloat),
            shape((1, model_width), single),
        ),
        in_specs=[smem] + [vmem] * 3 + [hbm] * 7,
        out_specs=[hbm] + [vmem] * 4,
        scratch=[
            pltpu.VMEM((3, row_count, model_width), bfloat),
            pltpu.VMEM((row_count, model_width), single),
            pltpu.VMEM((row_count, model_width), single),
            pltpu.VMEM((row_count, model_width), bfloat),
            pltpu.VMEM((4, model_width, model_width), bfloat),
            pltpu.VMEM((3, row_count, model_width), bfloat),
            pltpu.VMEM((row_count, model_width), bfloat),
            pltpu.VMEM((model_width // HDIM, row_count), single),
            pltpu.VMEM((row_count, model_width), bfloat),
            pltpu.VMEM((row_count, model_width), single),
            pltpu.VMEM((3, model_width, model_width), bfloat),
            pltpu.VMEM((row_count, model_width), single),
            pltpu.SemaphoreType.DMA((7,)),
            pltpu.SemaphoreType.DMA((row_count // CHUNK,)),
        ],
        micros=1,
    )(
        core, gain1, segc, segr, proj, grad_heads, stat, tokens, grad_res, weights, grad_out,
    )

    for by_x in range(1, head_count // 2):
        other = after(grid.shift(grads[0, by_x, 0], "x", -by_x), grad_tokens)
        grads[0, 0, 0] = add(grads[0, 0, 0], other)
    smalls = jnp.concatenate([grad_gain1, grad_gain2, grad_router[:expert_count]]).astype(bfloat)
    ahead = [grads[0, 0, 0], *out_parcels[3:]]
    if wide % LANES or grid.size("x") != 2:
        if wide % LANES:
            packed = grad_own.reshape(4, model_width, -1, 2, wide).transpose(3, 0, 1, 2, 4)
            packed = grid.scatter_sum(packed, "c").reshape(4, model_width, -1)
        else:
            other = [grid.shift(v, "c", 1) for v in (other_top, other_rest)]
            packed = add(grad_own, jnp.concatenate(other))
        packed = packed.reshape(4, model_width, -1, wide).transpose(2, 0, 1, 3)
        packed = grid.scatter_sum(after(packed, *ahead), "x", output)
    else:
        other = [grid.shift(v, "c", 1) for v in (other_top, other_rest)]
        other = lax.optimization_barrier((*other, *ahead))[:2]

        def columns_of(x):
            def pick(value):
                return jnp.where(x == 0, value[..., :wide], value[..., wide:]).astype(single)

            both = zip((grad_own[:2], grad_own[2:]), other)
            return jnp.concatenate([pick(kept) + pick(crossed_in) for kept, crossed_in in both])

        got = grid.shift(columns_of(1 - names["x"]).astype(bfloat), "x", 1)
        packed = columns_of(names["x"]) + after(got, output).astype(single)
        packed = packed.astype(bfloat)
    grad_piece = grads[0, 0, 0].astype(single) + grid.exchange(
        grads[1, 0, 0], "zh", packed
    ).astype(single)
    grad_in_own = grad_piece[: hidden // model_width * deep_in]
    grad_in_own = grad_in_own.reshape(-1, deep_in, model_width).transpose(1, 0, 2)
    grad_in_own = grad_in_own.reshape(1, deep_in, hidden)
    grad_hidden_own = grad_piece[hidden // model_width * deep_in :][None]
    for name in ("c", "x"):
        total = smalls.astype(single)
        for by in range(1, grid.size(name)):
            total = total + grid.shift(smalls, name, by).astype(single)
        smalls = total.astype(bfloat)
    smalls = smalls.reshape(2 + expert_count, expert_count, deep).transpose(1, 0, 2)
    smalls = smalls.reshape(expert_count, -1)
    smalls = jnp.pad(smalls, ((0, 0), (0, small_rows * wide - smalls.shape[1])))
    packed = packed.reshape(4, expert_count, deep, wide).transpose(1, 0, 2, 3)
    packed = packed.reshape(expert_count, 4 * deep, wide)
    packed = jnp.concatenate([packed, smalls.reshape(expert_count, small_rows, wide)], axis=1)
    packed = packed.reshape(*grid.shape[:3], 4 * deep + small_rows, wide).transpose(2, 1, 0, 3, 4)
    packed = after(packed, grad_piece)
    for name in ("y", "zl", "zh"):
        packed = grid.scatter_sum(packed, name)
    pieces = packed[: 4 * deep].reshape(4, deep, wide).astype(single)
    smalls = packed[4 * deep :].reshape(-1)[: (2 + expert_count) * deep].astype(single)
    smalls = smalls.reshape(2 + expert_count, deep)
    return (
        output,
        grad_tokens,
        pieces[:3],
        pieces[3].T,
        smalls[0],
        smalls[1],
        smalls[2:].T,
        grad_in_own,
        grad_hidden_own,
    )


def solution(mesh):
    grid = Grid(mesh)
    placed = (
        P(("expert", "head"), None),
        P("expert"),
        P(),
        P(),
        P(None, "expert", "head"),
        P("head", "expert"),
        P("expert"),
        P("expert"),
        P("expert", None),
        P("expert", "head", None),
        P("expert", "head", None),
        P(("expert", "head"), None),
    )

    def step(*arrays):
        return per_device(grid, *arrays)

    return jax.shard_map(
        step,
        mesh=mesh,
        in_specs=placed,
        out_specs=(
            P(("expert", "head"), None),
            P(("expert", "head"), None),
            P(None, "expert", "head"),
            P("head", "expert"),
            P("expert"),
            P("expert"),
            P("expert", None),
            P("expert", "head", None),
            P("expert", "head", None),
        ),
        check_vma=False,
    )
```

```python
import jax
import jax.numpy as jnp
from jax import lax
from jax.experimental import pallas as pl
from jax.experimental.pallas import tpu as pltpu
from jax.sharding import PartitionSpec as P

HDIM = 64
PACK = 1024
SPAN = 64
BLOCK = 128
WINDOW = BLOCK + 2 * SPAN
CHUNK = 256
LANES = 128
TILE = 256
HALF = 64
EXTRA = 16
PART = 256
ABSENT = -1e6
SCALE = 1153e6 / 8

EPSILON = 1e-05
NEGATIVE = -1e30

bfloat = jnp.bfloat16
single = jnp.float32
VMEM_LIMIT = 56 * 1024 * 1024


def dot_nn(a, b):
    return lax.dot_general(a, b, (((1,), (0,)), ((), ())), preferred_element_type=single)


def dot_nt(a, b):
    return lax.dot_general(a, b, (((1,), (1,)), ((), ())), preferred_element_type=single)


def dot_tn(a, b):
    return lax.dot_general(a, b, (((0,), (0,)), ((), ())), preferred_element_type=single)


def normalise(values):
    centered = values - jnp.mean(values, axis=-1, keepdims=True)
    inverse = lax.rsqrt(jnp.mean(centered * centered, axis=-1, keepdims=True) + EPSILON)
    return centered * inverse, inverse


def norm_pull(grad_normed, scaled, inverse, gain):
    weighted = grad_normed * gain
    return inverse * (
        weighted
        - jnp.mean(weighted, axis=-1, keepdims=True)
        - scaled * jnp.mean(weighted * scaled, axis=-1, keepdims=True)
    )


def split_heads(pair, first_half):
    zero = jnp.zeros_like(pair)
    return jnp.concatenate(
        [jnp.where(first_half, pair, zero), jnp.where(first_half, zero, pair)], axis=0
    )


def segment_bias(segc, segr, q_at, k_at):
    bias = jnp.where(segc[k_at, :] == segr[:, q_at], 0.0, NEGATIVE)
    return jnp.concatenate([bias, bias], axis=1)


def window_start(block, rows):
    return pl.multiple_of(jnp.clip(block * BLOCK - SPAN, 0, rows - WINDOW), SPAN)


def fetch_weights(core, own, other, weights, sem):
    copies = []
    if own.shape == weights.shape:
        copies = [pltpu.make_async_copy(own, weights, sem.at[0, 0])]
    else:
        parts_x, parts_y, parts_zl, parts_zh, _, deep, wide = own.shape
        places = [
            (x, y, zl, zh)
            for x in range(parts_x)
            for y in range(parts_y)
            for zl in range(parts_zl)
            for zh in range(parts_zh)
        ]
        for at, (x, y, zl, zh) in enumerate(places):
            row = ((zh * parts_zl + zl) * parts_y + y) * deep
            for i, (ref, half) in enumerate(((own, core), (other, 1 - core))):
                start = pl.multiple_of((2 * x + half) * wide, LANES)
                copies.append(
                    pltpu.make_async_copy(
                        ref.at[x, y, zl, zh],
                        weights.at[:, pl.ds(row, deep), pl.ds(start, wide)],
                        sem.at[i, at],
                    )
                )
    for copy in copies:
        copy.start()
    for copy in copies:
        copy.wait()


def forward_kernel(
    meta, tok, weights_own, weights_other, gain1, gain2, router, segc, segr, first, second,
    proj_out, attn_out, res_out, two_out, stat_out, gate, weights_out,
    proj, attn, res, two, stat, weights, sem, out_sem,
):
    rows, width = tok.shape
    fetch_weights(meta[0], weights_own, weights_other, weights, sem)
    wqkv, wot = weights, weights.at[3]
    leaving = [pltpu.make_async_copy(weights, weights_out, out_sem.at[0, 0])]
    leaving[0].start()

    def project(step, carry):
        at = pl.ds(pl.multiple_of(step * CHUNK, CHUNK), CHUNK)
        scaled, _ = normalise(tok[at, :].astype(single))
        low = (scaled * gain1[...]).astype(bfloat)
        for part in range(3):
            proj[part, at, :] = dot_nn(low, wqkv[part]).astype(bfloat)
        return carry

    lax.fori_loop(0, rows // CHUNK, project, 0)
    leaving.append(pltpu.make_async_copy(proj, proj_out, out_sem.at[0, 1]))
    leaving[1].start()

    def block_copies(block):
        at = pl.ds(pl.multiple_of(block * BLOCK, BLOCK), BLOCK)
        return [
            pltpu.make_async_copy(held.at[at, :], out.at[at, :], out_sem.at[1 + i, block])
            for i, (held, out) in enumerate(
                ((attn, attn_out), (res, res_out), (two, two_out))
            )
        ]

    lane = lax.broadcasted_iota(jnp.int32, (BLOCK, LANES), 1)
    first_half = lane < HDIM
    expert = lax.broadcasted_iota(jnp.int32, (router.shape[0], BLOCK), 0)

    def attend(block, carry):
        q_at = pl.ds(pl.multiple_of(block * BLOCK, BLOCK), BLOCK)
        k_at = pl.ds(window_start(block, rows), WINDOW)
        bias = segment_bias(segc, segr, q_at, k_at)
        for pair in range(width // LANES):
            cols = slice(pair * LANES, (pair + 1) * LANES)
            queries = split_heads(proj[0, q_at, cols] * HDIM**-0.5, first_half)
            scores = dot_nt(proj[1, k_at, cols], queries) + bias
            peak = jnp.max(scores, axis=0, keepdims=True)
            exponent = jnp.exp(scores - peak)
            total = jnp.sum(exponent, axis=0, keepdims=True)
            probs = (exponent * (1.0 / total)).astype(bfloat)
            out = dot_tn(probs, proj[2, k_at, cols])
            attn[q_at, cols] = jnp.where(first_half, out[:BLOCK], out[BLOCK:]).astype(bfloat)
            log_total = peak + jnp.log(total)
            stat[2 * pair : 2 * pair + 1, q_at] = log_total[:, :BLOCK]
            stat[2 * pair + 1 : 2 * pair + 2, q_at] = log_total[:, BLOCK:]
        residual = tok[q_at, :].astype(single) + dot_nt(attn[q_at, :], wot[...])
        res[q_at, :] = residual
        scaled, _ = normalise(residual)
        low = (scaled * gain2[...]).astype(bfloat)
        two[q_at, :] = low
        logits = dot_nt(router[...], low)
        mark0 = first[:, q_at] == expert
        mark1 = second[:, q_at] == expert
        logit0 = jnp.sum(jnp.where(mark0, logits, 0.0), axis=0, keepdims=True)
        logit1 = jnp.sum(jnp.where(mark1, logits, 0.0), axis=0, keepdims=True)
        top = jnp.maximum(logit0, logit1)
        part0, part1 = jnp.exp(logit0 - top), jnp.exp(logit1 - top)
        scale = 1.0 / (part0 + part1)
        gate[:, q_at] = jnp.where(mark0, part0 * scale, jnp.where(mark1, part1 * scale, 0.0))
        for copy in block_copies(block):
            copy.start()
        return carry

    lax.fori_loop(0, rows // BLOCK, attend, 0)
    count = gate.shape[0]
    at = rows
    for part in split_two(gate[...]):
        for start in range(0, rows, width):
            two[at : at + count, :] = part[:, start : start + width]
            at += count
    leaving.append(pltpu.make_async_copy(stat, stat_out, out_sem.at[0, 3]))
    leaving[2].start()
    rest = pl.ds(rows, two.shape[0] - rows)
    leaving.append(
        pltpu.make_async_copy(two.at[rest, :], two_out.at[rest, :], out_sem.at[0, 2])
    )
    leaving[3].start()
    for copy in leaving:
        copy.wait()

    def settle(block, carry):
        for copy in block_copies(block):
            copy.wait()
        return carry

    lax.fori_loop(0, rows // BLOCK, settle, 0)


def split_two(values):
    high = values.astype(bfloat)
    return high, (values - high.astype(single)).astype(bfloat)


def pack_rows(rows):
    at = lax.broadcasted_iota(jnp.int32, (EXTRA, rows.shape[1]), 0)
    out = jnp.zeros((EXTRA, rows.shape[1]), single)
    for local in range(2):
        high = rows[local : local + 1, :].astype(bfloat).astype(single)
        out = jnp.where(at == 2 * local, high, out)
        out = jnp.where(at == 2 * local + 1, rows[local : local + 1, :] - high, out)
    return out.astype(bfloat)


def unpack_row(packed, local):
    packed = packed.astype(single)
    return packed[2 * local : 2 * local + 1, :] + packed[2 * local + 1 : 2 * local + 2, :]


def routing_kernel(
    cap, segments, tasks, table, weight_in, weight_hidden, cot,
    first, second, route, piece, sent,
):
    rows = segments.shape[1]
    deep, hidden = weight_in.shape[1:]
    width = piece.shape[1]
    for part in range(hidden // width):
        piece[part * deep : (part + 1) * deep, :] = weight_in[
            0, :, part * width : (part + 1) * width
        ].astype(bfloat)
    piece[hidden // width * deep :, :] = weight_hidden[0].astype(bfloat)
    names = lax.broadcasted_iota(jnp.int32, (table.shape[1], tasks.shape[1]), 0)
    experts = dot_nn(table[...], jnp.where(names == tasks[...], 1.0, 0.0).astype(bfloat))
    experts = experts.astype(bfloat)
    chosen = jnp.zeros((table.shape[0], rows), single)
    for start in range(0, tasks.shape[1], 1024):
        size = min(1024, tasks.shape[1] - start)
        at = lax.broadcasted_iota(jnp.int32, (size, rows), 0) + start
        ones = jnp.where(at == segments[...], 1.0, 0.0).astype(bfloat)
        chosen = chosen + dot_nn(experts[:, start : start + size], ones)
    zero, one = chosen[0:1, :], chosen[1:2, :]
    first[...] = zero.astype(jnp.int32)
    second[...] = one.astype(jnp.int32)
    which = lax.broadcasted_iota(jnp.int32, route.shape, 0).astype(single)
    is_first, is_second = which == zero, which == one
    marks = jnp.where(is_first | is_second, 1.0, 0.0)
    earlier = lax.broadcasted_iota(jnp.int32, (rows, rows), 0) < lax.broadcasted_iota(
        jnp.int32, (rows, rows), 1
    )
    places = dot_nn(marks.astype(bfloat), jnp.where(earlier, 1.0, 0.0).astype(bfloat))
    inside = (marks > 0.5) & (places < cap)
    slots = jnp.where(inside, places, ABSENT)
    route[...] = slots
    total = jnp.sum(jnp.where(inside, 1.0, 0.0), axis=1, keepdims=True)
    total = jnp.broadcast_to(total, (route.shape[0], width))
    sent[:rows, :] = cot[...]
    at = rows
    for part in range(2):
        for start in range(0, rows, width):
            sent[at : at + route.shape[0], :] = sixteens(slots[:, start : start + width])[part]
            at += route.shape[0]
    for part in range(2):
        sent[at : at + route.shape[0], :] = sixteens(total)[part]
        at += route.shape[0]


def sixteens(values):
    high = jnp.floor(values * 0.0625) * 16.0
    high = jnp.where(values < 0.0, values, high)
    return high.astype(bfloat), jnp.where(values < 0.0, 0.0, values - high).astype(bfloat)


def output_kernel(providers, cap, meta, res, gate, slots, *refs):
    parcels, out = refs[:providers], refs[providers]
    for step in range(res.shape[0] // CHUNK):
        at = slice(step * CHUNK, (step + 1) * CHUNK)
        out[at, :] = (res[at, :] + returned_rows(parcels, cap, meta, gate, slots, at)).astype(bfloat)


def returned_rows(parcels, cap, meta, gate, slots, at):
    total = 0.0
    for provider, parcel in enumerate(parcels):
        for local in range(2):
            chosen = pl.ds(meta[2 * provider + local], 1)
            ones = onehot(slots[chosen, at], 0, cap, gate[chosen, at])
            total = total + dot_tn(ones, parcel[local * cap : (local + 1) * cap, :])
    return total


def middle_kernel(
    providers, cap, waited, meta,
    cot_in, res_in, two_in, attn_in, weights_in, gain2, router, gate, slots,
    *refs,
):
    parcels = refs[:providers]
    (
        res_left, heads_left, grad_out, grad_gain2, grad_router,
        products, grad_attn, grad_res, grad_heads, cot, res, two, attn, wot, parcel_bufs, sem, out_sem,
    ) = refs[providers + waited :]
    rows, width = cot.shape
    two_rows = two_in.at[pl.ds(0, rows), :]
    arriving = [
        pltpu.make_async_copy(given, held, sem.at[i])
        for i, (given, held) in enumerate(
            [(parcel, parcel_bufs.at[at]) for at, parcel in enumerate(parcels)]
            + [(res_in, res), (cot_in, cot), (weights_in.at[3], wot), (two_rows, two), (attn_in, attn)]
        )
    ]
    for copy in arriving:
        copy.start()
    parcels = [parcel_bufs.at[at] for at in range(providers)]
    for copy in arriving[:providers]:
        copy.wait()
    products[...] = jnp.zeros_like(products)
    for provider in range(providers):
        for local in range(2):
            chosen = meta[2 * provider + local]
            ones = onehot(slots[pl.ds(chosen, 1), :], 0, cap)
            moved = dot_nn(parcels[provider][2 * cap :, :cap], ones)
            products[pl.ds(chosen, 1), :] = unpack_row(moved, local)
    gates = gate[...]
    inner_products = products[...]
    grad_logits = gates * (
        inner_products - jnp.sum(gates * inner_products, axis=0, keepdims=True)
    )
    grad_logits = jnp.concatenate(split_two(grad_logits), axis=0)
    router_twice = jnp.concatenate([router[...], router[...]], axis=0)
    count = router.shape[0]
    grad_gain2[...] = jnp.zeros_like(grad_gain2)
    for copy in arriving[providers : providers + 3]:
        copy.wait()
    leaving = []
    for step in range(rows // CHUNK):
        at = slice(step * CHUNK, (step + 1) * CHUNK)
        scaled, inverse = normalise(res[at, :])
        grad_normed = dot_tn(grad_logits[:, at], router_twice)
        grad_normed = grad_normed + returned_rows(parcels, cap, meta, gate, slots, at)
        grad_gain2[...] += jnp.sum(grad_normed * scaled, axis=0, keepdims=True)
        grad_row = cot[at, :].astype(single) + norm_pull(grad_normed, scaled, inverse, gain2[...])
        grad_res[at, :] = grad_row
        low = grad_row.astype(bfloat)
        grad_attn[at, :] = low
        grad_heads[at, :] = dot_nn(low, wot[...]).astype(bfloat)
        part = pl.ds(step * CHUNK, CHUNK)
        for i, (held, out) in enumerate(((grad_res, res_left), (grad_heads, heads_left))):
            leaving.append(
                pltpu.make_async_copy(held.at[part, :], out.at[part, :], out_sem.at[i, step])
            )
            leaving[-1].start()
    for copy in arriving[providers + 3 :]:
        copy.wait()
    routed = dot_nn(grad_logits, two[...])
    grad_router[...] = routed[:count] + routed[count:]
    grad_out[...] = dot_tn(grad_attn[...], attn[...]).astype(bfloat)
    for copy in leaving:
        copy.wait()


def backward_kernel(
    heads, core, gain1, segc, segr,
    proj_in, heads_in, stat_in, tok_in, res_in, weights_in, out_in,
    tok_left, grad_own, other_top, other_rest, grad_gain1,
    grad_proj, grad_key, grad_value, normed, grad_w,
    proj, grad_heads, stat, tok, grad_res, wqkv, grad_tok, sem, out_sem,
):
    rows, width = tok.shape
    arriving = [
        pltpu.make_async_copy(given, held, sem.at[i])
        for i, (given, held) in enumerate(
            (
                (proj_in, proj), (heads_in, grad_heads), (stat_in, stat), (tok_in, tok),
                (res_in, grad_res), (weights_in.at[pl.ds(0, 3)], wqkv), (out_in, grad_w.at[3]),
            )
        )
    ]
    for copy in arriving:
        copy.start()
    grad_gain1[...] = jnp.zeros_like(grad_gain1)
    grad_key[...] = jnp.zeros_like(grad_key)
    grad_value[...] = jnp.zeros_like(grad_value)
    for copy in arriving[:3]:
        copy.wait()
    lane = lax.broadcasted_iota(jnp.int32, (BLOCK, LANES), 1)
    first_half = lane < HDIM

    def attend(block, carry):
        q_at = pl.ds(pl.multiple_of(block * BLOCK, BLOCK), BLOCK)
        k_at = pl.ds(window_start(block, rows), WINDOW)
        bias = segment_bias(segc, segr, q_at, k_at)
        for pair in range(width // LANES):
            cols = slice(pair * LANES, (pair + 1) * LANES)
            queries = split_heads(proj[0, q_at, cols] * HDIM**-0.5, first_half)
            keys_block = proj[1, k_at, cols]
            log_total = jnp.concatenate(
                [stat[2 * pair + half : 2 * pair + half + 1, q_at] for half in range(2)], axis=1
            )
            probs = jnp.exp(dot_nt(keys_block, queries) + bias - log_total)
            heads_low = split_heads(grad_heads[q_at, cols], first_half)
            grad_probs = dot_nt(proj[2, k_at, cols], heads_low)
            delta = jnp.sum(probs * grad_probs, axis=0, keepdims=True)
            grad_scores = (probs * (grad_probs - delta)).astype(bfloat)
            grad_query = dot_tn(grad_scores, keys_block) * HDIM**-0.5
            grad_proj[0, q_at, cols] = jnp.where(
                first_half, grad_query[:BLOCK], grad_query[BLOCK:]
            ).astype(bfloat)
            grad_key[k_at, cols] += dot_nn(grad_scores, queries)
            grad_value[k_at, cols] += dot_nn(probs.astype(bfloat), heads_low)
        return carry

    lax.fori_loop(0, rows // BLOCK, attend, 0)
    for copy in arriving[3:]:
        copy.wait()
    leaving = []
    for step in range(rows // CHUNK):
        at = slice(step * CHUNK, (step + 1) * CHUNK)
        grad_proj[1, at, :] = grad_key[at, :].astype(bfloat)
        grad_proj[2, at, :] = grad_value[at, :].astype(bfloat)
        grad_normed = dot_nt(grad_proj[0, at, :], wqkv[0])
        for part in (1, 2):
            grad_normed += dot_nt(grad_proj[part, at, :], wqkv[part])
        scaled, inverse = normalise(tok[at, :].astype(single))
        normed[at, :] = (scaled * gain1[...]).astype(bfloat)
        grad_gain1[...] += jnp.sum(grad_normed * scaled, axis=0, keepdims=True)
        grad_tok[at, :] = grad_res[at, :] + norm_pull(grad_normed, scaled, inverse, gain1[...])
        part = pl.ds(step * CHUNK, CHUNK)
        leaving.append(
            pltpu.make_async_copy(grad_tok.at[part, :], tok_left.at[part, :], out_sem.at[step])
        )
        leaving[-1].start()
    for part in range(3):
        grad_w[part] = dot_tn(normed[...], grad_proj[part]).astype(bfloat)
    if grad_own.shape == grad_w.shape:
        grad_own[...] = grad_w[...]
        other_top[...] = grad_w[:2]
        other_rest[...] = grad_w[2:]
    else:
        wide = width // heads
        for by in range(heads // 2):
            cols = slice(by * wide, (by + 1) * wide)
            start = pl.multiple_of((2 * by + core[0]) * wide, LANES)
            grad_own[:, :, cols] = grad_w[:, :, pl.ds(start, wide)]
            start = pl.multiple_of((2 * by + 1 - core[0]) * wide, LANES)
            other_top[:, :, cols] = grad_w[:2, :, pl.ds(start, wide)]
            other_rest[:, :, cols] = grad_w[2:, :, pl.ds(start, wide)]
    for copy in leaving:
        copy.wait()


def onehot(slots, base, rows, marks=1.0):
    places = lax.broadcasted_iota(jnp.int32, (rows, slots.shape[1]), 0).astype(single)
    return jnp.where(places == slots - base, marks, 0.0).astype(bfloat)


def gelu_both(values):
    bent = values * (0.7978845608028654 + 0.035677408136300125 * (values * values))
    half = 0.5 * jnp.tanh(bent) + 0.5
    steep = 6.0 * bent - 3.1915382432114616 * values
    return values * half, half * (1.0 + (1.0 - half) * steep)


def expert_kernel(work, heads, cap, tokens, count, fresh, first, meta, before, *refs):
    refs = list(refs)
    sources = len(work)
    needed = sorted({local for locals_of in work for local in locals_of})

    def take(count):
        taken = refs[:count]
        del refs[:count]
        return taken

    rows_in, grads_in = take(sources), take(sources)
    carried = [] if fresh else take(2)
    pieces = take(len(needed) * heads)
    if not first:
        take(4)
    saved = take(4)
    outs, grads = take(sources), take(sources)
    (now,) = take(1)
    (
        win, wout, row_all, grad_all, row_buf, grad_buf, gate_buf,
        out_buf, copy_buf, product_buf, now_x, now_g, now_gate,
        st_x, st_g, st_act, st_pre, table, w_sem, in_sem, s_sem, out_sem,
    ) = refs
    width = row_buf.shape[2]
    hidden = wout.shape[1]
    deep, wide = width // heads, hidden // heads
    head_x, head_c = meta[0], meta[1]
    staged = (st_x, st_g, st_act, st_pre)

    def weight_copies(local):
        at = 0
        for by_x in range(heads // 2):
            for by_c in range(2):
                head = lax.rem(head_x + by_x, heads // 2) * 2 + lax.rem(head_c + by_c, 2)
                piece = pieces[(needed.index(local) * (heads // 2) + by_x) * 2 + by_c]
                for part in range(hidden // width):
                    yield pltpu.make_async_copy(
                        piece.at[pl.ds(part * deep, deep), :],
                        win.at[
                            local,
                            pl.ds(pl.multiple_of(head * deep, deep), deep),
                            pl.ds(part * width, width),
                        ],
                        w_sem.at[local, at],
                    )
                    at += 1
                yield pltpu.make_async_copy(
                    piece.at[pl.ds(hidden // width * deep, wide), :],
                    wout.at[local, pl.ds(pl.multiple_of(head * wide, wide), wide), :],
                    w_sem.at[local, at],
                )
                at += 1

    def source_copies():
        for source in range(sources):
            for i, (given, held) in enumerate(((rows_in, row_all), (grads_in, grad_all))):
                yield pltpu.make_async_copy(given[source], held.at[source], in_sem.at[i, source])

    for copy in source_copies():
        copy.start()
    for local in needed:
        for copy in weight_copies(local):
            copy.start()
    carry_copies = [
        pltpu.make_async_copy(given, held.at[0], out_sem.at[i, 0])
        for i, (given, held) in enumerate(zip(carried, (out_buf, copy_buf)))
    ]
    for copy in carry_copies:
        copy.start()
    for source in range(0 if fresh else 1, sources):
        out_buf[source] = jnp.zeros_like(out_buf[source])
        copy_buf[source] = jnp.zeros_like(copy_buf[source])
    product_buf[...] = jnp.zeros_like(product_buf)

    def save_copies(slot, local, tile):
        at = pl.ds(pl.multiple_of(tile * TILE, TILE), TILE)
        return [
            pltpu.make_async_copy(stage.at[slot], save.at[local, at, :], s_sem.at[slot, i])
            for i, (stage, save) in enumerate(zip(staged, saved))
        ]

    eye = lax.broadcasted_iota(jnp.int32, (HALF, HALF), 0) == lax.broadcasted_iota(
        jnp.int32, (HALF, HALF), 1
    )
    for copy in source_copies():
        copy.wait()
    step_rows = min(TILE, cap)
    which = lax.broadcasted_iota(jnp.int32, (count, 1), 0)
    numbers, halves = {}, []
    for local in range(2):
        number = 0
        for source in range(sources):
            if local not in work[source]:
                continue
            at = grad_all.shape[1] - 2 * count
            total = grad_all[source, at : at + count, :LANES].astype(single)
            total = total + grad_all[source, at + count :, :LANES].astype(single)
            total = jnp.max(jnp.where(which == meta[2 + local], total, 0.0)).astype(jnp.int32)
            numbers[source, local] = total
            for half in range(cap // HALF):
                table[local, number] = source * (cap // HALF) + half
                number = number + jnp.where(total > half * HALF, 1, 0)
        halves.append(number)
        now[local] = before[local] + (number + TILE // HALF - 1) // (TILE // HALF)
    places = lax.broadcasted_iota(jnp.int32, (step_rows, tokens), 0).astype(single)
    for source in range(sources):
        for local in work[source]:
            expert = meta[2 + local]

            def by_token(ref):
                row = []
                for part in range(tokens // width):
                    parts = [
                        ref[source, pl.ds(tokens + (i * (tokens // width) + part) * count, count), :]
                        for i in range(2)
                    ]
                    both = parts[0].astype(single) + parts[1].astype(single)
                    both = jnp.where(which == expert, both, 0.0)
                    row.append(jnp.sum(both, axis=0, keepdims=True))
                return jnp.concatenate(row, axis=1)

            gate_row, slot_row = by_token(row_all), by_token(grad_all)
            for step in range(cap // step_rows):

                @pl.when(numbers[source, local] > step * step_rows)
                def _():
                    at = slice(local * cap + step * step_rows, local * cap + (step + 1) * step_rows)
                    slots = slot_row - step * step_rows
                    ones = jnp.where(places == slots, 1.0, 0.0).astype(bfloat)
                    row_buf[source, at, :] = dot_nn(ones, row_all[source, :tokens, :]).astype(bfloat)
                    grad_buf[source, at, :] = dot_nn(ones, grad_all[source, :tokens, :]).astype(
                        bfloat
                    )
                    gate_buf[source, at, :] = jnp.sum(
                        jnp.where(places == slots, gate_row, 0.0), axis=1, keepdims=True
                    )

    for copy in carry_copies:
        copy.wait()
    if not fresh:
        for local in range(2):
            if local not in work[0]:
                row = unpack_row(copy_buf[0, 2 * cap :, :cap], local)
                for step in range(cap // HALF):
                    at = local * (cap // HALF) + step
                    product_buf[0, at : at + 1, :] = row[:, step * HALF : (step + 1) * HALF]
    done = 0
    for local in needed:
        for copy in weight_copies(local):
            copy.wait()
        number = halves[local]

        def place(tile, half):
            entry = table[local, (TILE // HALF) * tile + half]
            step = lax.rem(entry, cap // HALF)
            rows = pl.ds(pl.multiple_of(local * cap + step * HALF, HALF), HALF)
            return entry // (cap // HALF), rows, pl.ds(local * (cap // HALF) + step, 1)

        def one_tile(tile, done):
            slot = lax.rem(done, 2)

            @pl.when(done >= 2)
            def _():
                for copy in save_copies(slot, local, tile):
                    copy.wait()

            for half in range(TILE // HALF):
                at = pl.ds(half * HALF, HALF)

                @pl.when((TILE // HALF) * tile + half < number)
                def _():
                    source, rows, lanes = place(tile, half)
                    now_x[at, :] = row_buf[source, rows, :]
                    now_g[at, :] = grad_buf[source, rows, :]
                    now_gate[at, :] = gate_buf[source, rows, :]

                @pl.when((TILE // HALF) * tile + half >= number)
                def _():
                    now_x[at, :] = jnp.zeros((HALF, width), bfloat)
                    now_g[at, :] = jnp.zeros((HALF, width), bfloat)
                    now_gate[at, :] = jnp.zeros((HALF, 1), single)

            rows_low, grad_low, gate = now_x[...], now_g[...], now_gate[...]
            st_x[slot] = (rows_low.astype(single) * gate).astype(bfloat)
            st_g[slot] = (grad_low.astype(single) * gate).astype(bfloat)
            for start in range(0, hidden, PART):
                cols = slice(start, start + PART)
                pre = dot_nn(rows_low, win[local, :, cols])
                grad_act = dot_nt(grad_low, wout[local, cols, :])
                act, slope = gelu_both(pre)
                st_act[slot, :, cols] = act.astype(bfloat)
                st_pre[slot, :, cols] = (slope * grad_act).astype(bfloat)
            result = dot_nn(st_act[slot], wout[local]).astype(bfloat).astype(single)
            grad_copy = dot_nt(st_pre[slot], win[local]).astype(bfloat)
            product = jnp.sum(grad_low.astype(single) * result, axis=1, keepdims=True)
            result = result.astype(bfloat)
            for half in range(TILE // HALF):
                at = slice(half * HALF, (half + 1) * HALF)

                @pl.when((TILE // HALF) * tile + half < number)
                def _():
                    source, rows, lanes = place(tile, half)
                    out_buf[source, rows, :] = result[at]
                    copy_buf[source, rows, :] = grad_copy[at]
                    product_buf[source, lanes, :] = jnp.sum(
                        jnp.where(eye, product[at], 0.0), axis=0, keepdims=True
                    )

            for copy in save_copies(slot, local, before[local] + tile):
                copy.start()
            return done + 1

        done = lax.fori_loop(
            0, (number + TILE // HALF - 1) // (TILE // HALF), one_tile, done
        )

    def result_copies():
        for source in range(sources):
            yield pltpu.make_async_copy(copy_buf.at[source], grads[source], out_sem.at[0, source])
            yield pltpu.make_async_copy(out_buf.at[source], outs[source], out_sem.at[1, source])

    for source in range(sources):
        rows = []
        for local in range(2):
            at = range(local * (cap // HALF), (local + 1) * (cap // HALF))
            rows.append(jnp.concatenate([product_buf[source, i : i + 1, :] for i in at], axis=1))
        copy_buf[source, 2 * cap :, :cap] = pack_rows(jnp.concatenate(rows, axis=0))
    for copy in result_copies():
        copy.start()
    for back in (1, 2):

        @pl.when(done >= back)
        def _():
            for copy in save_copies(lax.rem(done - back, 2), 0, 0):
                copy.wait()

    for copy in result_copies():
        copy.wait()


def weight_kernel(heads, waited, meta, tiles_saved, save_x, save_g, save_act, save_pre, *refs):
    refs = list(refs[waited:])
    outs = [
        [refs.pop(0) for _ in range(2 if local and by_x and by_c else 1)]
        for local in range(2)
        for by_x in range(heads // 2)
        for by_c in range(2)
    ]
    grad_in, grad_out, buf_x, buf_g, buf_act, buf_pre, sem, staged, out_sem = refs
    width, hidden = grad_in.shape
    leaving = []
    deep, wide = width // heads, hidden // heads
    buffers = (buf_x, buf_g, buf_act, buf_pre)

    def fetch(slot, local, tile):
        at = pl.ds(pl.multiple_of(tile * TILE, TILE), TILE)
        return [
            pltpu.make_async_copy(save.at[local, at, :], buf.at[slot], sem.at[slot, i])
            for i, (save, buf) in enumerate(zip((save_x, save_g, save_act, save_pre), buffers))
        ]

    for local in (1, 0):
        tiles = tiles_saved[local]

        @pl.when(tiles > 0)
        def _():
            for copy in fetch(0, local, 0):
                copy.start()

        @pl.when(tiles == 0)
        def _():
            grad_in[...] = jnp.zeros_like(grad_in)
            grad_out[...] = jnp.zeros_like(grad_out)

        def one_tile(tile, carry):
            slot = lax.rem(tile, 2)

            @pl.when(tile + 1 < tiles)
            def _():
                for copy in fetch(1 - slot, local, tile + 1):
                    copy.start()

            for copy in fetch(slot, local, tile):
                copy.wait()

            @pl.when(tile == 0)
            def _():
                for part in range(hidden // width):
                    cols = slice(part * width, (part + 1) * width)
                    grad_in[:, cols] = dot_tn(buf_x[slot], buf_pre[slot, :, cols])
                    grad_out[:, cols] = dot_tn(buf_g[slot], buf_act[slot, :, cols])

            @pl.when(tile > 0)
            def _():
                for part in range(hidden // width):
                    cols = slice(part * width, (part + 1) * width)
                    grad_in[:, cols] += dot_tn(buf_x[slot], buf_pre[slot, :, cols])
                    grad_out[:, cols] += dot_tn(buf_g[slot], buf_act[slot, :, cols])

            return carry

        lax.fori_loop(0, tiles, one_tile, 0)
        for by_x in range(heads // 2):
            for by_c in range(2):
                head = lax.rem(meta[0] + by_x, heads // 2) * 2 + lax.rem(meta[1] + by_c, 2)
                at = (local * (heads // 2) + by_x) * 2 + by_c
                out = staged.at[at]
                for part in range(hidden // width):
                    out[part * deep : (part + 1) * deep, :] = grad_in[
                        pl.ds(pl.multiple_of(head * deep, deep), deep),
                        part * width : (part + 1) * width,
                    ].astype(bfloat)
                block = grad_out[:, pl.ds(pl.multiple_of(head * wide, wide), wide)]
                out[hidden // width * deep :, :] = block.T.astype(bfloat)
                start = 0
                for i, left in enumerate(outs[at]):
                    part = out.at[pl.ds(start, left.shape[0]), :]
                    leaving.append(pltpu.make_async_copy(part, left, out_sem.at[at, i]))
                    leaving[-1].start()
                    start += left.shape[0]
    for copy in leaving:
        copy.wait()


def whole_call(kernel, out_shape, scratch=(), micros=1, in_specs=None, out_specs=None, aliases=None):
    specs = {}
    if in_specs is not None:
        specs["in_specs"] = in_specs
    if out_specs is not None:
        specs["out_specs"] = out_specs
    return pl.pallas_call(
        kernel,
        out_shape=out_shape,
        scratch_shapes=scratch,
        input_output_aliases=aliases or {},
        compiler_params=pltpu.CompilerParams(vmem_limit_bytes=VMEM_LIMIT),
        cost_estimate=pl.CostEstimate(
            flops=int(micros * SCALE), bytes_accessed=0, transcendentals=0
        ),
        **specs,
    )


class Grid:
    names = ("zh", "zl", "y", "x", "c")

    def __init__(self, mesh):
        experts, heads = mesh.shape["expert"], mesh.shape["head"]
        self.shape = (2, experts // 4, 2, heads // 2, 2)
        self.experts, self.heads = experts, heads
        self.total = experts * heads

    def size(self, name):
        return self.shape[self.names.index(name)]

    def coords(self, linear):
        out = []
        for extent in reversed(self.shape):
            out.append(linear % extent)
            linear = linear // extent
        return dict(zip(self.names, reversed(out)))

    def linear(self, coords):
        at = 0
        for name, extent in zip(self.names, self.shape):
            at = at * extent + coords[name] % extent
        return at

    def me(self, name):
        linear = lax.axis_index("expert") * self.heads + lax.axis_index("head")
        return self.coords(linear)[name]

    def send(self, value, target):
        pairs = [(i, self.linear(target(self.coords(i)))) for i in range(self.total)]
        return lax.ppermute(value, ("expert", "head"), pairs)

    def move(self, value, **by):
        return self.send(value, lambda at: {name: at[name] - by.get(name, 0) for name in at})

    def shift(self, value, name, by):
        return self.move(value, **{name: by})

    def exchange(self, value, name, *others):
        stride = self.linear({**dict.fromkeys(self.names, 0), name: 1}) // self.heads
        groups = [[at, at + stride] for at in range(self.experts) if at // stride % 2 == 0]
        both = jnp.broadcast_to(value[None], (2, *value.shape))
        both = lax.all_to_all(
            both, "expert", split_axis=0, concat_axis=0, tiled=True, axis_index_groups=groups
        )
        both = after(both, *others) if others else both
        return jnp.where(self.me(name) == 0, both[1], both[0])

    def gather(self, value, name, *others):
        extent, own = self.size(name), self.me(name)
        parts = [value] + [self.shift(value, name, by) for by in range(1, extent)]
        if others:
            parts[1] = after(parts[1], *others)
        if extent == 2:
            return jnp.where(own == 0, jnp.stack(parts), jnp.stack(parts[::-1]))
        return jnp.roll(jnp.stack(parts), own, axis=0)

    def scatter_sum(self, value, name, *waited):
        extent, own = self.size(name), self.me(name)
        if extent == 2:
            kept = jnp.where(own == 0, value[0], value[1])
            others = [self.shift(jnp.where(own == 0, value[1], value[0]), name, 1)]
        else:
            value = jnp.roll(value, -own, axis=0)
            kept = value[0]
            others = [self.shift(value[by], name, -by) for by in range(1, extent)]
        if waited:
            others[0] = after(others[0], *waited)
        total = kept.astype(single)
        for other in others:
            total = total + other.astype(single)
        return total.astype(value.dtype)


def after(value, *others):
    return lax.optimization_barrier((value, *others))[0]


def per_device(
    grid,
    tokens,
    segment_ids,
    task_ids,
    task_table,
    weight_qkv,
    weight_out,
    gain_one,
    gain_two,
    weight_router,
    weight_in,
    weight_hidden,
    cotangent,
):
    expert_count, head_count = grid.experts, grid.heads
    head_index = lax.axis_index("head")
    row_count, model_width = tokens.shape
    cap = 4 * row_count // expert_count
    deep, wide = weight_qkv.shape[1:]
    padded = -(-expert_count // 16) * 16

    pieces = jnp.concatenate([weight_qkv, weight_out.T[None]]).astype(bfloat)
    small = jnp.concatenate(
        [gain_one[None], gain_two[None], weight_router.T]
    ).astype(bfloat).reshape(-1)
    small_rows = -(-small.shape[0] // wide)
    small = jnp.pad(small, (0, small_rows * wide - small.shape[0])).reshape(small_rows, wide)
    packed = jnp.concatenate([pieces.reshape(4 * deep, wide), small])
    own_segments = lax.dynamic_slice_in_dim(segment_ids, head_index * row_count, row_count)
    shape = jax.ShapeDtypeStruct
    vmem, hbm = pl.BlockSpec(memory_space=pltpu.VMEM), pl.BlockSpec(memory_space=pl.ANY)
    smem = pl.BlockSpec(memory_space=pltpu.SMEM)
    table = jnp.pad(task_table.T, ((0, 16 - task_table.shape[1]), (0, 0))).astype(bfloat)
    hidden = weight_in.shape[2]
    deep_in = weight_in.shape[1]
    piece = shape((hidden // model_width * deep_in + weight_hidden.shape[1], model_width), bfloat)
    route_rows = padded * (2 * (row_count // model_width) + 2)
    first, second, route, own_piece, sent = whole_call(
        lambda *refs: routing_kernel(cap, *refs),
        [shape((1, row_count), jnp.int32)] * 2
        + [
            shape((padded, row_count), single),
            piece,
            shape((row_count + route_rows, model_width), bfloat),
        ],
        micros=3,
    )(own_segments[None], task_ids[None], table, weight_in, weight_hidden, cotangent)
    names = {name: grid.me(name) for name in grid.names}
    extent = grid.size("zl")
    offsets = [(dl, dy) for dl in range(extent) for dy in range(2)]
    offsets.sort(key=lambda by: by[0] * by[1] != 0)
    providers = len(offsets)

    def expert_of(zl, y, local):
        return ((names["zh"] + local) % 2 * extent + zl % extent) * 2 + y % 2

    def ints(*values):
        return jnp.concatenate([jnp.asarray(v, jnp.int32).reshape(-1) for v in values])

    targets = ints(
        *[expert_of(names["zl"] - dl, names["y"] - dy, k) for dl, dy in offsets for k in range(2)],
        names["c"],
    )
    parcel = shape((2 * cap + EXTRA, model_width), bfloat)
    packed = grid.gather(grid.gather(packed, "zh"), "zl")
    nearly = packed
    packed = grid.gather(packed, "y")
    smalls = packed.transpose(2, 1, 0, 3, 4).reshape(expert_count, -1)[:, 4 * deep * wide :]
    smalls = smalls[:, : (2 + expert_count) * deep].reshape(expert_count, 2 + expert_count, deep)
    smalls = smalls.transpose(1, 0, 2).reshape(2 + expert_count, model_width)
    gain1, gain2 = smalls[0:1].astype(single), smalls[1:2].astype(single)
    router = jnp.pad(smalls[2:], ((0, padded - expert_count), (0, 0)))
    packed = grid.gather(packed[..., : 4 * deep, :], "x")
    packed = packed.reshape(*packed.shape[:4], 4, deep, wide)
    if wide % LANES:
        packed = grid.gather(packed, "c").transpose(5, 4, 3, 2, 6, 1, 0, 7)
        packed = packed.reshape(4, model_width, model_width)
        weights = (packed, packed)
    else:
        weights = (packed, grid.shift(packed, "c", 1))

    segc = own_segments[:, None]
    segr = own_segments[None]

    core = ints(names["c"])
    gate_rows = 2 * padded * (row_count // model_width)
    proj, attn, res, two_low, stat, gate, weights = whole_call(
        forward_kernel,
        [
            shape((3, row_count, model_width), bfloat),
            shape((row_count, model_width), bfloat),
            shape((row_count, model_width), single),
            shape((row_count + gate_rows, model_width), bfloat),
            shape((model_width // HDIM, row_count), single),
            shape((padded, row_count), single),
            shape((4, model_width, model_width), bfloat),
        ],
        in_specs=[smem, vmem, hbm, hbm] + [vmem] * 7,
        out_specs=[hbm] * 5 + [vmem, hbm],
        scratch=[
            pltpu.VMEM((3, row_count, model_width), bfloat),
            pltpu.VMEM((row_count, model_width), bfloat),
            pltpu.VMEM((row_count, model_width), single),
            pltpu.VMEM((row_count + gate_rows, model_width), bfloat),
            pltpu.VMEM((model_width // HDIM, row_count), single),
            pltpu.VMEM((4, model_width, model_width), bfloat),
            pltpu.SemaphoreType.DMA((2, head_count // 2 * expert_count)),
            pltpu.SemaphoreType.DMA((5, max(4, row_count // BLOCK))),
        ],
        micros=0.2,
    )(core, tokens, *weights, gain1, gain2, router, segc, segr, first, second)

    own_piece = after(own_piece, nearly)
    pieces = {(0, 0, 0): own_piece, (1, 0, 0): grid.exchange(own_piece, "zh")}
    for by_x in range(1, head_count // 2):
        pieces[0, by_x, 0] = grid.shift(own_piece, "x", by_x)
    own_experts = [expert_of(names["zl"], names["y"], local) for local in range(2)]
    sent = after(sent, nearly)
    cots = {(dl, 0): grid.move(sent, zl=dl) if dl else sent for dl in range(extent)}
    cots[0, 1] = grid.move(sent, y=1)
    pieces[1, 0, 0] = after(pieces[1, 0, 0], two_low)
    rows = {(dl, 0): grid.move(two_low, zl=dl) if dl else two_low for dl in range(extent)}
    rows[0, 1] = grid.move(two_low, y=1)
    for dl in range(1, extent):
        rows[dl, 1] = grid.move(two_low, zl=dl, y=1)
        cots[dl, 1] = grid.move(cots[dl, 0], y=1)
    for by_x in range(1, head_count // 2):
        pieces[1, by_x, 0] = grid.shift(after(pieces[1, 0, 0], cots[0, 1]), "x", by_x)
    for by_x in range(head_count // 2):
        pieces[0, by_x, 0] = after(pieces[0, by_x, 0], two_low)
        pieces[0, by_x, 1] = grid.shift(pieces[0, by_x, 0], "c", 1)
    piece_keys = [(k, bx, bc) for k in range(2) for bx in range(head_count // 2) for bc in range(2)]

    calls = [{0: (0,)}, {0: (1,), 1: (0, 1)}] + [{at: (0, 1)} for at in range(2, min(4, providers))]
    for at in range(4, providers, 3):
        calls.append({s: (0, 1) for s in range(at, min(at + 3, providers))})
    save_tiles = sum(-(-len(call) * cap // TILE) for call in calls)
    save_shapes = [
        shape((2, save_tiles * TILE, cols), bfloat)
        for cols in (model_width, model_width, hidden, hidden)
    ]
    saved = []
    tiles_before = jnp.zeros((2,), jnp.int32)
    results = {}
    left = len(calls)
    for call in calls:
        left -= 1
        group = list(call)
        count = len(group)
        needed = sorted({local for work in call.values() for local in work})
        carried = [results[s] for s in group if s in results]
        carried = [value for both in carried for value in both]
        held_pieces = [pieces[key] for key in piece_keys if key[0] in needed]
        keys = [offsets[s] for s in group]
        inputs = [ints(names["x"], names["c"], *own_experts), tiles_before]
        inputs += [rows[key] for key in keys] + [cots[key] for key in keys]
        inputs += carried + held_pieces + saved
        before = 2 + 2 * count + len(carried) + len(held_pieces)
        outs = whole_call(
            lambda *refs, work=tuple(call.values()), fresh=not carried, new=not saved: expert_kernel(
                work, head_count, cap, row_count, padded, fresh, new, *refs
            ),
            save_shapes + [parcel] * (2 * count) + [shape((2,), jnp.int32)],
            in_specs=[smem, smem]
            + [hbm] * (2 * count + len(carried) + len(held_pieces) + len(saved)),
            out_specs=[hbm] * (4 + 2 * count) + [smem],
            aliases={before + i: i for i in range(len(saved))},
            scratch=[
                pltpu.VMEM((2, model_width, hidden), bfloat),
                pltpu.VMEM((2, hidden, model_width), bfloat),
                pltpu.VMEM((count, row_count + gate_rows, model_width), bfloat),
                pltpu.VMEM((count, *sent.shape), bfloat),
                pltpu.VMEM((count, 2 * cap, model_width), bfloat),
                pltpu.VMEM((count, 2 * cap, model_width), bfloat),
                pltpu.VMEM((count, 2 * cap, 1), single),
                pltpu.VMEM((count, *parcel.shape), bfloat),
                pltpu.VMEM((count, *parcel.shape), bfloat),
                pltpu.VMEM((count, 2 * cap // HALF, HALF), single),
                pltpu.VMEM((TILE, model_width), bfloat),
                pltpu.VMEM((TILE, model_width), bfloat),
                pltpu.VMEM((TILE, 1), single),
                pltpu.VMEM((2, TILE, model_width), bfloat),
                pltpu.VMEM((2, TILE, model_width), bfloat),
                pltpu.VMEM((2, TILE, hidden), bfloat),
                pltpu.VMEM((2, TILE, hidden), bfloat),
                pltpu.SMEM((2, count * cap // HALF + 1), jnp.int32),
                pltpu.SemaphoreType.DMA((2, head_count * (hidden // model_width + 1))),
                pltpu.SemaphoreType.DMA((2, count)),
                pltpu.SemaphoreType.DMA((2, 4)),
                pltpu.SemaphoreType.DMA((2, count)),
            ],
            micros=(8, 40)[len(saved) // 4] if left > len(calls) - 3 else 16,
        )(*inputs)
        if not saved:
            near = ((0, 1), (1, 0))
            held = lax.optimization_barrier(
                (pieces, rows[0, 1], [cots[key] for key in near], outs[0])
            )
            pieces, rows[0, 1] = dict(held[0]), held[1]
            cots.update(zip(near, held[2]))
            for by_x in range(1, head_count // 2):
                ready = after(pieces[1, by_x, 0], cots[1, 0], rows[0, 1])
                pieces[1, by_x, 0] = ready
            for by_x in range(head_count // 2):
                pieces[1, by_x, 1] = grid.shift(pieces[1, by_x, 0], "c", 1)
        if len(calls) - left == 2:
            for dl in range(1, extent):
                rows[dl, 0] = after(rows[dl, 0], outs[0])
        saved, tiles_before = list(outs[:4]), outs[-1]
        for i, s in enumerate(group):
            results[s] = [outs[4 + i], outs[4 + count + i]]
    out_parcels, grad_parcels = [], []
    for s, (dl, dy) in enumerate(offsets):
        out_part, grad_part = results[s]
        if dl and dy:
            grad_part = after(grad_part, *grad_parcels[1:])
        if dl or dy:
            grad_part = grid.move(grad_part, zl=-dl, y=-dy)
            out_part = after(out_part, saved[0])
            if not (dl and dy):
                out_part = grid.move(out_part, zl=-dl, y=-dy)
        out_parcels.append(out_part)
        grad_parcels.append(grad_part)
    waited = []
    halves = [
        shape((hidden // model_width * deep_in, model_width), bfloat),
        shape((weight_hidden.shape[1], model_width), bfloat),
    ]
    done = whole_call(
        lambda *refs: weight_kernel(head_count, len(waited), *refs),
        [s for key in piece_keys for s in (halves if all(key) else [piece])],
        in_specs=[smem, smem] + [hbm] * (4 + len(waited)),
        out_specs=[hbm] * sum(2 if all(key) else 1 for key in piece_keys),
        scratch=[
            pltpu.VMEM((model_width, hidden), single),
            pltpu.VMEM((model_width, hidden), single),
            pltpu.VMEM((2, TILE, model_width), bfloat),
            pltpu.VMEM((2, TILE, model_width), bfloat),
            pltpu.VMEM((2, TILE, hidden), bfloat),
            pltpu.VMEM((2, TILE, hidden), bfloat),
            pltpu.SemaphoreType.DMA((2, 4)),
            pltpu.VMEM((len(piece_keys), *piece.shape), bfloat),
            pltpu.SemaphoreType.DMA((len(piece_keys), 2)),
        ],
        micros=1,
    )(ints(names["x"], names["c"]), tiles_before, *saved, *waited)
    done, grad_parcels = lax.optimization_barrier((done, grad_parcels))
    out_parcels = [
        grid.move(after(value, done[0]), zl=-dl, y=-dy) if dl and dy else value
        for value, (dl, dy) in zip(out_parcels, offsets)
    ]
    done = list(done)
    grads = {
        key: [done.pop(0) for _ in halves] if all(key) else done.pop(0) for key in piece_keys
    }

    def add(kept, other):
        return (kept.astype(single) + other.astype(single)).astype(bfloat)

    crossed = {}
    for key in piece_keys:
        if key[2] == 0:
            other = grads[key[0], key[1], 1]
            parts = other if isinstance(other, list) else [other]
            parts = [grid.shift(part, "c", -1) for part in parts]
            crossed[key] = jnp.concatenate(parts) if len(parts) > 1 else parts[0]
    for by_x in range(1, head_count // 2):
        grads[1, by_x, 0] = add(grads[1, by_x, 0], crossed.pop((1, by_x, 0)))
    waited = []
    output = whole_call(
        lambda *refs: output_kernel(providers, cap, *refs),
        shape((row_count, model_width), bfloat),
        in_specs=[smem] + [vmem] * (3 + providers),
        micros=8,
    )(targets, res, gate, route, *out_parcels)

    grad_res, grad_heads, grad_out, grad_gain2, grad_router = whole_call(
        lambda *refs: middle_kernel(providers, cap, len(waited), *refs),
        (
            shape((row_count, model_width), single),
            shape((row_count, model_width), bfloat),
            shape((model_width, model_width), bfloat),
            shape((1, model_width), single),
            shape((padded, model_width), single),
        ),
        in_specs=[smem] + [hbm] * 5 + [vmem] * 4 + [hbm] * (providers + len(waited)),
        out_specs=[hbm] * 2 + [vmem] * 3,
        scratch=[
            pltpu.VMEM((padded, row_count), single),
            pltpu.VMEM((row_count, model_width), bfloat),
            pltpu.VMEM((row_count, model_width), single),
            pltpu.VMEM((row_count, model_width), bfloat),
            pltpu.VMEM((row_count, model_width), bfloat),
            pltpu.VMEM((row_count, model_width), single),
            pltpu.VMEM((row_count, model_width), bfloat),
            pltpu.VMEM((row_count, model_width), bfloat),
            pltpu.VMEM((model_width, model_width), bfloat),
            pltpu.VMEM((providers, *parcel.shape), bfloat),
            pltpu.SemaphoreType.DMA((providers + 5,)),
            pltpu.SemaphoreType.DMA((2, row_count // CHUNK)),
        ],
        micros=4,
    )(
        targets, cotangent, res, two_low, attn, weights, gain2, router, gate, route,
        *grad_parcels, *waited,
    )
    for key, other in crossed.items():
        grads[key] = add(grads[key], after(other, grad_gain2))
    for by_x in range(1, head_count // 2):
        other = after(grid.shift(grads[1, by_x, 0], "x", -by_x), grad_gain2)
        grads[1, 0, 0] = add(grads[1, 0, 0], other)
    grad_res = after(grad_res, grads[1, 0, 0], grads[0, 1, 0], *out_parcels[1:-1])
    columns = model_width if wide % LANES else model_width // 2
    grad_tokens, grad_own, other_top, other_rest, grad_gain1 = whole_call(
        lambda *refs: backward_kernel(head_count, *refs),
        (
            shape((row_count, model_width), single),
            shape((4, model_width, columns), bfloat),
            shape((2, model_width, columns), bfloat),
            shape((2, model_width, columns), bfloat),
            shape((1, model_width), single),
        ),
        in_specs=[smem] + [vmem] * 3 + [hbm] * 7,
        out_specs=[hbm] + [vmem] * 4,
        scratch=[
            pltpu.VMEM((3, row_count, model_width), bfloat),
            pltpu.VMEM((row_count, model_width), single),
            pltpu.VMEM((row_count, model_width), single),
            pltpu.VMEM((row_count, model_width), bfloat),
            pltpu.VMEM((4, model_width, model_width), bfloat),
            pltpu.VMEM((3, row_count, model_width), bfloat),
            pltpu.VMEM((row_count, model_width), bfloat),
            pltpu.VMEM((model_width // HDIM, row_count), single),
            pltpu.VMEM((row_count, model_width), bfloat),
            pltpu.VMEM((row_count, model_width), single),
            pltpu.VMEM((3, model_width, model_width), bfloat),
            pltpu.VMEM((row_count, model_width), single),
            pltpu.SemaphoreType.DMA((7,)),
            pltpu.SemaphoreType.DMA((row_count // CHUNK,)),
        ],
        micros=1,
    )(
        core, gain1, segc, segr, proj, grad_heads, stat, tokens, grad_res, weights, grad_out,
    )

    across = [
        after(grid.shift(grads[0, by_x, 0], "x", -by_x), grad_tokens)
        for by_x in range(1, head_count // 2)
    ]
    smalls = jnp.concatenate([grad_gain1, grad_gain2, grad_router[:expert_count]]).astype(bfloat)
    if wide % LANES or grid.size("x") != 2:
        if wide % LANES:
            packed = grad_own.reshape(4, model_width, -1, 2, wide).transpose(3, 0, 1, 2, 4)
            packed = grid.scatter_sum(packed, "c").reshape(4, model_width, -1)
        else:
            other = [grid.shift(v, "c", 1) for v in (other_top, other_rest)]
            packed = add(grad_own, jnp.concatenate(other))
        packed = packed.reshape(4, model_width, -1, wide).transpose(2, 0, 1, 3)
        packed, across, _ = lax.optimization_barrier((packed, across, out_parcels[3:]))
        packed = grid.scatter_sum(packed, "x", output)
    else:
        other = [grid.shift(v, "c", 1) for v in (other_top, other_rest)]
        other, across, _ = lax.optimization_barrier((other, across, out_parcels[3:]))

        def columns_of(x):
            def pick(value):
                return jnp.where(x == 0, value[..., :wide], value[..., wide:]).astype(single)

            both = zip((grad_own[:2], grad_own[2:]), other)
            return jnp.concatenate([pick(kept) + pick(crossed_in) for kept, crossed_in in both])

        got = grid.shift(columns_of(1 - names["x"]).astype(bfloat), "x", 1)
        packed = columns_of(names["x"]) + after(got, output).astype(single)
        packed = packed.astype(bfloat)
    grad_piece = grads[0, 0, 0].astype(single)
    for other in [*across, grid.exchange(grads[1, 0, 0], "zh", packed)]:
        grad_piece = grad_piece + other.astype(single)
    grad_in_own = grad_piece[: hidden // model_width * deep_in]
    grad_in_own = grad_in_own.reshape(-1, deep_in, model_width).transpose(1, 0, 2)
    grad_in_own = grad_in_own.reshape(1, deep_in, hidden)
    grad_hidden_own = grad_piece[hidden // model_width * deep_in :][None]
    for name in ("c", "x"):
        total = smalls.astype(single)
        for by in range(1, grid.size(name)):
            total = total + grid.shift(smalls, name, by).astype(single)
        smalls = total.astype(bfloat)
    smalls = smalls.reshape(2 + expert_count, expert_count, deep).transpose(1, 0, 2)
    smalls = smalls.reshape(expert_count, -1)
    smalls = jnp.pad(smalls, ((0, 0), (0, small_rows * wide - smalls.shape[1])))
    packed = packed.reshape(4, expert_count, deep, wide).transpose(1, 0, 2, 3)
    packed = packed.reshape(expert_count, 4 * deep, wide)
    packed = jnp.concatenate([packed, smalls.reshape(expert_count, small_rows, wide)], axis=1)
    packed = packed.reshape(*grid.shape[:3], 4 * deep + small_rows, wide).transpose(2, 1, 0, 3, 4)
    packed = after(packed, grad_piece)
    for name in ("y", "zl", "zh"):
        packed = grid.scatter_sum(packed, name)
    pieces = packed[: 4 * deep].reshape(4, deep, wide).astype(single)
    smalls = packed[4 * deep :].reshape(-1)[: (2 + expert_count) * deep].astype(single)
    smalls = smalls.reshape(2 + expert_count, deep)
    return (
        output,
        grad_tokens,
        pieces[:3],
        pieces[3].T,
        smalls[0],
        smalls[1],
        smalls[2:].T,
        grad_in_own,
        grad_hidden_own,
    )


def solution(mesh):
    grid = Grid(mesh)
    placed = (
        P(("expert", "head"), None),
        P("expert"),
        P(),
        P(),
        P(None, "expert", "head"),
        P("head", "expert"),
        P("expert"),
        P("expert"),
        P("expert", None),
        P("expert", "head", None),
        P("expert", "head", None),
        P(("expert", "head"), None),
    )

    def step(*arrays):
        return per_device(grid, *arrays)

    return jax.shard_map(
        step,
        mesh=mesh,
        in_specs=placed,
        out_specs=(
            P(("expert", "head"), None),
            P(("expert", "head"), None),
            P(None, "expert", "head"),
            P("head", "expert"),
            P("expert"),
            P("expert"),
            P("expert", None),
            P("expert", "head", None),
            P("expert", "head", None),
        ),
        check_vma=False,
    )
```
